32 devices in a mesh: rows: 16 (over z, y, x), inner: 2 (over core).
Axes of the slice: x: 2, y: 2, z: 4, core: 2. Of those that a mesh axis runs over, the one named last changes fastest.
Arguments:
- hidden: bfloat16 [16, 1568, 384], P('rows', 'inner'), may hold values from -6 to 6
- kept: int32 [16, 392], P('rows'), may hold values from 0 to 1567, as said below
- counts: int32 [16], P('rows'), may hold values from 196 to 392, as said below
- norm_gain: float32 [384], replicated, may hold values from 0.5 to 1.5
- in_weight: bfloat16 [2, 384, 768], P(None, None, 'inner'), may hold values from -0.3125 to 0.3125
- conv_weight: bfloat16 [2, 4, 768], P(None, None, 'inner'), may hold values from -3 to 3
- conv_bias: float32 [2, 768], P(None, 'inner'), may hold values from -3 to 3
- x_weight: bfloat16 [2, 768, 56], P(None, 'inner'), may hold values from -0.21875 to 0.21875
- dt_weight: bfloat16 [2, 24, 768], P(None, None, 'inner'), may hold values from -1.25 to 1.25
- dt_bias: float32 [2, 768], P(None, 'inner'), may hold values from -6 to -1
- a_log: float32 [2, 16, 768], P(None, None, 'inner'), may hold values from 0 to 2.77
- skip_gain: float32 [2, 768], P(None, 'inner'), may hold values from 0.5 to 1.5
- out_weight: bfloat16 [768, 384], P('inner'), may hold values from -0.21875 to 0.21875
- cotangent: bfloat16 [16, 392, 384], P('rows', 'inner'), may hold values from -6 to 6
Outputs:
- output: bfloat16 [16, 392, 384], P('rows', 'inner')
- hidden_grad: bfloat16 [16, 1568, 384], P('rows', 'inner')
- norm_gain_grad: float32 [384], P('inner')
- in_weight_grad: float32 [2, 384, 768], P(None, None, 'inner')
- conv_weight_grad: float32 [2, 4, 768], P(None, None, 'inner')
- conv_bias_grad: float32 [2, 768], P(None, 'inner')
- x_weight_grad: float32 [2, 768, 56], P(None, 'inner')
- dt_weight_grad: float32 [2, 24, 768], P(None, None, 'inner')
- dt_bias_grad: float32 [2, 768], P(None, 'inner')
- a_log_grad: float32 [2, 16, 768], P(None, None, 'inner')
- skip_gain_grad: float32 [2, 768], P(None, 'inner')
- out_weight_grad: float32 [768, 384], P('inner')
- dt_mean: float32 [2, 768], P(None, 'inner')
- dt_var: float32 [2, 768], P(None, 'inner')
The draws below stay inside these ranges and needn't reach their ends.
Inputs may be any that keep to these rules, and one draw needn't show every extreme that they name: `kept`: in clip c, slots 0 to counts[c] - 1 hold distinct positions of that clip in increasing order; the remaining slots hold other distinct positions and are not used. `counts`: kept tokens of each clip; some clip keeps 392.
All inputs are finite; a program needn't handle non-finite values.
Results may differ from the reference program's by a relative error of at most 0.011.
Values may be sent and summed in bfloat16 or wider, within the bound.
A program may use at most 128 MiB of HBM per device.

```python
import jax
import jax.numpy as jnp
from jax import lax

D = 384
DI = 768
STATE = 16
RANK = 24
KC = 4
XWIDTH = 56
FULL = 1568
KMAX = 392
CLIPS_DEV = 1
CLIPS = 16


def kept_plan(key):
    count_key, pick_key, order_key = jax.random.split(key, 3)
    drawn_counts = jax.random.randint(count_key, (CLIPS,), KMAX // 2, KMAX + 1)
    chosen = jax.random.randint(pick_key, (), 0, CLIPS)
    drawn_counts = jnp.where(jnp.arange(CLIPS) == chosen, KMAX, drawn_counts)
    ranks = jax.vmap(lambda one_key: jax.random.permutation(one_key, FULL))(jax.random.split(order_key, CLIPS))
    dropped = (ranks >= drawn_counts[:, None]).astype(jnp.int32)
    order = jnp.argsort(dropped, axis=1, stable=True)
    return (order[:, :KMAX].astype(jnp.int32), drawn_counts.astype(jnp.int32))


def draw_kept(key, part):
    return kept_plan(key)[0]


def draw_counts(key, part):
    return kept_plan(key)[1]


def levels(own_key, dims, cuts, smallest, largest):
    def one(axis_at, blocks):
        steps = jax.random.uniform(jax.random.fold_in(jax.random.fold_in(own_key, 6), axis_at), (blocks,), jnp.float32, smallest / len(cuts), largest / len(cuts))
        return jnp.repeat(jnp.exp(steps), dims[axis_at] // blocks).reshape((-1,) + (1,) * (len(dims) - axis_at - 1))

    factor_of = one(*cuts[0])
    for cut in cuts[1:]:
        factor_of = factor_of * one(*cut)
    return factor_of


def bell_draw(key, extent, scale, bound, cuts=(), kind=jnp.bfloat16):
    drawn = jax.random.normal(key, extent, jnp.float32) * scale
    if len(cuts) > 0:
        drawn = levels(key, extent, cuts, -0.22, 0.18) * drawn
    return jnp.clip(drawn, min=-bound, max=bound).astype(kind)


def setup_inputs(seed: int = 0) -> dict:
    splits = jax.random.split(jax.random.key(seed), 15)
    hidden = bell_draw(splits[0], (CLIPS, FULL, D), 1.0, 6.0, ((0, 16), (1, 2)))
    kept = draw_kept(jax.random.fold_in(splits[14], 71), 0)
    counts = draw_counts(jax.random.fold_in(splits[14], 71), 0)
    norm_gain = jnp.clip(1.0 + 0.1 * jax.random.normal(splits[3], (D,), jnp.float32), 0.5, 1.5)
    in_weight = bell_draw(splits[4], (2, D, DI), D ** -0.5, 0.3125, ((2, 2),))
    conv_weight = bell_draw(splits[5], (2, KC, DI), KC ** -0.5, 3.0, ((2, 2),))
    conv_bias = bell_draw(splits[6], (2, DI), 0.5, 3.0, ((1, 2),), jnp.float32)
    x_weight = bell_draw(splits[7], (2, DI, XWIDTH), DI ** -0.5, 0.21875, ((1, 2),))
    dt_weight = bell_draw(splits[8], (2, RANK, DI), RANK ** -0.5, 1.25, ((2, 2),))
    dt_bias = jnp.clip(-6.0 + 5.0 * jax.random.uniform(splits[9], (2, DI), jnp.float32) ** levels(splits[9], (2, DI), ((1, 2),), -0.2, 0.2), -6.0, -1.0)
    a_log = jnp.clip(2.77 * jax.random.uniform(splits[10], (2, STATE, DI), jnp.float32) ** levels(splits[10], (2, STATE, DI), ((2, 2),), -0.2, 0.2), 0.0, 2.77)
    skip_gain = jnp.clip(0.5 + 1.0 * jax.random.uniform(splits[11], (2, DI), jnp.float32) ** levels(splits[11], (2, DI), ((1, 2),), -0.2, 0.2), 0.5, 1.5)
    out_weight = bell_draw(splits[12], (DI, D), DI ** -0.5, 0.21875, ((0, 2),))
    cotangent = bell_draw(splits[13], (CLIPS, KMAX, D), 1.0, 6.0, ((0, 16), (1, 2)))
    return {"hidden": hidden, "kept": kept, "counts": counts, "norm_gain": norm_gain, "in_weight": in_weight, "conv_weight": conv_weight, "conv_bias": conv_bias, "x_weight": x_weight, "dt_weight": dt_weight, "dt_bias": dt_bias, "a_log": a_log, "skip_gain": skip_gain, "out_weight": out_weight, "cotangent": cotangent}


@jax.custom_vjp
def low(v):
    return lax.optimization_barrier(v.astype(jnp.bfloat16)).astype(jnp.float32)

@jax.custom_vjp
def low_back(v):
    return v

def low_keep(v):
    return (low(v), None)

def low_pass(kept, grad):
    return (grad,)

def back_keep(v):
    return (v, None)

def back_low(kept, grad):
    return (low(grad),)
low.defvjp(low_keep, low_pass)
low_back.defvjp(back_keep, back_low)
epsilon = 1e-05
highest = lax.Precision.HIGHEST

def product(left, right):
    return jnp.einsum('...i,ij->...j', left, right, precision=highest)

def causal_conv(values, kernel, bias):
    width = kernel.shape[0]
    length = values.shape[1]
    padded = jnp.pad(values, ((0, 0), (width - 1, 0), (0, 0)))
    total = bias + jnp.zeros_like(values)
    for place in range(width):
        total = total + kernel[place] * padded[:, place:place + length]
    return total

def selective(activated, delta, b_input, c_output, a_rates):

    def stepper(state, items):
        value, rate, b_row, c_row = items
        state = jnp.exp(rate[:, None, :] * a_rates) * state + rate[:, None, :] * b_row[:, :, None] * value[:, None, :]
        return (state, lax.optimization_barrier(jnp.sum(c_row[:, :, None] * state, axis=1)))
    start = jnp.zeros((activated.shape[0], a_rates.shape[0], activated.shape[2]), jnp.float32)
    items = tuple((jnp.swapaxes(item, 0, 1) for item in (activated, delta, b_input, c_output)))
    final, result = lax.scan(jax.checkpoint(stepper), start, items)
    return jnp.swapaxes(result, 0, 1)

def block_forward(gathered, valid, norm_gain, in_weight, conv_weight, conv_bias, x_weight, dt_weight, dt_bias, a_log, skip_gain, out_weight):
    inverse_rms = lax.rsqrt(lax.optimization_barrier(jnp.mean(gathered * gathered, axis=2, keepdims=True)) + epsilon)
    normed = low(gathered * inverse_rms * norm_gain)
    projected_x = low_back(product(normed, in_weight[0]))
    projected_z = low_back(product(normed, in_weight[1]))
    mask = valid[:, :, None]
    summed = jnp.zeros_like(projected_x)
    deltas = []
    for which in range(2):
        turned = which == 1
        source = jnp.flip(projected_x, 1) if turned else projected_x
        frame_mask = jnp.flip(mask, 1) if turned else mask
        activated = low(jax.nn.silu(causal_conv(source, conv_weight[which], conv_bias[which])) * frame_mask)
        joined = low_back(low(product(activated, x_weight[which])))
        low_rank = joined[:, :, :RANK]
        b_input = joined[:, :, RANK:RANK + STATE]
        c_output = joined[:, :, RANK + STATE:]
        delta = jax.nn.softplus(product(low_rank, dt_weight[which]) + dt_bias[which])
        scanned = selective(activated, delta, b_input, c_output, -jnp.exp(a_log[which])) + skip_gain[which] * activated
        if turned:
            scanned = jnp.flip(scanned, 1)
            delta = jnp.flip(delta, 1)
        summed = summed + scanned
        deltas.append(delta)
    gated = low(0.5 * summed * jax.nn.silu(projected_z))
    mixer = product(gated, out_weight)
    return ((gathered + mixer) * mask, jnp.stack(deltas))

def reference(hidden, kept, counts, norm_gain, in_weight, conv_weight, conv_bias, x_weight, dt_weight, dt_bias, a_log, skip_gain, out_weight, cotangent):
    weights = tuple((item.astype(jnp.float32) for item in (norm_gain, in_weight, conv_weight, conv_bias, x_weight, dt_weight, dt_bias, a_log, skip_gain, out_weight)))
    groups = CLIPS // CLIPS_DEV

    def split_groups(array):
        return array.reshape((groups, CLIPS_DEV) + array.shape[1:])

    def one_group(totals, items):
        clip_rows, clip_kept, clip_counts, clip_cotangent = items
        valid = (jnp.arange(KMAX)[None, :] < clip_counts[:, None]).astype(jnp.float32)

        def lifted(rows, *params):
            picked = jnp.take_along_axis(rows, clip_kept[:, :, None], axis=1) * valid[:, :, None]
            return block_forward(picked, valid, *params)
        output, pull, deltas = jax.vjp(lifted, clip_rows.astype(jnp.float32), *weights, has_aux=True)
        grads = pull(clip_cotangent.astype(jnp.float32))
        weighting = valid[None, :, :, None]
        moments = (lax.optimization_barrier(jnp.sum(deltas * weighting, axis=(1, 2))), lax.optimization_barrier(jnp.sum(deltas * deltas * weighting, axis=(1, 2))))
        updated = tuple((left + right for left, right in zip(totals, tuple(grads[1:]) + moments)))
        return (updated, (output.astype(jnp.bfloat16), grads[0].astype(jnp.bfloat16)))
    start = tuple((jnp.zeros_like(item) for item in weights)) + (jnp.zeros((2, DI), jnp.float32), jnp.zeros((2, DI), jnp.float32))
    totals, stacked = lax.scan(one_group, start, (split_groups(hidden), split_groups(kept), split_groups(counts), split_groups(cotangent)))
    output_rows = stacked[0].reshape(CLIPS, KMAX, D)
    hidden_grad = stacked[1].reshape(CLIPS, FULL, D)
    kept_total = jnp.sum(counts).astype(jnp.float32)
    dt_mean = totals[10] / kept_total
    dt_var = totals[11] / kept_total - dt_mean * dt_mean
    return (output_rows, hidden_grad, totals[0], totals[1], totals[2], totals[3], totals[4], totals[5], totals[6], totals[7], totals[8], totals[9], dt_mean, dt_var)
```

```python
import functools

import jax
import jax.numpy as jnp
from jax import lax
from jax.experimental import pallas as pl
from jax.experimental.pallas import tpu as pltpu
from jax.sharding import PartitionSpec as P

EPSILON = 1e-05
BLOCK = 16
LOG2E = 1.4426950408889634
MESH = pl.DeviceIdType.MESH
F32 = jnp.float32
BF16 = jnp.bfloat16


def dot(left, right):
    return jnp.dot(left, right, preferred_element_type=F32)


def dot_nt(left, right):
    return lax.dot_general(left, right, (((1,), (1,)), ((), ())), preferred_element_type=F32)


def dot_tn(left, right):
    return lax.dot_general(left, right, (((0,), (0,)), ((), ())), preferred_element_type=F32)


def iota(shape, axis):
    return lax.broadcasted_iota(jnp.int32, shape, axis)


def round_up(value, unit):
    return (value + unit - 1) // unit * unit


def block_kernel(
    sizes,
    hidden,
    kept,
    counts,
    norm_gain,
    in_weight,
    conv_weight,
    conv_bias,
    x_weight,
    dt_weight,
    dt_bias,
    a_log,
    skip_gain,
    out_weight,
    cotangent,
    output,
    hidden_grad,
    gain_grad,
    in_grad,
    conv_w_grad,
    conv_b_grad,
    xw_grad,
    dtw_grad,
    dtb_grad,
    alog_grad,
    skip_grad,
    out_grad,
    dt_sums,
    picked,
    picked_in,
    cot_pair,
    gout_f,
    gout,
    gathered,
    inverse,
    normed,
    px,
    pz,
    slope,
    act,
    xw_cat,
    dtw_pad,
    rates2,
    rates,
    part,
    part_in,
    proj,
    projb,
    delta,
    sig,
    u,
    up,
    gate,
    zslope,
    zgrad,
    gated,
    terms,
    terms_pair,
    terms_in,
    blkm,
    turned_rows,
    sel,
    states,
    ys,
    adj_0,
    adj_1,
    car_0,
    car_1,
    bsum_0,
    bsum_1,
    csum_0,
    csum_1,
    s1,
    cas,
    pgm,
    soft,
    actg,
    pgrad,
    pgrad_in,
    pgb,
    cgrad,
    xgrad,
    npart,
    npart_b,
    npart_in,
    sgrad,
    send_sem,
    recv_sem,
):
    half_full, width, slots, padded, half_slots, half_pad, inner_w, rank, state = sizes
    blocks = padded // BLOCK
    inner = lax.axis_index("inner")
    peer = 1 - inner

    def remote(source, target, index):
        return pltpu.make_async_remote_copy(
            src_ref=source,
            dst_ref=target,
            send_sem=send_sem.at[index],
            recv_sem=recv_sem.at[index],
            device_id={"inner": peer},
            device_id_type=MESH,
        )

    def rows_at(block):
        return pl.ds(pl.multiple_of(block * BLOCK, BLOCK), BLOCK)

    def each_block(body, unroll=5):
        def step(block, carry):
            body(block)
            return carry

        lax.fori_loop(0, blocks, step, 0, unroll=unroll)

    barrier = pltpu.get_barrier_semaphore()
    pl.semaphore_signal(barrier, inc=1, device_id={"inner": peer}, device_id_type=MESH)

    count = counts[0]
    kept_row = kept[...].astype(F32)
    first = (inner * half_full).astype(F32)

    own_cot = cotangent[...].astype(F32)
    cot_rows = iota((half_slots, 1), 0) + inner * half_slots
    own_cot = jnp.where(cot_rows < count, own_cot, 0.0)
    cot_full = jnp.concatenate([own_cot, jnp.zeros((half_pad - half_slots, width), F32)], 0)
    cot_pair[pl.ds(inner, 1)] = cot_full.astype(BF16)[None]

    def pick_rows(block):
        rows = iota((BLOCK, slots), 0) + block * BLOCK
        mine = jnp.where(rows == iota((BLOCK, slots), 1), kept_row, 0.0)
        place = jnp.sum(mine, axis=1, keepdims=True) - first
        slot = iota((BLOCK, 1), 0) + block * BLOCK
        place = jnp.where(slot < count, place, -1.0)
        column = iota((BLOCK, half_full), 1).astype(F32)
        chosen = jnp.where(place == column, 1.0, 0.0).astype(BF16)
        picked[rows_at(block), :] = dot(chosen, hidden[...]).astype(BF16)

    each_block(pick_rows, 1)
    pl.semaphore_wait(barrier, 1)
    send_pick = remote(picked, picked_in, 0)
    send_pick.start()
    send_cot = remote(cot_pair.at[inner], cot_pair.at[inner], 1)
    send_cot.start()

    pad_lane = jnp.zeros((inner_w, 64 - rank - 2 * state), F32)
    for r in range(2):
        mine = jnp.concatenate([x_weight[r].astype(F32), pad_lane], 1)
        other = jnp.zeros((inner_w, 64), F32)
        both = [mine, other] if r == 0 else [other, mine]
        xw_cat[r] = jnp.concatenate(both, 1).astype(BF16)
        low = dt_weight[r].astype(F32)
        parts = [low, jnp.zeros((128 - 64 * r - rank, inner_w), F32)]
        if r:
            parts = [jnp.zeros((64 * r, inner_w), F32)] + parts
        dtw_pad[r] = jnp.concatenate(parts, 0).astype(BF16)
        rate = -jnp.exp(a_log[r])
        rates[r] = rate
        rates2[r] = rate * LOG2E
    lane = iota((128, 1024), 1)
    chunk = lane // 256
    start = jnp.where(
        chunk == 0,
        rank,
        jnp.where(chunk == 1, rank + state, jnp.where(chunk == 2, 64 + rank, 64 + rank + state)),
    )
    sel[...] = jnp.where(iota((128, 1024), 0) == start + lane % state, 1.0, 0.0).astype(BF16)
    zero_rows = jnp.zeros((8, inner_w), F32)
    px[0:8, :] = zero_rows
    px[8 + padded : 16 + padded, :] = zero_rows
    for r in range(2):
        cgrad[r, 0:8, :] = zero_rows
        cgrad[r, 8 + padded : 16 + padded, :] = zero_rows
    states[0, 0:16, :] = jnp.zeros((16, inner_w), BF16)
    states[1, padded * 16 : padded * 16 + 16, :] = jnp.zeros((16, inner_w), BF16)

    send_pick.wait()
    gain = norm_gain[...]

    def norm_rows(block):
        rows = rows_at(block)
        held = picked[rows, :].astype(F32) + picked_in[rows, :].astype(F32)
        gathered[rows, :] = held
        scale = lax.rsqrt(jnp.sum(held * held, axis=1, keepdims=True) / width + EPSILON)
        inverse[rows, :] = scale
        normed[rows, :] = (held * scale * gain).astype(BF16)

    each_block(norm_rows)
    px[8 : 8 + padded, :] = dot(normed[...], in_weight[0])
    pz[...] = dot(normed[...], in_weight[1])

    taps = conv_weight[...].astype(F32)

    def conv_rows(block):
        base = pl.multiple_of(block * BLOCK, BLOCK)
        rows = rows_at(block)
        slot = iota((BLOCK, 1), 0) + block * BLOCK
        valid = jnp.where(slot < count, 1.0, 0.0)
        window = px[pl.ds(base, BLOCK + 16), :]
        for r in range(2):
            total = conv_bias[r : r + 1, :]
            for k in range(4):
                shift = k - 3 if r == 0 else 3 - k
                total = total + taps[r, k : k + 1, :] * window[8 + shift : 8 + shift + BLOCK, :]
            logistic = jax.nn.sigmoid(total)
            act[r, rows, :] = (total * logistic * valid).astype(BF16)
            slope[r, rows, :] = logistic * (1.0 + total * (1.0 - logistic)) * valid

    each_block(conv_rows, 1)
    part[...] = dot(act[0], xw_cat[0]) + dot(act[1], xw_cat[1])
    send_part = remote(part, part_in, 2)
    send_part.start()

    send_cot.wait()
    gout_f[0:half_pad, :] = cot_pair[0].astype(F32)
    gout_f[half_pad:, :] = jnp.zeros((gout_f.shape[0] - half_pad, width), F32)
    gout_f[half_slots : half_slots + half_pad, :] = cot_pair[1].astype(F32)
    gout[...] = gout_f[0:padded, :].astype(BF16)
    up[...] = dot_nt(gout[...], out_weight[...])

    def gate_rows(block):
        rows = rows_at(block)
        value = pz[rows, :]
        logistic = jax.nn.sigmoid(value)
        silu = value * logistic
        half_grad = 0.5 * up[rows, :]
        gate[rows, :] = 0.5 * silu
        zslope[rows, :] = half_grad * logistic * (1.0 + value * (1.0 - logistic))
        up[rows, :] = half_grad * silu

    each_block(gate_rows)

    send_part.wait()

    diagonal = jnp.where(iota((BLOCK, 1024), 0) == (iota((BLOCK, 1024), 1) // state) % BLOCK, 1.0, 0.0)

    def proj_rows(block):
        rows = rows_at(block)
        low = (part[rows, :] + part_in[rows, :]).astype(BF16)
        projb[rows, :] = low
        value = low.astype(F32)
        turned_rows[block] = value.T
        blkm[rows, :] = (dot(low, sel[...]) * diagonal).astype(BF16)

    each_block(proj_rows, 1)

    for r in range(2):
        sig[r] = dot(projb[...], dtw_pad[r])

    def delta_rows(block):
        rows = rows_at(block)
        for r in range(2):
            pre = sig[r, rows, :] + dt_bias[r : r + 1, :]
            small = jnp.exp(-jnp.abs(pre))
            inv = 1.0 / (1.0 + small)
            sig[r, rows, :] = jnp.where(pre >= 0.0, inv, small * inv)
            soft_plus = jnp.maximum(pre, 0.0) + jnp.log1p(small)
            delta[r, rows, :] = soft_plus
            u[r, rows, :] = soft_plus * act[r, rows, :].astype(F32)

    each_block(delta_rows, 1)

    def state_rows(place):
        return pl.ds(pl.multiple_of(place * 16, 16), 16)

    def emit_y(step):
        for r in range(2):
            block = step if r == 0 else blocks - 1 - step
            first_row = block * 256 + (16 if r == 0 else 0)
            held = states[r, pl.ds(pl.multiple_of(first_row, 16), 256), :]
            ys[r, rows_at(block), :] = dot(
                blkm[rows_at(block), 512 * r + 256 : 512 * r + 512], held
            )

    def forward_step(step, carry):
        emit_y(jnp.maximum(step - 1, 0))
        out = []
        for r in range(2):
            held = carry[r]
            block = step if r == 0 else blocks - 1 - step
            base = block * BLOCK
            b_cols = turned_rows[block, 64 * r + rank : 64 * r + rank + state, :]
            for j in range(BLOCK):
                t = j if r == 0 else BLOCK - 1 - j
                decay = jnp.exp2(delta[r, pl.ds(base + t, 1), :] * rates2[r])
                b_wide = jnp.broadcast_to(b_cols[:, t : t + 1], (state, inner_w))
                held = decay * held + u[r, pl.ds(base + t, 1), :] * b_wide
                states[r, state_rows(base + t + (1 if r == 0 else 0)), :] = held.astype(BF16)
            out.append(held)
        return tuple(out)

    zero_state = jnp.zeros((state, inner_w), F32)
    lax.fori_loop(0, blocks, forward_step, (zero_state, zero_state))
    emit_y(blocks - 1)

    def mix_rows(block):
        rows = rows_at(block)
        summed = ys[0, rows, :] + ys[1, rows, :]
        for r in range(2):
            summed = summed + skip_gain[r : r + 1, :] * act[r, rows, :].astype(F32)
        gated[rows, :] = (summed * gate[rows, :]).astype(BF16)
        zgrad[rows, :] = (summed * zslope[rows, :]).astype(BF16)

    each_block(mix_rows)
    terms[0:padded, :] = dot(gated[...], out_weight[...])
    terms_pair[0] = terms[0:half_pad, :]
    terms_pair[1] = terms[half_slots : half_slots + half_pad, :]
    send_terms = remote(terms_pair.at[peer], terms_in, 3)
    send_terms.start()
    out_grad[...] = dot_tn(gated[...], gout[...])
    in_grad[1] = dot_tn(normed[...], zgrad[...])
    npart[...] = dot_nt(zgrad[...], in_weight[1])

    adj_refs, car_refs = (adj_0, adj_1), (car_0, car_1)
    bsum_refs, csum_refs = (bsum_0, bsum_1), (csum_0, csum_1)
    block_mask = diagonal[:, 0:256]
    ones_block = block_mask.astype(BF16)
    ones_rows = jnp.ones((BLOCK, 128), BF16)

    def fold_lanes(value):
        total = value[:, 0:128]
        for at in range(128, inner_w, 128):
            total = total + value[:, at : at + 128]
        return total.astype(BF16)

    def emit_back(step):
        for r in range(2):
            block = blocks - 1 - step if r == 0 else step
            rows = rows_at(block)
            s1[r, rows, :] = dot(blkm[rows, 512 * r : 512 * r + 256], adj_refs[r][...])
            cas[r, rows, :] = dot(ones_block, car_refs[r][...])
            b_sums = dot_nt(ones_rows, bsum_refs[r][...])
            c_sums = dot_nt(ones_rows, csum_refs[r][...])
            pgm[rows, 512 * r : 512 * r + 256] = (b_sums * block_mask).astype(BF16)
            pgm[rows, 512 * r + 256 : 512 * r + 512] = (c_sums * block_mask).astype(BF16)

    def backward_step(step, carry):
        emit_back(jnp.maximum(step - 1, 0))
        out = []
        for r in range(2):
            passed, rate_sum, after = carry[r]
            block = blocks - 1 - step if r == 0 else step
            base = block * BLOCK
            c_cols = turned_rows[block, 64 * r + rank + state : 64 * r + rank + 2 * state, :]
            for j in range(BLOCK):
                t = BLOCK - 1 - j if r == 0 else j
                own = slice(t * 16, t * 16 + 16)
                step_size = delta[r, pl.ds(base + t, 1), :]
                upstream = up[pl.ds(base + t, 1), :]
                decay = jnp.exp2(step_size * rates2[r])
                c_wide = jnp.broadcast_to(c_cols[:, t : t + 1], (state, inner_w))
                adjoint = upstream * c_wide + passed
                passed = decay * adjoint
                adj_refs[r][own, :] = adjoint.astype(BF16)
                before = states[r, state_rows(base + t + (0 if r == 0 else 1)), :].astype(F32)
                carried = passed * before
                car_refs[r][own, :] = (carried * rates[r]).astype(BF16)
                rate_sum = rate_sum + carried * step_size
                bsum_refs[r][own, :] = fold_lanes(adjoint * u[r, pl.ds(base + t, 1), :])
                csum_refs[r][own, :] = fold_lanes(after * upstream)
                after = before
            out.append((passed, rate_sum, after))
        return tuple(out)

    last = states[0, padded * 16 : padded * 16 + 16, :].astype(F32)
    top = states[1, 0:16, :].astype(F32)
    final = lax.fori_loop(
        0,
        blocks,
        backward_step,
        ((zero_state, zero_state, last), (zero_state, zero_state, top)),
    )
    emit_back(blocks - 1)
    for r in range(2):
        alog_grad[r] = final[r][1] * rates[r]

    def soft_rows(block, carry):
        rows = rows_at(block)
        slot = iota((BLOCK, 1), 0) + block * BLOCK
        valid = slot < count
        out = []
        upstream = up[rows, :]
        for r in range(2):
            bias_sum, skip_sum, delta_sum, square_sum = carry[r]
            active = act[r, rows, :].astype(F32)
            step_size = delta[r, rows, :]
            first_sum = s1[r, rows, :]
            pre_grad = (active * first_sum + cas[r, rows, :]) * sig[r, rows, :]
            soft[r, rows, :] = pre_grad.astype(BF16)
            actg[r, rows, :] = first_sum * step_size + skip_gain[r : r + 1, :] * upstream
            kept_step = jnp.where(valid, step_size, 0.0)
            out.append(
                (
                    bias_sum + pre_grad,
                    skip_sum + upstream * active,
                    delta_sum + kept_step,
                    square_sum + kept_step * step_size,
                )
            )
        return tuple(out)

    wide = jnp.zeros((BLOCK, inner_w), F32)
    sums = lax.fori_loop(0, blocks, soft_rows, ((wide,) * 4,) * 2)
    pgrad[...] = (
        dot_nt(pgm[...], sel[...]) + dot_nt(soft[0], dtw_pad[0]) + dot_nt(soft[1], dtw_pad[1])
    )
    send_pgrad = remote(pgrad, pgrad_in, 4)
    send_pgrad.start()
    for r in range(2):
        dtb_grad[r : r + 1, :] = jnp.sum(sums[r][0], axis=0, keepdims=True)
        skip_grad[r : r + 1, :] = jnp.sum(sums[r][1], axis=0, keepdims=True)
        dt_sums[r : r + 1, :] = jnp.sum(sums[r][2], axis=0, keepdims=True)
        dt_sums[2 + r : 3 + r, :] = jnp.sum(sums[r][3], axis=0, keepdims=True)
        low_grad = dot_tn(projb[...], soft[r])
        dtw_grad[r] = low_grad[64 * r : 64 * r + rank, :]

    send_terms.wait()
    gathered_half = jnp.where(
        inner == 0, gathered[0:half_slots, :], gathered[half_slots : 2 * half_slots, :]
    )
    mixer = terms_pair[inner][0:half_slots, :] + terms_in[0:half_slots, :]
    output[...] = jnp.where(cot_rows < count, gathered_half + mixer, 0.0).astype(BF16)

    send_pgrad.wait()
    pgb[...] = (pgrad[...] + pgrad_in[...]).astype(BF16)
    for r in range(2):
        actg[r] = actg[r] + dot_nt(pgb[...], xw_cat[r])

    def back_rows(block):
        rows = rows_at(block)
        inside = pl.ds(pl.multiple_of(block * BLOCK, BLOCK) + 8, BLOCK)
        for r in range(2):
            cgrad[r, inside, :] = actg[r, rows, :] * slope[r, rows, :]

    each_block(back_rows)

    def conv_back_rows(block, carry):
        base = pl.multiple_of(block * BLOCK, BLOCK)
        window = px[pl.ds(base, BLOCK + 16), :]
        total = jnp.zeros((BLOCK, inner_w), F32)
        out = []
        for r in range(2):
            grads = cgrad[r, pl.ds(base, BLOCK + 16), :]
            here = grads[8 : 8 + BLOCK, :]
            for k in range(4):
                shift = k - 3 if r == 0 else 3 - k
                total = total + taps[r, k : k + 1, :] * grads[8 - shift : 8 - shift + BLOCK, :]
                out.append(carry[5 * r + k] + here * window[8 + shift : 8 + shift + BLOCK, :])
            out.append(carry[5 * r + 4] + here)
        xgrad[rows_at(block), :] = total.astype(BF16)
        return tuple(out)

    conv_sums = lax.fori_loop(0, blocks, conv_back_rows, (wide,) * 10)
    npart[...] = npart[...] + dot_nt(xgrad[...], in_weight[0])
    send_npart = remote(npart, npart_in, 5)
    send_npart.start()
    for r in range(2):
        for k in range(4):
            conv_w_grad[r, k : k + 1, :] = jnp.sum(conv_sums[5 * r + k], axis=0, keepdims=True)
        conv_b_grad[r : r + 1, :] = jnp.sum(conv_sums[5 * r + 4], axis=0, keepdims=True)
        wide_grad = dot_tn(act[r], pgb[...])
        xw_grad[r] = wide_grad[:, 64 * r : 64 * r + rank + 2 * state]
    in_grad[0] = dot_tn(normed[...], xgrad[...])

    send_npart.wait()

    def slot_rows(block, carry):
        rows = rows_at(block)
        whole = npart[rows, :] + npart_in[rows, :]
        held = gathered[rows, :]
        scale = inverse[rows, :]
        by_gain = whole * held * scale
        scaled = whole * gain
        row_dot = jnp.sum(scaled * held, axis=1, keepdims=True)
        factor = scale * scale * scale * row_dot / width
        grad = scale * scaled - held * factor + gout_f[rows, :]
        slot = iota((BLOCK, 1), 0) + block * BLOCK
        sgrad[rows, :] = jnp.where(slot < count, grad, 0.0).astype(BF16)
        return carry + by_gain

    gain_sum = lax.fori_loop(0, blocks, slot_rows, wide)
    gain_grad[...] = jnp.sum(gain_sum, axis=0, keepdims=True)

    slot_lane = iota((1, slots), 1)
    places = jnp.where(slot_lane < count, kept_row - first, -1.0)
    spread = 112

    def scatter_rows(step, carry):
        base = pl.multiple_of(step * spread, 16)
        row = (iota((spread, slots), 0) + step * spread).astype(F32)
        chosen = jnp.where(row == places, 1.0, 0.0).astype(BF16)
        hidden_grad[pl.ds(base, spread), :] = dot(chosen, sgrad[0:slots, :]).astype(BF16)
        return carry

    lax.fori_loop(0, half_full // spread, scatter_rows, 0)


def per_device(
    hidden,
    kept,
    counts,
    norm_gain,
    in_weight,
    conv_weight,
    conv_bias,
    x_weight,
    dt_weight,
    dt_bias,
    a_log,
    skip_gain,
    out_weight,
    cotangent,
):
    half_full, width = hidden.shape[1:]
    slots = kept.shape[1]
    half_slots = cotangent.shape[1]
    padded = round_up(slots, BLOCK)
    half_pad = round_up(half_slots, BLOCK)
    inner_w = in_weight.shape[2]
    rank = dt_weight.shape[1]
    state = a_log.shape[1]
    xwidth = x_weight.shape[2]
    sizes = (half_full, width, slots, padded, half_slots, half_pad, inner_w, rank, state)
    inner_index = lax.axis_index("inner")
    inner_count = lax.axis_size("inner")

    def shape(*dims, kind=F32):
        return jax.ShapeDtypeStruct(dims, kind)

    outs = [
        shape(half_slots, width, kind=BF16),
        shape(half_full, width, kind=BF16),
        shape(1, width),
        shape(2, width, inner_w),
        shape(2, 4, inner_w),
        shape(2, inner_w),
        shape(2, inner_w, xwidth),
        shape(2, rank, inner_w),
        shape(2, inner_w),
        shape(2, state, inner_w),
        shape(2, inner_w),
        shape(inner_w, width),
        shape(4, inner_w),
    ]
    vm = pltpu.VMEM
    scratch = [
        vm((padded, width), BF16),
        vm((padded, width), BF16),
        vm((2, half_pad, width), BF16),
        vm((round_up(half_slots + half_pad, BLOCK) + 16, width), F32),
        vm((padded, width), BF16),
        vm((padded, width), F32),
        vm((padded, 1), F32),
        vm((padded, width), BF16),
        vm((padded + 16, inner_w), F32),
        vm((padded, inner_w), F32),
        vm((2, padded, inner_w), F32),
        vm((2, padded, inner_w), BF16),
        vm((2, inner_w, 128), BF16),
        vm((2, 128, inner_w), BF16),
        vm((2, state, inner_w), F32),
        vm((2, state, inner_w), F32),
        vm((padded, 128), F32),
        vm((padded, 128), F32),
        vm((padded, 128), F32),
        vm((padded, 128), BF16),
        vm((2, padded, inner_w), F32),
        vm((2, padded, inner_w), F32),
        vm((2, padded, inner_w), F32),
        vm((padded, inner_w), F32),
        vm((padded, inner_w), F32),
        vm((padded, inner_w), F32),
        vm((padded, inner_w), BF16),
        vm((padded, inner_w), BF16),
        vm((round_up(half_slots + half_pad, BLOCK), width), F32),
        vm((2, half_pad, width), F32),
        vm((half_pad, width), F32),
        vm((padded, 1024), BF16),
        vm((padded // BLOCK, 128, BLOCK), F32),
        vm((128, 1024), BF16),
        vm((2, padded * 16 + 16, inner_w), BF16),
        vm((2, padded, inner_w), F32),
        vm((256, inner_w), BF16),
        vm((256, inner_w), BF16),
        vm((256, inner_w), BF16),
        vm((256, inner_w), BF16),
        vm((256, 128), BF16),
        vm((256, 128), BF16),
        vm((256, 128), BF16),
        vm((256, 128), BF16),
        vm((2, padded, inner_w), F32),
        vm((2, padded, inner_w), F32),
        vm((padded, 1024), BF16),
        vm((2, padded, inner_w), BF16),
        vm((2, padded, inner_w), F32),
        vm((padded, 128), F32),
        vm((padded, 128), F32),
        vm((padded, 128), BF16),
        vm((2, padded + 16, inner_w), F32),
        vm((padded, inner_w), BF16),
        vm((padded, width), F32),
        vm((padded, width), BF16),
        vm((padded, width), F32),
        vm((padded, width), BF16),
        pltpu.SemaphoreType.DMA((6,)),
        pltpu.SemaphoreType.DMA((6,)),
    ]
    in_vmem = pl.BlockSpec(memory_space=pltpu.VMEM)
    in_smem = pl.BlockSpec(memory_space=pltpu.SMEM)
    in_specs = [in_vmem, in_vmem, in_smem] + [in_vmem] * 11
    (
        output,
        hidden_grad,
        gain_whole,
        in_grad,
        conv_w_grad,
        conv_b_grad,
        xw_grad,
        dtw_grad,
        dtb_grad,
        alog_grad,
        skip_grad,
        out_grad,
        dt_sums,
    ) = pl.pallas_call(
        functools.partial(block_kernel, sizes),
        out_shape=outs,
        in_specs=in_specs,
        out_specs=[in_vmem] * len(outs),
        scratch_shapes=scratch,
        compiler_params=pltpu.CompilerParams(
            collective_id=0, has_side_effects=True, vmem_limit_bytes=63 * 2**20
        ),
    )(
        hidden[0],
        kept,
        counts,
        norm_gain[None],
        in_weight,
        conv_weight,
        conv_bias,
        x_weight,
        dt_weight,
        dt_bias,
        a_log,
        skip_gain,
        out_weight,
        cotangent[0],
    )
    gain_part = width // inner_count
    gain_grad = lax.dynamic_slice_in_dim(gain_whole[0], inner_index * gain_part, gain_part, 0)
    kept_total = jnp.sum(counts).astype(F32)
    (
        gain_grad,
        in_grad,
        conv_w_grad,
        conv_b_grad,
        xw_grad,
        dtw_grad,
        dtb_grad,
        alog_grad,
        skip_grad,
        out_grad,
        dt_sums,
        kept_total,
    ) = lax.psum(
        (
            gain_grad,
            in_grad,
            conv_w_grad,
            conv_b_grad,
            xw_grad,
            dtw_grad,
            dtb_grad,
            alog_grad,
            skip_grad,
            out_grad,
            dt_sums,
            kept_total,
        ),
        "rows",
    )
    dt_mean = dt_sums[0:2] / kept_total
    dt_var = dt_sums[2:4] / kept_total - dt_mean * dt_mean
    return (
        output[None],
        hidden_grad[None],
        gain_grad,
        in_grad,
        conv_w_grad,
        conv_b_grad,
        xw_grad,
        dtw_grad,
        dtb_grad,
        alog_grad,
        skip_grad,
        out_grad,
        dt_mean,
        dt_var,
    )


def solution(mesh):
    in_specs = (
        P("rows", "inner", None),
        P("rows", None),
        P("rows"),
        P(),
        P(None, None, "inner"),
        P(None, None, "inner"),
        P(None, "inner"),
        P(None, "inner", None),
        P(None, None, "inner"),
        P(None, "inner"),
        P(None, None, "inner"),
        P(None, "inner"),
        P("inner", None),
        P("rows", "inner", None),
    )
    out_specs = (
        P("rows", "inner", None),
        P("rows", "inner", None),
        P("inner"),
        P(None, None, "inner"),
        P(None, None, "inner"),
        P(None, "inner"),
        P(None, "inner", None),
        P(None, None, "inner"),
        P(None, "inner"),
        P(None, None, "inner"),
        P(None, "inner"),
        P("inner", None),
        P(None, "inner"),
        P(None, "inner"),
    )
    return jax.shard_map(
        per_device, mesh=mesh, in_specs=in_specs, out_specs=out_specs, check_vma=False
    )
```

```python
import functools

import jax
import jax.numpy as jnp
from jax import lax
from jax.experimental import pallas as pl
from jax.experimental.pallas import tpu as pltpu
from jax.sharding import PartitionSpec as P

EPSILON = 1e-05
BLOCK = 16
LOG2E = 1.4426950408889634
MESH = pl.DeviceIdType.MESH
F32 = jnp.float32
BF16 = jnp.bfloat16


def dot(left, right):
    return jnp.dot(left, right, preferred_element_type=F32)


def dot_nt(left, right):
    return lax.dot_general(left, right, (((1,), (1,)), ((), ())), preferred_element_type=F32)


def dot_tn(left, right):
    return lax.dot_general(left, right, (((0,), (0,)), ((), ())), preferred_element_type=F32)


def iota(shape, axis):
    return lax.broadcasted_iota(jnp.int32, shape, axis)


def round_up(value, unit):
    return (value + unit - 1) // unit * unit


def chunk_tiles(total, devices):
    first = -(-2 * total // (3 * devices))
    return first, max(1, -(-(total - first * devices) // devices))


def tile_at(pair, tile):
    ref = pair[0]
    capacity = ref.shape[0] * ref.shape[1] * ref.shape[2] // BLOCK
    if tile >= capacity:
        tile, ref = tile - capacity, pair[1]
    each = ref.shape[2] // BLOCK
    chunk, place = tile // each, tile % each
    outer, middle = chunk // ref.shape[1], chunk % ref.shape[1]
    return ref, (outer, middle, slice(place * BLOCK, place * BLOCK + BLOCK), slice(None))


class Reducer:
    def __init__(self, a, b, sems, near, far, my_near, my_far, near_peer, far_peer):
        self.ways = [
            (a, (near, my_near, near_peer), (far, my_far, far_peer)),
            (b, (far, my_far, far_peer), (near, my_near, near_peer)),
        ]
        self.sems = sems
        self.copies = []

    def put(self, first, value):
        columns = value.shape[1] // 128
        pair = (self.ways[0][0][0], self.ways[1][0][0])
        for tile in range(value.shape[0] // BLOCK):
            for lane in range(columns):
                ref, at = tile_at(pair, first + tile * columns + lane)
                part = value[tile * BLOCK : tile * BLOCK + BLOCK, lane * 128 : lane * 128 + 128]
                ref[at] = part.astype(BF16)

    def send(self, phase, make):
        self.copies = []
        place = 0
        for refs, one, two in self.ways:
            number, mine, peer_of = one if phase in (0, 3) else two
            for offset in range(1, number):
                source, target = make(refs, one, two, lax.rem(mine + offset, number))
                copy = pltpu.make_async_remote_copy(
                    src_ref=source,
                    dst_ref=target,
                    send_sem=self.sems.at[phase, 0, place],
                    recv_sem=self.sems.at[phase, 1, place],
                    device_id={"rows": peer_of(offset)},
                    device_id_type=MESH,
                )
                copy.start()
                self.copies.append(copy)
                place += 1

    def wait(self):
        for copy in self.copies:
            copy.wait()

    def first(self):
        self.send(0, lambda refs, one, two, other: (refs[0].at[other], refs[1].at[one[1]]))

    def second(self):
        self.wait()
        for refs, one, two in self.ways:
            number, mine, _ = one
            for part in range(two[0]):
                held = refs[0][mine, part].astype(F32)
                for offset in range(1, number):
                    held = held + refs[1][lax.rem(mine + offset, number), part].astype(F32)
                refs[2][part] = held.astype(BF16)
        self.send(1, lambda refs, one, two, other: (refs[2].at[other], refs[3].at[two[1]]))

    def third(self):
        self.wait()
        for refs, one, two in self.ways:
            number, mine, _ = two
            held = refs[2][mine].astype(F32)
            for offset in range(1, number):
                held = held + refs[3][lax.rem(mine + offset, number)].astype(F32)
            refs[4][one[1], mine] = held.astype(BF16)
        self.send(
            2,
            lambda refs, one, two, other: (
                refs[4].at[one[1], two[1]],
                refs[4].at[one[1], two[1]],
            ),
        )

    def fourth(self):
        self.wait()
        self.send(3, lambda refs, one, two, other: (refs[4].at[one[1]], refs[4].at[one[1]]))

    def finish(self):
        self.wait()


def block_kernel(
    sizes,
    hidden,
    kept,
    counts,
    norm_gain,
    in_weight,
    conv_weight,
    conv_bias,
    x_weight,
    dt_weight,
    dt_bias,
    a_log,
    skip_gain,
    out_weight,
    cotangent,
    output,
    hidden_grad,
    early_a_out,
    early_b_out,
    late_a_out,
    late_b_out,
    tiny_out,
    picked,
    picked_in,
    cot_pair,
    gout_f,
    gout,
    gathered,
    inverse,
    normed,
    px,
    pz,
    slope,
    act,
    xw_cat,
    dtw_pad,
    rates2,
    rates,
    part,
    part_in,
    proj,
    projb,
    delta,
    sig,
    u,
    up,
    gate,
    zslope,
    zgrad,
    gated,
    terms,
    terms_pair,
    terms_in,
    blkm,
    turned_rows,
    sel,
    states,
    ys,
    adj_0,
    adj_1,
    car_0,
    car_1,
    bsum_0,
    bsum_1,
    csum_0,
    csum_1,
    s1,
    cas,
    pgm,
    soft,
    actg,
    pgrad,
    pgrad_in,
    pgb,
    cgrad,
    xgrad,
    npart,
    npart_b,
    npart_in,
    sgrad,
    chosen,
    spread_rows,
    early_a,
    early_a1,
    early_am,
    early_a2,
    early_b,
    early_b1,
    early_bm,
    early_b2,
    late_a,
    late_a1,
    late_am,
    late_a2,
    late_b,
    late_b1,
    late_bm,
    late_b2,
    tiny,
    tiny_low,
    tiny_mid,
    tiny_high,
    send_sem,
    recv_sem,
    early_sems,
    late_sems,
    tiny_sems,
):
    half_full, width, slots, padded, half_slots, half_pad, inner_w, rank, state, near, far = sizes
    blocks = padded // BLOCK
    inner = lax.axis_index("inner")
    peer = 1 - inner

    def remote(source, target, index):
        return pltpu.make_async_remote_copy(
            src_ref=source,
            dst_ref=target,
            send_sem=send_sem.at[index],
            recv_sem=recv_sem.at[index],
            device_id={"inner": peer},
            device_id_type=MESH,
        )

    def rows_at(block):
        return pl.ds(pl.multiple_of(block * BLOCK, BLOCK), BLOCK)

    def each_block(body, unroll=5):
        def step(block, carry):
            body(block)
            return carry

        lax.fori_loop(0, blocks, step, 0, unroll=unroll)

    row = lax.axis_index("rows")
    my_near, my_far = lax.rem(row, near), row // near

    def near_peer(offset):
        return my_far * near + lax.rem(my_near + offset, near)

    def far_peer(offset):
        return lax.rem(my_far + offset, far) * near + my_near

    barrier = pltpu.get_barrier_semaphore()
    pl.semaphore_signal(barrier, inc=1, device_id={"inner": peer}, device_id_type=MESH)
    for offset in range(1, near):
        pl.semaphore_signal(
            barrier, inc=1, device_id={"rows": near_peer(offset)}, device_id_type=MESH
        )
    for offset in range(1, far):
        pl.semaphore_signal(
            barrier, inc=1, device_id={"rows": far_peer(offset)}, device_id_type=MESH
        )

    early = Reducer(
        (early_a, early_a1, early_am, early_a2, early_a_out),
        (early_b, early_b1, early_bm, early_b2, early_b_out),
        early_sems, near, far, my_near, my_far, near_peer, far_peer,
    )
    late = Reducer(
        (late_a, late_a1, late_am, late_a2, late_a_out),
        (late_b, late_b1, late_bm, late_b2, late_b_out),
        late_sems, near, far, my_near, my_far, near_peer, far_peer,
    )

    count = counts[0]
    kept_row = kept[...].astype(F32)
    first = (inner * half_full).astype(F32)

    own_cot = cotangent[...].astype(F32)
    cot_rows = iota((half_slots, 1), 0) + inner * half_slots
    own_cot = jnp.where(cot_rows < count, own_cot, 0.0)
    cot_full = jnp.concatenate([own_cot, jnp.zeros((half_pad - half_slots, width), F32)], 0)
    cot_pair[pl.ds(inner, 1)] = cot_full.astype(BF16)[None]

    def pick_rows(block):
        rows = iota((BLOCK, slots), 0) + block * BLOCK
        mine = jnp.where(rows == iota((BLOCK, slots), 1), kept_row, 0.0)
        place = jnp.sum(mine, axis=1, keepdims=True) - first
        slot = iota((BLOCK, 1), 0) + block * BLOCK
        place = jnp.where(slot < count, place, -1.0)
        column = iota((BLOCK, half_full), 1).astype(F32)
        chosen[rows_at(block), :] = jnp.where(place == column, 1.0, 0.0).astype(BF16)

    each_block(pick_rows)
    picked[...] = dot(chosen[...], hidden[...]).astype(BF16)
    pl.semaphore_wait(barrier, near + far - 1)
    send_pick = remote(picked, picked_in, 0)
    send_pick.start()
    send_cot = remote(cot_pair.at[inner], cot_pair.at[inner], 1)
    send_cot.start()

    def at_rows(value, r):
        parts = [value, jnp.zeros((128 - 64 * r - value.shape[0], inner_w), F32)]
        if r:
            parts = [jnp.zeros((64 * r, inner_w), F32)] + parts
        return jnp.concatenate(parts, 0).astype(BF16)

    for r in range(2):
        xw_cat[r] = at_rows(x_weight[r].astype(F32), r)
        dtw_pad[r] = at_rows(dt_weight[r].astype(F32), r)
        rate = -jnp.exp(a_log[r])
        rates[r] = rate
        rates2[r] = rate * LOG2E
    lane = iota((128, 1024), 1)
    chunk = lane // 256
    start = jnp.where(
        chunk == 0,
        rank,
        jnp.where(chunk == 1, rank + state, jnp.where(chunk == 2, 64 + rank, 64 + rank + state)),
    )
    sel[...] = jnp.where(iota((128, 1024), 0) == start + lane % state, 1.0, 0.0).astype(BF16)
    zero_rows = jnp.zeros((8, inner_w), F32)
    px[0:8, :] = zero_rows
    px[8 + padded : 16 + padded, :] = zero_rows
    for r in range(2):
        cgrad[r, 0:8, :] = zero_rows
        cgrad[r, 8 + padded : 16 + padded, :] = zero_rows
    states[0, 0:16, :] = jnp.zeros((16, inner_w), BF16)
    states[1, padded * 16 : padded * 16 + 16, :] = jnp.zeros((16, inner_w), BF16)

    send_pick.wait()
    gain = norm_gain[...].reshape(1, width)

    def norm_rows(block):
        rows = rows_at(block)
        held = picked[rows, :].astype(F32) + picked_in[rows, :].astype(F32)
        gathered[rows, :] = held
        scale = lax.rsqrt(jnp.sum(held * held, axis=1, keepdims=True) / width + EPSILON)
        inverse[rows, :] = scale
        normed[rows, :] = (held * scale * gain).astype(BF16)

    each_block(norm_rows)
    px[8 : 8 + padded, :] = dot(normed[...], in_weight[0])
    pz[...] = dot(normed[...], in_weight[1])

    taps = conv_weight[...].astype(F32)

    def conv_rows(block):
        base = pl.multiple_of(block * BLOCK, BLOCK)
        rows = rows_at(block)
        slot = iota((BLOCK, 1), 0) + block * BLOCK
        valid = jnp.where(slot < count, 1.0, 0.0)
        window = px[pl.ds(base, BLOCK + 16), :]
        for r in range(2):
            total = conv_bias[r : r + 1, :]
            for k in range(4):
                shift = k - 3 if r == 0 else 3 - k
                total = total + taps[r, k : k + 1, :] * window[8 + shift : 8 + shift + BLOCK, :]
            logistic = jax.nn.sigmoid(total)
            act[r, rows, :] = (total * logistic * valid).astype(BF16)
            slope[r, rows, :] = logistic * (1.0 + total * (1.0 - logistic)) * valid

    each_block(conv_rows)
    part[...] = dot_nt(act[0], xw_cat[0]) + dot_nt(act[1], xw_cat[1])
    send_part = remote(part, part_in, 2)
    send_part.start()

    send_cot.wait()
    gout_f[0:half_pad, :] = cot_pair[0].astype(F32)
    gout_f[half_pad:, :] = jnp.zeros((gout_f.shape[0] - half_pad, width), F32)
    gout_f[half_slots : half_slots + half_pad, :] = cot_pair[1].astype(F32)
    gout[...] = gout_f[0:padded, :].astype(BF16)
    up[...] = dot_nt(gout[...], out_weight[...])

    def gate_rows(block):
        rows = rows_at(block)
        value = pz[rows, :]
        logistic = jax.nn.sigmoid(value)
        silu = value * logistic
        half_grad = 0.5 * up[rows, :]
        gate[rows, :] = 0.5 * silu
        zslope[rows, :] = half_grad * logistic * (1.0 + value * (1.0 - logistic))
        up[rows, :] = half_grad * silu

    each_block(gate_rows)

    send_part.wait()

    diagonal = jnp.where(iota((BLOCK, 1024), 0) == (iota((BLOCK, 1024), 1) // state) % BLOCK, 1.0, 0.0)

    def proj_rows(block):
        rows = rows_at(block)
        low = (part[rows, :] + part_in[rows, :]).astype(BF16)
        projb[rows, :] = low
        value = low.astype(F32)
        turned_rows[block] = value.T

    each_block(proj_rows)
    spread_rows[...] = dot(projb[...], sel[...])

    def mask_rows(block):
        rows = rows_at(block)
        blkm[rows, :] = (spread_rows[rows, :] * diagonal).astype(BF16)

    each_block(mask_rows)

    for r in range(2):
        sig[r] = dot(projb[...], dtw_pad[r])

    def delta_rows(block):
        rows = rows_at(block)
        for r in range(2):
            pre = sig[r, rows, :] + dt_bias[r : r + 1, :]
            small = jnp.exp(-jnp.abs(pre))
            inv = 1.0 / (1.0 + small)
            sig[r, rows, :] = jnp.where(pre >= 0.0, inv, small * inv)
            soft_plus = jnp.maximum(pre, 0.0) + jnp.log1p(small)
            delta[r, rows, :] = soft_plus
            u[r, rows, :] = soft_plus * act[r, rows, :].astype(F32)

    each_block(delta_rows)

    def state_rows(place):
        return pl.ds(pl.multiple_of(place * 16, 16), 16)

    def emit_y(step):
        for r in range(2):
            block = step if r == 0 else blocks - 1 - step
            first_row = block * 256 + (16 if r == 0 else 0)
            held = states[r, pl.ds(pl.multiple_of(first_row, 16), 256), :]
            ys[r, rows_at(block), :] = dot(
                blkm[rows_at(block), 512 * r + 256 : 512 * r + 512], held
            )

    def forward_step(step, carry):
        emit_y(jnp.maximum(step - 1, 0))
        out = []
        for r in range(2):
            held = carry[r]
            block = step if r == 0 else blocks - 1 - step
            base = block * BLOCK
            b_cols = turned_rows[block, 64 * r + rank : 64 * r + rank + state, :]
            for j in range(BLOCK):
                t = j if r == 0 else BLOCK - 1 - j
                decay = jnp.exp2(delta[r, pl.ds(base + t, 1), :] * rates2[r])
                b_wide = jnp.broadcast_to(b_cols[:, t : t + 1], (state, inner_w))
                held = decay * held + u[r, pl.ds(base + t, 1), :] * b_wide
                states[r, state_rows(base + t + (1 if r == 0 else 0)), :] = held.astype(BF16)
            out.append(held)
        return tuple(out)

    zero_state = jnp.zeros((state, inner_w), F32)
    lax.fori_loop(0, blocks, forward_step, (zero_state, zero_state))
    emit_y(blocks - 1)

    def mix_rows(block):
        rows = rows_at(block)
        summed = ys[0, rows, :] + ys[1, rows, :]
        for r in range(2):
            summed = summed + skip_gain[r : r + 1, :] * act[r, rows, :].astype(F32)
        gated[rows, :] = (summed * gate[rows, :]).astype(BF16)
        zgrad[rows, :] = (summed * zslope[rows, :]).astype(BF16)

    each_block(mix_rows)
    terms[0:padded, :] = dot(gated[...], out_weight[...])
    terms_pair[0] = terms[0:half_pad, :]
    terms_pair[1] = terms[half_slots : half_slots + half_pad, :]
    send_terms = remote(terms_pair.at[peer], terms_in, 3)
    send_terms.start()
    early.put(0, dot_tn(gated[...], gout[...]))
    early.put(inner_w // BLOCK * (width // 128), dot_tn(normed[...], zgrad[...]))
    early.first()
    npart[...] = dot_nt(zgrad[...], in_weight[1])

    adj_refs, car_refs = (adj_0, adj_1), (car_0, car_1)
    bsum_refs, csum_refs = (bsum_0, bsum_1), (csum_0, csum_1)
    block_mask = diagonal[:, 0:256]
    ones_block = block_mask.astype(BF16)
    ones_rows = jnp.ones((BLOCK, 128), BF16)

    def fold_lanes(value):
        total = value[:, 0:128]
        for at in range(128, inner_w, 128):
            total = total + value[:, at : at + 128]
        return total.astype(BF16)

    def emit_back(step):
        for r in range(2):
            block = blocks - 1 - step if r == 0 else step
            rows = rows_at(block)
            s1[r, rows, :] = dot(blkm[rows, 512 * r : 512 * r + 256], adj_refs[r][...])
            cas[r, rows, :] = dot(ones_block, car_refs[r][...])
            b_sums = dot_nt(ones_rows, bsum_refs[r][...])
            c_sums = dot_nt(ones_rows, csum_refs[r][...])
            pgm[rows, 512 * r : 512 * r + 256] = (b_sums * block_mask).astype(BF16)
            pgm[rows, 512 * r + 256 : 512 * r + 512] = (c_sums * block_mask).astype(BF16)

    def backward_step(step, carry):
        emit_back(jnp.maximum(step - 1, 0))
        out = []
        for r in range(2):
            passed, rate_sum, after = carry[r]
            block = blocks - 1 - step if r == 0 else step
            base = block * BLOCK
            c_cols = turned_rows[block, 64 * r + rank + state : 64 * r + rank + 2 * state, :]
            for j in range(BLOCK):
                t = BLOCK - 1 - j if r == 0 else j
                own = slice(t * 16, t * 16 + 16)
                step_size = delta[r, pl.ds(base + t, 1), :]
                upstream = up[pl.ds(base + t, 1), :]
                decay = jnp.exp2(step_size * rates2[r])
                c_wide = jnp.broadcast_to(c_cols[:, t : t + 1], (state, inner_w))
                adjoint = upstream * c_wide + passed
                passed = decay * adjoint
                adj_refs[r][own, :] = adjoint.astype(BF16)
                before = states[r, state_rows(base + t + (0 if r == 0 else 1)), :].astype(F32)
                carried = passed * before
                car_refs[r][own, :] = (carried * rates[r]).astype(BF16)
                rate_sum = rate_sum + carried * step_size
                bsum_refs[r][own, :] = fold_lanes(adjoint * u[r, pl.ds(base + t, 1), :])
                csum_refs[r][own, :] = fold_lanes(after * upstream)
                after = before
            out.append((passed, rate_sum, after))
        return tuple(out)

    last = states[0, padded * 16 : padded * 16 + 16, :].astype(F32)
    top = states[1, 0:16, :].astype(F32)
    cuts = [0, blocks * 2 // 5, blocks * 7 // 10, blocks]
    final = ((zero_state, zero_state, last), (zero_state, zero_state, top))
    final = lax.fori_loop(cuts[0], cuts[1], backward_step, final)
    early.second()
    final = lax.fori_loop(cuts[1], cuts[2], backward_step, final)
    early.third()
    final = lax.fori_loop(cuts[2], cuts[3], backward_step, final)
    emit_back(blocks - 1)
    early.fourth()
    wide_tiles = inner_w // 128
    at_xw = width // BLOCK * wide_tiles
    at_dtw = at_xw + 2 * (rank + 2 * state) // BLOCK * wide_tiles
    at_alog = at_dtw + 2 * rank // BLOCK * wide_tiles
    at_small = at_alog + 2 * state // BLOCK * wide_tiles
    late.put(at_alog, jnp.concatenate([final[r][1] * rates[r] for r in range(2)], 0))

    def soft_rows(block, carry):
        rows = rows_at(block)
        slot = iota((BLOCK, 1), 0) + block * BLOCK
        valid = slot < count
        out = []
        upstream = up[rows, :]
        for r in range(2):
            bias_sum, skip_sum, delta_sum, square_sum = carry[r]
            active = act[r, rows, :].astype(F32)
            step_size = delta[r, rows, :]
            first_sum = s1[r, rows, :]
            pre_grad = (active * first_sum + cas[r, rows, :]) * sig[r, rows, :]
            soft[r, rows, :] = pre_grad.astype(BF16)
            actg[r, rows, :] = first_sum * step_size + skip_gain[r : r + 1, :] * upstream
            kept_step = jnp.where(valid, step_size, 0.0)
            out.append(
                (
                    bias_sum + pre_grad,
                    skip_sum + upstream * active,
                    delta_sum + kept_step,
                    square_sum + kept_step * step_size,
                )
            )
        return tuple(out)

    wide = jnp.zeros((BLOCK, inner_w), F32)
    sums = lax.fori_loop(0, blocks, soft_rows, ((wide,) * 4,) * 2)
    pgrad[...] = (
        dot_nt(pgm[...], sel[...]) + dot_nt(soft[0], dtw_pad[0]) + dot_nt(soft[1], dtw_pad[1])
    )
    send_pgrad = remote(pgrad, pgrad_in, 4)
    send_pgrad.start()
    def total(value):
        return jnp.sum(value, axis=0, keepdims=True)

    low_grads = [
        dot_tn(projb[...], soft[r])[64 * r : 64 * r + rank, :] for r in range(2)
    ]
    late.put(at_dtw, jnp.concatenate(low_grads, 0))
    for r in range(2):
        tiny[r : r + 1, :] = total(sums[r][2])
        tiny[2 + r : 3 + r, :] = total(sums[r][3])
    tiny[5:8, :] = jnp.full((3, inner_w), count.astype(F32))

    send_terms.wait()
    gathered_half = jnp.where(
        inner == 0, gathered[0:half_slots, :], gathered[half_slots : 2 * half_slots, :]
    )
    mixer = terms_pair[inner][0:half_slots, :] + terms_in[0:half_slots, :]
    output[...] = jnp.where(cot_rows < count, gathered_half + mixer, 0.0).astype(BF16)

    send_pgrad.wait()
    pgb[...] = (pgrad[...] + pgrad_in[...]).astype(BF16)
    xwidth = rank + 2 * state
    xw_grads = [dot_tn(pgb[...], act[r])[64 * r : 64 * r + xwidth, :] for r in range(2)]
    late.put(at_xw, jnp.concatenate(xw_grads, 0))
    for r in range(2):
        actg[r] = actg[r] + dot(pgb[...], xw_cat[r])

    def back_rows(block):
        rows = rows_at(block)
        inside = pl.ds(pl.multiple_of(block * BLOCK, BLOCK) + 8, BLOCK)
        for r in range(2):
            cgrad[r, inside, :] = actg[r, rows, :] * slope[r, rows, :]

    each_block(back_rows)

    def conv_back_rows(block, carry):
        base = pl.multiple_of(block * BLOCK, BLOCK)
        window = px[pl.ds(base, BLOCK + 16), :]
        total = jnp.zeros((BLOCK, inner_w), F32)
        out = []
        for r in range(2):
            grads = cgrad[r, pl.ds(base, BLOCK + 16), :]
            here = grads[8 : 8 + BLOCK, :]
            for k in range(4):
                shift = k - 3 if r == 0 else 3 - k
                total = total + taps[r, k : k + 1, :] * grads[8 - shift : 8 - shift + BLOCK, :]
                out.append(carry[5 * r + k] + here * window[8 + shift : 8 + shift + BLOCK, :])
            out.append(carry[5 * r + 4] + here)
        xgrad[rows_at(block), :] = total.astype(BF16)
        return tuple(out)

    conv_sums = lax.fori_loop(0, blocks, conv_back_rows, (wide,) * 10)
    late.put(0, dot_tn(normed[...], xgrad[...]))
    small = [total(conv_sums[5 * r + k]) for r in range(2) for k in range(4)]
    small += [total(conv_sums[5 * r + 4]) for r in range(2)]
    small += [total(sums[r][i]) for i in range(2) for r in range(2)]
    small += [jnp.zeros((BLOCK - len(small), inner_w), F32)]
    late.put(at_small, jnp.concatenate(small, 0))
    late.first()
    npart[...] = npart[...] + dot_nt(xgrad[...], in_weight[0])
    send_npart = remote(npart, npart_in, 5)
    send_npart.start()

    send_npart.wait()

    def slot_rows(block, carry):
        rows = rows_at(block)
        whole = npart[rows, :] + npart_in[rows, :]
        held = gathered[rows, :]
        scale = inverse[rows, :]
        by_gain = whole * held * scale
        scaled = whole * gain
        row_dot = jnp.sum(scaled * held, axis=1, keepdims=True)
        factor = scale * scale * scale * row_dot / width
        grad = scale * scaled - held * factor + gout_f[rows, :]
        slot = iota((BLOCK, 1), 0) + block * BLOCK
        sgrad[rows, :] = jnp.where(slot < count, grad, 0.0).astype(BF16)
        return carry + by_gain

    gain_sum = lax.fori_loop(0, blocks, slot_rows, wide, unroll=5)
    tiny[4:5, :] = total(gain_sum)

    def tiny_sends(source, target, peer_of, mine, number, base):
        copies = []
        for offset in range(1, number):
            copies.append(
                pltpu.make_async_remote_copy(
                    src_ref=source,
                    dst_ref=target.at[mine],
                    send_sem=tiny_sems.at[0, base + offset - 1],
                    recv_sem=tiny_sems.at[1, base + offset - 1],
                    device_id={"rows": peer_of(offset)},
                    device_id_type=MESH,
                )
            )
            copies[-1].start()
        return copies

    copies = tiny_sends(tiny, tiny_low, near_peer, my_near, near, 0)
    late.second()

    slot_lane = iota((1, slots), 1)
    places = jnp.where(slot_lane < count, kept_row - first, -1.0)
    spread = 112

    def scatter_rows(step, carry):
        base = pl.multiple_of(step * spread, 16)
        row = (iota((spread, slots), 0) + step * spread).astype(F32)
        chosen = jnp.where(row == places, 1.0, 0.0).astype(BF16)
        hidden_grad[pl.ds(base, spread), :] = dot(chosen, sgrad[0:slots, :]).astype(BF16)
        return carry

    lax.fori_loop(0, half_full // spread, scatter_rows, 0)
    for copy in copies:
        copy.wait()
    held = tiny[...]
    for offset in range(1, near):
        held = held + tiny_low[lax.rem(my_near + offset, near)]
    tiny_mid[...] = held
    copies = tiny_sends(tiny_mid, tiny_high, far_peer, my_far, far, near - 1)
    late.third()
    for copy in copies:
        copy.wait()
    held = tiny_mid[...]
    for offset in range(1, far):
        held = held + tiny_high[lax.rem(my_far + offset, far)]
    tiny_out[...] = held
    late.fourth()
    early.finish()
    late.finish()


def finish_kernel(
    tiles,
    early_a,
    early_b,
    late_a,
    late_b,
    tiny,
    output_in,
    hidden_in,
    inner_ref,
    output,
    hidden_grad,
    gain_grad,
    in_grad,
    conv_w_grad,
    conv_b_grad,
    xw_grad,
    dtw_grad,
    dtb_grad,
    alog_grad,
    skip_grad,
    out_grad,
    dt_mean,
    dt_var,
):
    rank, state = dtw_grad.shape[1], alog_grad.shape[1]
    xwidth = rank + 2 * state
    width, inner_w = in_grad.shape[1:]
    wide_tiles = inner_w // 128

    def take(pair, first, rows, columns):
        parts = []
        for tile in range(rows // BLOCK):
            line = []
            for lane in range(columns // 128):
                ref, at = tile_at(pair, first + tile * (columns // 128) + lane)
                line.append(ref[at])
            parts.append(jnp.concatenate(line, 1))
        return jnp.concatenate(parts, 0).astype(F32)

    early, late = (early_a, early_b), (late_a, late_b)
    out_grad[...] = take(early, 0, inner_w, width)
    in_grad[1] = take(early, inner_w // BLOCK * (width // 128), width, inner_w)
    in_grad[0] = take(late, 0, width, inner_w)
    at = width // BLOCK * wide_tiles
    both = take(late, at, 2 * xwidth, inner_w)
    for r in range(2):
        xw_grad[r] = both[r * xwidth : (r + 1) * xwidth, :]
    at += 2 * xwidth // BLOCK * wide_tiles
    both = take(late, at, 2 * rank, inner_w)
    for r in range(2):
        dtw_grad[r] = both[r * rank : (r + 1) * rank, :]
    at += 2 * rank // BLOCK * wide_tiles
    both = take(late, at, 2 * state, inner_w)
    for r in range(2):
        alog_grad[r] = both[r * state : (r + 1) * state, :]
    at += 2 * state // BLOCK * wide_tiles
    small = take(late, at, BLOCK, inner_w)
    for r in range(2):
        conv_w_grad[r] = small[4 * r : 4 * r + 4, :]
    conv_b_grad[...] = small[8:10, :]
    dtb_grad[...] = small[10:12, :]
    skip_grad[...] = small[12:14, :]
    sums = tiny[...]
    mean = sums[0:2, :] / sums[5:6, :]
    dt_mean[...] = mean
    dt_var[...] = sums[2:4, :] / sums[5:6, :] - mean * mean
    part = width // 2
    gain = jnp.where(inner_ref[0] == 0, sums[4:5, 0:part], sums[4:5, part:width])
    gain_grad[...] = gain.reshape(part)
    output[...] = output_in[...]
    hidden_grad[...] = hidden_in[...]


def per_device(
    hidden,
    kept,
    counts,
    norm_gain,
    in_weight,
    conv_weight,
    conv_bias,
    x_weight,
    dt_weight,
    dt_bias,
    a_log,
    skip_gain,
    out_weight,
    cotangent,
):
    half_full, width = hidden.shape[1:]
    slots = kept.shape[1]
    half_slots = cotangent.shape[1]
    padded = round_up(slots, BLOCK)
    half_pad = round_up(half_slots, BLOCK)
    inner_w = in_weight.shape[2]
    rank = dt_weight.shape[1]
    state = a_log.shape[1]
    xwidth = x_weight.shape[2]
    rows_count = lax.axis_size("rows")
    near = 4 if rows_count % 4 == 0 else 1
    far = rows_count // near
    sizes = (
        half_full, width, slots, padded, half_slots, half_pad, inner_w, rank, state, near, far
    )
    wide_tiles = inner_w // 128
    early_tiles = 2 * (inner_w // BLOCK) * (width // 128)
    late_rows = width + 2 * xwidth + 2 * rank + 2 * state + BLOCK
    late_tiles = late_rows // BLOCK * wide_tiles

    def shape(*dims, kind=F32):
        return jax.ShapeDtypeStruct(dims, kind)

    vm = pltpu.VMEM
    sum_outs, sum_scratch = [], []
    for tiles in (early_tiles, late_tiles):
        for each, (one, two) in zip(
            chunk_tiles(tiles, rows_count), ((near, far), (far, near))
        ):
            sum_outs.append(shape(one, two, each * BLOCK, 128, kind=BF16))
            sum_scratch += [
                vm((one, two, each * BLOCK, 128), BF16),
                vm((one, two, each * BLOCK, 128), BF16),
                vm((two, each * BLOCK, 128), BF16),
                vm((two, each * BLOCK, 128), BF16),
            ]
    outs = [
        shape(half_slots, width, kind=BF16),
        shape(half_full, width, kind=BF16),
        *sum_outs,
        shape(8, inner_w),
    ]
    scratch = [
        vm((padded, width), BF16),
        vm((padded, width), BF16),
        vm((2, half_pad, width), BF16),
        vm((round_up(half_slots + half_pad, BLOCK) + 16, width), F32),
        vm((padded, width), BF16),
        vm((padded, width), F32),
        vm((padded, 1), F32),
        vm((padded, width), BF16),
        vm((padded + 16, inner_w), F32),
        vm((padded, inner_w), F32),
        vm((2, padded, inner_w), F32),
        vm((2, padded, inner_w), BF16),
        vm((2, 128, inner_w), BF16),
        vm((2, 128, inner_w), BF16),
        vm((2, state, inner_w), F32),
        vm((2, state, inner_w), F32),
        vm((padded, 128), F32),
        vm((padded, 128), F32),
        vm((padded, 128), F32),
        vm((padded, 128), BF16),
        vm((2, padded, inner_w), F32),
        vm((2, padded, inner_w), F32),
        vm((2, padded, inner_w), F32),
        vm((padded, inner_w), F32),
        vm((padded, inner_w), F32),
        vm((padded, inner_w), F32),
        vm((padded, inner_w), BF16),
        vm((padded, inner_w), BF16),
        vm((round_up(half_slots + half_pad, BLOCK), width), F32),
        vm((2, half_pad, width), F32),
        vm((half_pad, width), F32),
        vm((padded, 1024), BF16),
        vm((padded // BLOCK, 128, BLOCK), F32),
        vm((128, 1024), BF16),
        vm((2, padded * 16 + 16, inner_w), BF16),
        vm((2, padded, inner_w), F32),
        vm((256, inner_w), BF16),
        vm((256, inner_w), BF16),
        vm((256, inner_w), BF16),
        vm((256, inner_w), BF16),
        vm((256, 128), BF16),
        vm((256, 128), BF16),
        vm((256, 128), BF16),
        vm((256, 128), BF16),
        vm((2, padded, inner_w), F32),
        vm((2, padded, inner_w), F32),
        vm((padded, 1024), BF16),
        vm((2, padded, inner_w), BF16),
        vm((2, padded, inner_w), F32),
        vm((padded, 128), F32),
        vm((padded, 128), F32),
        vm((padded, 128), BF16),
        vm((2, padded + 16, inner_w), F32),
        vm((padded, inner_w), BF16),
        vm((padded, width), F32),
        vm((padded, width), BF16),
        vm((padded, width), F32),
        vm((padded, width), BF16),
        vm((padded, half_full), BF16),
        vm((padded, 1024), F32),
        *sum_scratch,
        vm((8, inner_w), F32),
        vm((near, 8, inner_w), F32),
        vm((8, inner_w), F32),
        vm((far, 8, inner_w), F32),
        pltpu.SemaphoreType.DMA((6,)),
        pltpu.SemaphoreType.DMA((6,)),
        pltpu.SemaphoreType.DMA((4, 2, near + far - 2)),
        pltpu.SemaphoreType.DMA((4, 2, near + far - 2)),
        pltpu.SemaphoreType.DMA((2, near + far - 2)),
    ]
    in_vmem = pl.BlockSpec(memory_space=pltpu.VMEM)
    in_smem = pl.BlockSpec(memory_space=pltpu.SMEM)
    in_specs = [in_vmem, in_vmem, in_smem] + [in_vmem] * 11
    output, hidden_grad, *sums, tiny = pl.pallas_call(
        functools.partial(block_kernel, sizes),
        out_shape=outs,
        in_specs=in_specs,
        out_specs=[in_vmem] * len(outs),
        scratch_shapes=scratch,
        compiler_params=pltpu.CompilerParams(
            collective_id=0, has_side_effects=True, vmem_limit_bytes=63 * 2**20
        ),
    )(
        hidden[0],
        kept,
        counts,
        norm_gain,
        in_weight,
        conv_weight,
        conv_bias,
        jnp.swapaxes(x_weight, 1, 2),
        dt_weight,
        dt_bias,
        a_log,
        skip_gain,
        out_weight,
        cotangent[0],
    )
    inner_index = lax.axis_index("inner").astype(jnp.int32)[None]
    outs = [
        shape(half_slots, width, kind=BF16),
        shape(half_full, width, kind=BF16),
        shape(width // lax.axis_size("inner")),
        shape(2, width, inner_w),
        shape(2, 4, inner_w),
        shape(2, inner_w),
        shape(2, xwidth, inner_w),
        shape(2, rank, inner_w),
        shape(2, inner_w),
        shape(2, state, inner_w),
        shape(2, inner_w),
        shape(inner_w, width),
        shape(2, inner_w),
        shape(2, inner_w),
    ]
    outs = pl.pallas_call(
        functools.partial(finish_kernel, None),
        out_shape=outs,
        in_specs=[in_vmem] * 7 + [in_smem],
        out_specs=[in_vmem] * len(outs),
        compiler_params=pltpu.CompilerParams(vmem_limit_bytes=32 * 2**20),
    )(*sums, tiny, output, hidden_grad, inner_index)
    outs = list(outs)
    outs[0], outs[1] = outs[0][None], outs[1][None]
    outs[6] = jnp.swapaxes(outs[6], 1, 2)
    return tuple(outs)


def solution(mesh):
    in_specs = (
        P("rows", "inner", None),
        P("rows", None),
        P("rows"),
        P(),
        P(None, None, "inner"),
        P(None, None, "inner"),
        P(None, "inner"),
        P(None, "inner", None),
        P(None, None, "inner"),
        P(None, "inner"),
        P(None, None, "inner"),
        P(None, "inner"),
        P("inner", None),
        P("rows", "inner", None),
    )
    out_specs = (
        P("rows", "inner", None),
        P("rows", "inner", None),
        P("inner"),
        P(None, None, "inner"),
        P(None, None, "inner"),
        P(None, "inner"),
        P(None, "inner", None),
        P(None, None, "inner"),
        P(None, "inner"),
        P(None, None, "inner"),
        P(None, "inner"),
        P("inner", None),
        P(None, "inner"),
        P(None, "inner"),
    )
    return jax.shard_map(
        per_device, mesh=mesh, in_specs=in_specs, out_specs=out_specs, check_vma=False
    )
```

```python
import functools

import jax
import jax.numpy as jnp
from jax import lax
from jax.experimental import pallas as pl
from jax.experimental.pallas import tpu as pltpu
from jax.sharding import PartitionSpec as P

EPSILON = 1e-05
BLOCK = 16
LOG2E = 1.4426950408889634
MESH = pl.DeviceIdType.MESH
F32 = jnp.float32
BF16 = jnp.bfloat16


def dot(left, right):
    return jnp.dot(left, right, preferred_element_type=F32)


def dot_nt(left, right):
    return lax.dot_general(left, right, (((1,), (1,)), ((), ())), preferred_element_type=F32)


def dot_tn(left, right):
    return lax.dot_general(left, right, (((0,), (0,)), ((), ())), preferred_element_type=F32)


def logistic_of(value):
    return 0.5 * jnp.tanh(0.5 * value) + 0.5


def iota(shape, axis):
    return lax.broadcasted_iota(jnp.int32, shape, axis)


def round_up(value, unit):
    return (value + unit - 1) // unit * unit


def chunk_tiles(total, devices):
    each = -(-total // devices)
    first = max(1, each * 2 // 3)
    return first, max(1, each - first)


def tile_at(pair, tile):
    ref = pair[0]
    capacity = ref.shape[0] * ref.shape[1] * ref.shape[2] // BLOCK
    if tile >= capacity:
        tile, ref = tile - capacity, pair[1]
    each = ref.shape[2] // BLOCK
    chunk, place = tile // each, tile % each
    outer, middle = chunk // ref.shape[1], chunk % ref.shape[1]
    return ref, (outer, middle, slice(place * BLOCK, place * BLOCK + BLOCK), slice(None))


class Reducer:
    def __init__(self, a, b, sems, near, far, my_near, my_far, near_peer, far_peer):
        self.ways = [
            (a, (near, my_near, near_peer), (far, my_far, far_peer)),
            (b, (far, my_far, far_peer), (near, my_near, near_peer)),
        ]
        self.sems = sems
        self.copies = []

    def put(self, first, value):
        columns = value.shape[1] // 128
        pair = (self.ways[0][0][0], self.ways[1][0][0])
        for tile in range(value.shape[0] // BLOCK):
            for lane in range(columns):
                ref, at = tile_at(pair, first + tile * columns + lane)
                part = value[tile * BLOCK : tile * BLOCK + BLOCK, lane * 128 : lane * 128 + 128]
                ref[at] = part.astype(BF16)

    def send(self, phase, make):
        self.copies = []
        place = 0
        for refs, one, two in self.ways:
            number, mine, peer_of = one if phase in (0, 3) else two
            for offset in range(1, number):
                source, target = make(refs, one, two, lax.rem(mine + offset, number))
                copy = pltpu.make_async_remote_copy(
                    src_ref=source,
                    dst_ref=target,
                    send_sem=self.sems.at[phase, 0, place],
                    recv_sem=self.sems.at[phase, 1, place],
                    device_id={"rows": peer_of(offset)},
                    device_id_type=MESH,
                )
                copy.start()
                self.copies.append(copy)
                place += 1

    def wait(self):
        for copy in self.copies:
            copy.wait()

    def first(self):
        self.send(0, lambda refs, one, two, other: (refs[0].at[other], refs[1].at[one[1]]))

    def second(self):
        self.wait()
        for refs, one, two in self.ways:
            number, mine, _ = one
            for part in range(two[0]):
                held = refs[0][mine, part].astype(F32)
                for offset in range(1, number):
                    held = held + refs[1][lax.rem(mine + offset, number), part].astype(F32)
                refs[2][part] = held.astype(BF16)
        self.send(1, lambda refs, one, two, other: (refs[2].at[other], refs[3].at[two[1]]))

    def third(self):
        self.wait()
        for refs, one, two in self.ways:
            number, mine, _ = two
            held = refs[2][mine].astype(F32)
            for offset in range(1, number):
                held = held + refs[3][lax.rem(mine + offset, number)].astype(F32)
            refs[4][one[1], mine] = held.astype(BF16)
        self.send(
            2,
            lambda refs, one, two, other: (
                refs[4].at[one[1], two[1]],
                refs[4].at[one[1], two[1]],
            ),
        )

    def fourth(self):
        self.wait()
        self.send(3, lambda refs, one, two, other: (refs[4].at[one[1]], refs[4].at[one[1]]))

    def finish(self):
        self.wait()


def block_kernel(
    sizes,
    hidden,
    kept,
    counts,
    norm_gain,
    in_weight,
    conv_weight,
    conv_bias,
    x_weight,
    dt_weight,
    dt_bias,
    a_log,
    skip_gain,
    out_weight,
    cotangent,
    output,
    hidden_grad,
    early_a_out,
    early_b_out,
    mid_a_out,
    mid_b_out,
    late_a_out,
    late_b_out,
    tiny_out,
    picked,
    picked_in,
    cot_pair,
    gout_f,
    gout,
    gathered,
    inverse,
    normed,
    px,
    pz,
    slope,
    act,
    xw_cat,
    dtw_pad,
    rates2,
    rates,
    part,
    part_in,
    proj,
    projb,
    delta,
    sig,
    u,
    up,
    gate,
    zslope,
    zgrad,
    gated,
    terms,
    terms_pair,
    terms_in,
    blkm,
    turned_rows,
    sel,
    states,
    ys,
    adj_0,
    adj_1,
    car_0,
    car_1,
    csum_0,
    csum_1,
    s1,
    cas,
    pgm,
    soft,
    actg,
    pgrad,
    pgrad_in,
    pgb,
    cgrad,
    xgrad,
    npart,
    npart_b,
    npart_in,
    sgrad,
    chosen,
    spread_rows,
    early_a,
    early_a1,
    early_am,
    early_a2,
    early_b,
    early_b1,
    early_bm,
    early_b2,
    mid_a,
    mid_a1,
    mid_am,
    mid_a2,
    mid_b,
    mid_b1,
    mid_bm,
    mid_b2,
    late_a,
    late_a1,
    late_am,
    late_a2,
    late_b,
    late_b1,
    late_bm,
    late_b2,
    tiny,
    tiny_low,
    tiny_mid,
    tiny_high,
    send_sem,
    recv_sem,
    early_sems,
    mid_sems,
    late_sems,
    tiny_sems,
):
    half_full, width, slots, padded, half_slots, half_pad, inner_w, rank, state, near, far = sizes
    blocks = padded // BLOCK
    inner = lax.axis_index("inner")
    peer = 1 - inner

    def remote(source, target, index):
        return pltpu.make_async_remote_copy(
            src_ref=source,
            dst_ref=target,
            send_sem=send_sem.at[index],
            recv_sem=recv_sem.at[index],
            device_id={"inner": peer},
            device_id_type=MESH,
        )

    def rows_at(block):
        return pl.ds(pl.multiple_of(block * BLOCK, BLOCK), BLOCK)

    def each_block(body, unroll=5):
        def step(block, carry):
            body(block)
            return carry

        lax.fori_loop(0, blocks, step, 0, unroll=unroll)

    row = lax.axis_index("rows")
    my_near, my_far = lax.rem(row, near), row // near

    def near_peer(offset):
        return my_far * near + lax.rem(my_near + offset, near)

    def far_peer(offset):
        return lax.rem(my_far + offset, far) * near + my_near

    barrier = pltpu.get_barrier_semaphore()
    pl.semaphore_signal(barrier, inc=1, device_id={"inner": peer}, device_id_type=MESH)
    for offset in range(1, near):
        pl.semaphore_signal(
            barrier, inc=1, device_id={"rows": near_peer(offset)}, device_id_type=MESH
        )
    for offset in range(1, far):
        pl.semaphore_signal(
            barrier, inc=1, device_id={"rows": far_peer(offset)}, device_id_type=MESH
        )

    early = Reducer(
        (early_a, early_a1, early_am, early_a2, early_a_out),
        (early_b, early_b1, early_bm, early_b2, early_b_out),
        early_sems, near, far, my_near, my_far, near_peer, far_peer,
    )
    mid = Reducer(
        (mid_a, mid_a1, mid_am, mid_a2, mid_a_out),
        (mid_b, mid_b1, mid_bm, mid_b2, mid_b_out),
        mid_sems, near, far, my_near, my_far, near_peer, far_peer,
    )
    late = Reducer(
        (late_a, late_a1, late_am, late_a2, late_a_out),
        (late_b, late_b1, late_bm, late_b2, late_b_out),
        late_sems, near, far, my_near, my_far, near_peer, far_peer,
    )

    count = counts[0]
    kept_row = kept[...].astype(F32)
    first = (inner * half_full).astype(F32)

    own_cot = cotangent[...].astype(F32)
    cot_rows = iota((half_slots, 1), 0) + inner * half_slots
    own_cot = jnp.where(cot_rows < count, own_cot, 0.0)
    cot_full = jnp.concatenate([own_cot, jnp.zeros((half_pad - half_slots, width), F32)], 0)
    cot_pair[pl.ds(inner, 1)] = cot_full.astype(BF16)[None]

    def pick_rows(block):
        rows = iota((BLOCK, slots), 0) + block * BLOCK
        mine = jnp.where(rows == iota((BLOCK, slots), 1), kept_row, 0.0)
        place = jnp.sum(mine, axis=1, keepdims=True) - first
        slot = iota((BLOCK, 1), 0) + block * BLOCK
        place = jnp.where(slot < count, place, -1.0)
        column = iota((BLOCK, half_full), 1).astype(F32)
        chosen[rows_at(block), :] = jnp.where(place == column, 1.0, 0.0).astype(BF16)

    each_block(pick_rows)
    picked[...] = dot(chosen[...], hidden[...]).astype(BF16)
    pl.semaphore_wait(barrier, near + far - 1)
    send_pick = remote(picked, picked_in, 0)
    send_pick.start()
    send_cot = remote(cot_pair.at[inner], cot_pair.at[inner], 1)
    send_cot.start()

    def at_rows(value, r):
        parts = [value, jnp.zeros((128 - 64 * r - value.shape[0], inner_w), F32)]
        if r:
            parts = [jnp.zeros((64 * r, inner_w), F32)] + parts
        return jnp.concatenate(parts, 0).astype(BF16)

    for r in range(2):
        xw_cat[r] = at_rows(x_weight[r].astype(F32), r)
        dtw_pad[r] = at_rows(dt_weight[r].astype(F32), r)
        rate = -jnp.exp(a_log[r])
        rates[r] = rate
        rates2[r] = rate * LOG2E
    lane = iota((128, 1024), 1)
    chunk = lane // 256
    start = jnp.where(
        chunk == 0,
        rank,
        jnp.where(chunk == 1, rank + state, jnp.where(chunk == 2, 64 + rank, 64 + rank + state)),
    )
    sel[...] = jnp.where(iota((128, 1024), 0) == start + lane % state, 1.0, 0.0).astype(BF16)
    zero_rows = jnp.zeros((8, inner_w), F32)
    px[0:8, :] = zero_rows
    px[8 + padded : 16 + padded, :] = zero_rows
    for r in range(2):
        cgrad[r, 0:8, :] = zero_rows
        cgrad[r, 8 + padded : 16 + padded, :] = zero_rows
    states[0, 0:16, :] = jnp.zeros((16, inner_w), BF16)
    states[1, padded * 16 : padded * 16 + 16, :] = jnp.zeros((16, inner_w), BF16)

    send_pick.wait()
    gain = norm_gain[...].reshape(1, width)

    def norm_rows(block):
        rows = rows_at(block)
        held = picked[rows, :].astype(F32) + picked_in[rows, :].astype(F32)
        gathered[rows, :] = held
        scale = lax.rsqrt(jnp.sum(held * held, axis=1, keepdims=True) / width + EPSILON)
        inverse[rows, :] = scale
        normed[rows, :] = (held * scale * gain).astype(BF16)

    each_block(norm_rows)
    px[8 : 8 + padded, :] = dot(normed[...], in_weight[0])

    taps = conv_weight[...].astype(F32)

    def conv_rows(block):
        base = pl.multiple_of(block * BLOCK, BLOCK)
        rows = rows_at(block)
        slot = iota((BLOCK, 1), 0) + block * BLOCK
        valid = jnp.where(slot < count, 1.0, 0.0)
        window = px[pl.ds(base, BLOCK + 16), :]
        for r in range(2):
            total = conv_bias[r : r + 1, :]
            for k in range(4):
                shift = k - 3 if r == 0 else 3 - k
                total = total + taps[r, k : k + 1, :] * window[8 + shift : 8 + shift + BLOCK, :]
            logistic = logistic_of(total)
            act[r, rows, :] = (total * logistic * valid).astype(BF16)
            slope[r, rows, :] = logistic * (1.0 + total * (1.0 - logistic)) * valid

    each_block(conv_rows)
    part[...] = dot_nt(act[0], xw_cat[0]) + dot_nt(act[1], xw_cat[1])
    send_part = remote(part, part_in, 2)
    send_part.start()

    pz[...] = dot(normed[...], in_weight[1])
    send_cot.wait()
    gout_f[0:half_pad, :] = cot_pair[0].astype(F32)
    gout_f[half_pad:, :] = jnp.zeros((gout_f.shape[0] - half_pad, width), F32)
    gout_f[half_slots : half_slots + half_pad, :] = cot_pair[1].astype(F32)
    gout[...] = gout_f[0:padded, :].astype(BF16)
    up[...] = dot_nt(gout[...], out_weight[...])

    def gate_rows(block):
        rows = rows_at(block)
        value = pz[rows, :]
        logistic = logistic_of(value)
        silu = value * logistic
        half_grad = 0.5 * up[rows, :]
        gate[rows, :] = 0.5 * silu
        zslope[rows, :] = half_grad * logistic * (1.0 + value * (1.0 - logistic))
        up[rows, :] = half_grad * silu

    each_block(gate_rows)

    send_part.wait()

    diagonal = jnp.where(iota((BLOCK, 1024), 0) == (iota((BLOCK, 1024), 1) // state) % BLOCK, 1.0, 0.0)

    def proj_rows(block):
        rows = rows_at(block)
        low = (part[rows, :] + part_in[rows, :]).astype(BF16)
        projb[rows, :] = low

    each_block(proj_rows)
    quarter = iota((64, 128), 0) // state
    start = rank + quarter % 2 * state + quarter // 2 * 64
    picks = jnp.where(iota((64, 128), 1) == start + iota((64, 128), 0) % state, 1.0, 0.0)
    picks = picks.astype(BF16)

    turned = dot_nt(picks, projb[...])
    for block in range(blocks):
        turned_rows[block] = turned[:, block * BLOCK : block * BLOCK + BLOCK]
    spread_rows[...] = dot(projb[...], sel[...])

    def mask_rows(block):
        rows = rows_at(block)
        blkm[rows, :] = (spread_rows[rows, :] * diagonal).astype(BF16)

    each_block(mask_rows)

    for r in range(2):
        sig[r] = dot(projb[...], dtw_pad[r])

    def delta_rows(block):
        rows = rows_at(block)
        for r in range(2):
            pre = sig[r, rows, :] + dt_bias[r : r + 1, :]
            small = jnp.exp(-jnp.abs(pre))
            sig[r, rows, :] = pre
            soft_plus = jnp.maximum(pre, 0.0) + jnp.log1p(small)
            delta[r, rows, :] = soft_plus
            u[r, rows, :] = soft_plus * act[r, rows, :].astype(F32)

    each_block(delta_rows)

    def state_rows(place):
        return pl.ds(pl.multiple_of(place * 16, 16), 16)

    def emit_y(step):
        for r in range(2):
            block = step if r == 0 else blocks - 1 - step
            first_row = block * 256 + (16 if r == 0 else 0)
            held = states[r, pl.ds(pl.multiple_of(first_row, 16), 256), :]
            ys[r, rows_at(block), :] = dot(
                blkm[rows_at(block), 512 * r + 256 : 512 * r + 512], held
            )

    def forward_step(step, carry):
        emit_y(jnp.maximum(step - 1, 0))
        out = []
        for r in range(2):
            held = carry[r]
            block = step if r == 0 else blocks - 1 - step
            base = block * BLOCK
            b_cols = turned_rows[block, 32 * r : 32 * r + state, :]
            for j in range(BLOCK):
                t = j if r == 0 else BLOCK - 1 - j
                decay = jnp.exp2(delta[r, pl.ds(base + t, 1), :] * rates2[r])
                b_wide = jnp.broadcast_to(b_cols[:, t : t + 1], (state, inner_w))
                held = decay * held + u[r, pl.ds(base + t, 1), :] * b_wide
                states[r, state_rows(base + t + (1 if r == 0 else 0)), :] = held.astype(BF16)
            out.append(held)
        return tuple(out)

    zero_state = jnp.zeros((state, inner_w), F32)
    lax.fori_loop(0, blocks, forward_step, (zero_state, zero_state))
    emit_y(blocks - 1)

    def mix_rows(block):
        rows = rows_at(block)
        summed = ys[0, rows, :] + ys[1, rows, :]
        for r in range(2):
            summed = summed + skip_gain[r : r + 1, :] * act[r, rows, :].astype(F32)
        gated[rows, :] = (summed * gate[rows, :]).astype(BF16)
        zgrad[rows, :] = (summed * zslope[rows, :]).astype(BF16)

    each_block(mix_rows)
    early.put(0, dot_tn(gated[...], gout[...]))
    early.put(inner_w // BLOCK * (width // 128), dot_tn(normed[...], zgrad[...]))
    early.first()

    adj_refs, car_refs = (adj_0, adj_1), (car_0, car_1)
    csum_refs = (csum_0, csum_1)
    block_mask = diagonal[:, 0:256]
    ones_block = block_mask.astype(BF16)
    ones_rows = jnp.ones((BLOCK, 128), BF16)

    def fold_lanes(value):
        total = value[:, 0:128]
        for at in range(128, inner_w, 128):
            total = total + value[:, at : at + 128]
        return total.astype(BF16)

    def emit_back(step):
        for r in range(2):
            block = blocks - 1 - step if r == 0 else step
            rows = rows_at(block)
            s1[r, rows, :] = dot(blkm[rows, 512 * r : 512 * r + 256], adj_refs[r][...])
            cas[r, rows, :] = dot(ones_block, car_refs[r][...])
            b_sums = dot_nt(u[r, rows, :].astype(BF16), adj_refs[r][...])
            c_sums = dot_nt(ones_rows, csum_refs[r][...])
            pgm[rows, 512 * r : 512 * r + 256] = (b_sums * block_mask).astype(BF16)
            pgm[rows, 512 * r + 256 : 512 * r + 512] = (c_sums * block_mask).astype(BF16)

    def backward_step(step, carry):
        emit_back(jnp.maximum(step - 1, 0))
        out = []
        for r in range(2):
            passed, rate_sum, after = carry[r]
            block = blocks - 1 - step if r == 0 else step
            base = block * BLOCK
            c_cols = turned_rows[block, 32 * r + state : 32 * r + 2 * state, :]
            for j in range(BLOCK):
                t = BLOCK - 1 - j if r == 0 else j
                own = slice(t * 16, t * 16 + 16)
                step_size = delta[r, pl.ds(base + t, 1), :]
                upstream = up[pl.ds(base + t, 1), :]
                decay = jnp.exp2(step_size * rates2[r])
                c_wide = jnp.broadcast_to(c_cols[:, t : t + 1], (state, inner_w))
                adjoint = upstream * c_wide + passed
                passed = decay * adjoint
                adj_refs[r][own, :] = adjoint.astype(BF16)
                before = states[r, state_rows(base + t + (0 if r == 0 else 1)), :].astype(F32)
                carried = passed * before
                car_refs[r][own, :] = (carried * rates[r]).astype(BF16)
                rate_sum = rate_sum + carried * step_size
                csum_refs[r][own, :] = fold_lanes(after * upstream)
                after = before
            out.append((passed, rate_sum, after))
        return tuple(out)

    last = states[0, padded * 16 : padded * 16 + 16, :].astype(F32)
    top = states[1, 0:16, :].astype(F32)
    cuts = [0, blocks * 12 // 25, blocks * 21 // 25, blocks]
    final = ((zero_state, zero_state, last), (zero_state, zero_state, top))
    final = lax.fori_loop(cuts[0], cuts[1], backward_step, final)
    early.second()
    final = lax.fori_loop(cuts[1], cuts[2], backward_step, final)
    early.third()
    final = lax.fori_loop(cuts[2], cuts[3], backward_step, final)
    emit_back(blocks - 1)
    wide_tiles = inner_w // 128
    at_dtw = 2 * (rank + 2 * state) // BLOCK * wide_tiles
    at_alog = at_dtw + 2 * rank // BLOCK * wide_tiles
    at_small = at_alog + 2 * state // BLOCK * wide_tiles

    def soft_rows(block, carry):
        rows = rows_at(block)
        slot = iota((BLOCK, 1), 0) + block * BLOCK
        valid = slot < count
        out = []
        upstream = up[rows, :]
        for r in range(2):
            bias_sum, skip_sum, delta_sum, square_sum = carry[r]
            active = act[r, rows, :].astype(F32)
            step_size = delta[r, rows, :]
            first_sum = s1[r, rows, :]
            pre_grad = (active * first_sum + cas[r, rows, :]) * jnp.exp(sig[r, rows, :] - step_size)
            soft[r, rows, :] = pre_grad.astype(BF16)
            actg[r, rows, :] = first_sum * step_size + skip_gain[r : r + 1, :] * upstream
            kept_step = jnp.where(valid, step_size, 0.0)
            out.append(
                (
                    bias_sum + pre_grad,
                    skip_sum + upstream * active,
                    delta_sum + kept_step,
                    square_sum + kept_step * step_size,
                )
            )
        return tuple(out)

    wide = jnp.zeros((BLOCK, inner_w), F32)
    sums = lax.fori_loop(0, blocks, soft_rows, ((wide,) * 4,) * 2, unroll=5)
    pgrad[...] = (
        dot_nt(pgm[...], sel[...]) + dot_nt(soft[0], dtw_pad[0]) + dot_nt(soft[1], dtw_pad[1])
    )
    send_pgrad = remote(pgrad, pgrad_in, 4)
    send_pgrad.start()
    early.fourth()
    send_pgrad.wait()
    pgb[...] = (pgrad[...] + pgrad_in[...]).astype(BF16)
    for r in range(2):
        actg[r] = actg[r] + dot(pgb[...], xw_cat[r])

    def back_rows(block):
        rows = rows_at(block)
        inside = pl.ds(pl.multiple_of(block * BLOCK, BLOCK) + 8, BLOCK)
        for r in range(2):
            cgrad[r, inside, :] = actg[r, rows, :] * slope[r, rows, :]

    each_block(back_rows)

    def conv_back_rows(block):
        base = pl.multiple_of(block * BLOCK, BLOCK)
        total = jnp.zeros((BLOCK, inner_w), F32)
        for r in range(2):
            grads = cgrad[r, pl.ds(base, BLOCK + 16), :]
            for k in range(4):
                shift = k - 3 if r == 0 else 3 - k
                total = total + taps[r, k : k + 1, :] * grads[8 - shift : 8 - shift + BLOCK, :]
        xgrad[rows_at(block), :] = total.astype(BF16)

    each_block(conv_back_rows)
    late.put(0, dot_tn(normed[...], xgrad[...]))
    late.first()
    npart[...] = dot_nt(xgrad[...], in_weight[0]) + dot_nt(zgrad[...], in_weight[1])
    send_npart = remote(npart, npart_in, 5)
    send_npart.start()
    terms[0:padded, :] = dot(gated[...], out_weight[...])
    terms_pair[0] = terms[0:half_pad, :]
    terms_pair[1] = terms[half_slots : half_slots + half_pad, :]
    send_terms = remote(terms_pair.at[peer], terms_in, 3)
    send_terms.start()

    def conv_sum_rows(block, carry):
        base = pl.multiple_of(block * BLOCK, BLOCK)
        window = px[pl.ds(base, BLOCK + 16), :]
        out = []
        for r in range(2):
            here = cgrad[r, pl.ds(base + 8, BLOCK), :]
            for k in range(4):
                shift = k - 3 if r == 0 else 3 - k
                out.append(carry[5 * r + k] + here * window[8 + shift : 8 + shift + BLOCK, :])
            out.append(carry[5 * r + 4] + here)
        return tuple(out)

    conv_sums = lax.fori_loop(0, blocks, conv_sum_rows, (wide,) * 10)

    def total(value):
        return jnp.sum(value, axis=0, keepdims=True)

    low_grads = [
        dot_tn(projb[...], soft[r])[64 * r : 64 * r + rank, :] for r in range(2)
    ]
    mid.put(at_dtw, jnp.concatenate(low_grads, 0))
    for r in range(2):
        tiny[r : r + 1, :] = total(sums[r][2])
        tiny[2 + r : 3 + r, :] = total(sums[r][3])
    tiny[5:8, :] = jnp.full((3, inner_w), count.astype(F32))
    small = [total(conv_sums[5 * r + k]) for r in range(2) for k in range(4)]
    small += [total(conv_sums[5 * r + 4]) for r in range(2)]
    small += [total(sums[r][i]) for i in range(2) for r in range(2)]
    small += [jnp.zeros((BLOCK - len(small), inner_w), F32)]
    mid.put(at_small, jnp.concatenate(small, 0))
    xwidth = rank + 2 * state
    xw_grads = [dot_tn(pgb[...], act[r])[64 * r : 64 * r + xwidth, :] for r in range(2)]
    mid.put(0, jnp.concatenate(xw_grads, 0))

    mid.put(at_alog, jnp.concatenate([final[r][1] * rates[r] for r in range(2)], 0))
    mid.first()

    send_npart.wait()

    def slot_rows(block, carry):
        rows = rows_at(block)
        whole = npart[rows, :] + npart_in[rows, :]
        held = gathered[rows, :]
        scale = inverse[rows, :]
        by_gain = whole * held * scale
        scaled = whole * gain
        row_dot = jnp.sum(scaled * held, axis=1, keepdims=True)
        factor = scale * scale * scale * row_dot / width
        grad = scale * scaled - held * factor + gout_f[rows, :]
        slot = iota((BLOCK, 1), 0) + block * BLOCK
        sgrad[rows, :] = jnp.where(slot < count, grad, 0.0).astype(BF16)
        return carry + by_gain

    gain_sum = lax.fori_loop(0, blocks, slot_rows, wide, unroll=5)
    tiny[4:5, :] = total(gain_sum)

    def tiny_sends(source, target, peer_of, mine, number, base):
        copies = []
        for offset in range(1, number):
            copies.append(
                pltpu.make_async_remote_copy(
                    src_ref=source,
                    dst_ref=target.at[mine],
                    send_sem=tiny_sems.at[0, base + offset - 1],
                    recv_sem=tiny_sems.at[1, base + offset - 1],
                    device_id={"rows": peer_of(offset)},
                    device_id_type=MESH,
                )
            )
            copies[-1].start()
        return copies

    copies = tiny_sends(tiny, tiny_low, near_peer, my_near, near, 0)
    late.second()
    mid.second()

    send_terms.wait()
    gathered_half = jnp.where(
        inner == 0, gathered[0:half_slots, :], gathered[half_slots : 2 * half_slots, :]
    )
    mixer = terms_pair[inner][0:half_slots, :] + terms_in[0:half_slots, :]
    output[...] = jnp.where(cot_rows < count, gathered_half + mixer, 0.0).astype(BF16)


    slot_lane = iota((1, slots), 1)
    places = jnp.where(slot_lane < count, kept_row - first, -1.0)
    spread = 112

    def scatter_rows(step, carry):
        base = pl.multiple_of(step * spread, 16)
        row = (iota((spread, slots), 0) + step * spread).astype(F32)
        chosen = jnp.where(row == places, 1.0, 0.0).astype(BF16)
        hidden_grad[pl.ds(base, spread), :] = dot(chosen, sgrad[0:slots, :]).astype(BF16)
        return carry

    lax.fori_loop(0, half_full // spread, scatter_rows, 0)
    for copy in copies:
        copy.wait()
    held = tiny[...]
    for offset in range(1, near):
        held = held + tiny_low[lax.rem(my_near + offset, near)]
    tiny_mid[...] = held
    copies = tiny_sends(tiny_mid, tiny_high, far_peer, my_far, far, near - 1)
    late.third()
    mid.third()
    for copy in copies:
        copy.wait()
    held = tiny_mid[...]
    for offset in range(1, far):
        held = held + tiny_high[lax.rem(my_far + offset, far)]
    tiny_out[...] = held
    late.fourth()
    mid.fourth()
    early.finish()
    mid.finish()
    late.finish()


def finish_kernel(
    tiles,
    early_a,
    early_b,
    mid_a,
    mid_b,
    late_a,
    late_b,
    tiny,
    output_in,
    hidden_in,
    inner_ref,
    output,
    hidden_grad,
    gain_grad,
    in_grad,
    conv_w_grad,
    conv_b_grad,
    xw_grad,
    dtw_grad,
    dtb_grad,
    alog_grad,
    skip_grad,
    out_grad,
    dt_mean,
    dt_var,
):
    rank, state = dtw_grad.shape[1], alog_grad.shape[1]
    xwidth = rank + 2 * state
    width, inner_w = in_grad.shape[1:]
    wide_tiles = inner_w // 128

    def take(pair, first, rows, columns):
        parts = []
        for tile in range(rows // BLOCK):
            line = []
            for lane in range(columns // 128):
                ref, at = tile_at(pair, first + tile * (columns // 128) + lane)
                line.append(ref[at])
            parts.append(jnp.concatenate(line, 1))
        return jnp.concatenate(parts, 0).astype(F32)

    early, mid, late = (early_a, early_b), (mid_a, mid_b), (late_a, late_b)
    out_grad[...] = take(early, 0, inner_w, width)
    in_grad[1] = take(early, inner_w // BLOCK * (width // 128), width, inner_w)
    in_grad[0] = take(late, 0, width, inner_w)
    both = take(mid, 0, 2 * xwidth, inner_w)
    for r in range(2):
        xw_grad[r] = both[r * xwidth : (r + 1) * xwidth, :]
    at = 2 * xwidth // BLOCK * wide_tiles
    both = take(mid, at, 2 * rank, inner_w)
    for r in range(2):
        dtw_grad[r] = both[r * rank : (r + 1) * rank, :]
    at += 2 * rank // BLOCK * wide_tiles
    both = take(mid, at, 2 * state, inner_w)
    for r in range(2):
        alog_grad[r] = both[r * state : (r + 1) * state, :]
    at += 2 * state // BLOCK * wide_tiles
    small = take(mid, at, BLOCK, inner_w)
    for r in range(2):
        conv_w_grad[r] = small[4 * r : 4 * r + 4, :]
    conv_b_grad[...] = small[8:10, :]
    dtb_grad[...] = small[10:12, :]
    skip_grad[...] = small[12:14, :]
    sums = tiny[...]
    mean = sums[0:2, :] / sums[5:6, :]
    dt_mean[...] = mean
    dt_var[...] = sums[2:4, :] / sums[5:6, :] - mean * mean
    part = width // 2
    gain = jnp.where(inner_ref[0] == 0, sums[4:5, 0:part], sums[4:5, part:width])
    gain_grad[...] = gain.reshape(part)
    output[...] = output_in[...]
    hidden_grad[...] = hidden_in[...]


def per_device(
    hidden,
    kept,
    counts,
    norm_gain,
    in_weight,
    conv_weight,
    conv_bias,
    x_weight,
    dt_weight,
    dt_bias,
    a_log,
    skip_gain,
    out_weight,
    cotangent,
):
    half_full, width = hidden.shape[1:]
    slots = kept.shape[1]
    half_slots = cotangent.shape[1]
    padded = round_up(slots, BLOCK)
    half_pad = round_up(half_slots, BLOCK)
    inner_w = in_weight.shape[2]
    rank = dt_weight.shape[1]
    state = a_log.shape[1]
    xwidth = x_weight.shape[2]
    rows_count = lax.axis_size("rows")
    near = 4 if rows_count % 4 == 0 else 1
    far = rows_count // near
    sizes = (
        half_full, width, slots, padded, half_slots, half_pad, inner_w, rank, state, near, far
    )
    wide_tiles = inner_w // 128
    early_tiles = 2 * (inner_w // BLOCK) * (width // 128)
    mid_tiles = (2 * xwidth + 2 * rank + 2 * state + BLOCK) // BLOCK * wide_tiles
    late_tiles = width // BLOCK * wide_tiles

    def shape(*dims, kind=F32):
        return jax.ShapeDtypeStruct(dims, kind)

    vm = pltpu.VMEM
    sum_outs, sum_scratch = [], []
    for tiles in (early_tiles, mid_tiles, late_tiles):
        for each, (one, two) in zip(
            chunk_tiles(tiles, rows_count), ((near, far), (far, near))
        ):
            sum_outs.append(shape(one, two, each * BLOCK, 128, kind=BF16))
            sum_scratch += [
                vm((one, two, each * BLOCK, 128), BF16),
                vm((one, two, each * BLOCK, 128), BF16),
                vm((two, each * BLOCK, 128), BF16),
                vm((two, each * BLOCK, 128), BF16),
            ]
    outs = [
        shape(half_slots, width, kind=BF16),
        shape(half_full, width, kind=BF16),
        *sum_outs,
        shape(8, inner_w),
    ]
    scratch = [
        vm((padded, width), BF16),
        vm((padded, width), BF16),
        vm((2, half_pad, width), BF16),
        vm((round_up(half_slots + half_pad, BLOCK) + 16, width), F32),
        vm((padded, width), BF16),
        vm((padded, width), F32),
        vm((padded, 1), F32),
        vm((padded, width), BF16),
        vm((padded + 16, inner_w), F32),
        vm((padded, inner_w), F32),
        vm((2, padded, inner_w), F32),
        vm((2, padded, inner_w), BF16),
        vm((2, 128, inner_w), BF16),
        vm((2, 128, inner_w), BF16),
        vm((2, state, inner_w), F32),
        vm((2, state, inner_w), F32),
        vm((padded, 128), F32),
        vm((padded, 128), F32),
        vm((padded, 128), F32),
        vm((padded, 128), BF16),
        vm((2, padded, inner_w), F32),
        vm((2, padded, inner_w), F32),
        vm((2, padded, inner_w), F32),
        vm((padded, inner_w), F32),
        vm((padded, inner_w), F32),
        vm((padded, inner_w), F32),
        vm((padded, inner_w), BF16),
        vm((padded, inner_w), BF16),
        vm((round_up(half_slots + half_pad, BLOCK), width), F32),
        vm((2, half_pad, width), F32),
        vm((half_pad, width), F32),
        vm((padded, 1024), BF16),
        vm((padded // BLOCK, 64, BLOCK), F32),
        vm((128, 1024), BF16),
        vm((2, padded * 16 + 16, inner_w), BF16),
        vm((2, padded, inner_w), F32),
        vm((256, inner_w), BF16),
        vm((256, inner_w), BF16),
        vm((256, inner_w), BF16),
        vm((256, inner_w), BF16),
        vm((256, 128), BF16),
        vm((256, 128), BF16),
        vm((2, padded, inner_w), F32),
        vm((2, padded, inner_w), F32),
        vm((padded, 1024), BF16),
        vm((2, padded, inner_w), BF16),
        vm((2, padded, inner_w), F32),
        vm((padded, 128), F32),
        vm((padded, 128), F32),
        vm((padded, 128), BF16),
        vm((2, padded + 16, inner_w), F32),
        vm((padded, inner_w), BF16),
        vm((padded, width), F32),
        vm((padded, width), BF16),
        vm((padded, width), F32),
        vm((padded, width), BF16),
        vm((padded, half_full), BF16),
        vm((padded, 1024), F32),
        *sum_scratch,
        vm((8, inner_w), F32),
        vm((near, 8, inner_w), F32),
        vm((8, inner_w), F32),
        vm((far, 8, inner_w), F32),
        pltpu.SemaphoreType.DMA((6,)),
        pltpu.SemaphoreType.DMA((6,)),
        pltpu.SemaphoreType.DMA((4, 2, near + far - 2)),
        pltpu.SemaphoreType.DMA((4, 2, near + far - 2)),
        pltpu.SemaphoreType.DMA((4, 2, near + far - 2)),
        pltpu.SemaphoreType.DMA((2, near + far - 2)),
    ]
    in_vmem = pl.BlockSpec(memory_space=pltpu.VMEM)
    in_smem = pl.BlockSpec(memory_space=pltpu.SMEM)
    in_specs = [in_vmem, in_vmem, in_smem] + [in_vmem] * 11
    output, hidden_grad, *sums, tiny = pl.pallas_call(
        functools.partial(block_kernel, sizes),
        out_shape=outs,
        in_specs=in_specs,
        out_specs=[in_vmem] * len(outs),
        scratch_shapes=scratch,
        compiler_params=pltpu.CompilerParams(
            collective_id=0, has_side_effects=True, vmem_limit_bytes=63 * 2**20
        ),
    )(
        hidden[0],
        kept,
        counts,
        norm_gain,
        in_weight,
        conv_weight,
        conv_bias,
        jnp.swapaxes(x_weight, 1, 2),
        dt_weight,
        dt_bias,
        a_log,
        skip_gain,
        out_weight,
        cotangent[0],
    )
    inner_index = lax.axis_index("inner").astype(jnp.int32)[None]
    outs = [
        shape(half_slots, width, kind=BF16),
        shape(half_full, width, kind=BF16),
        shape(width // lax.axis_size("inner")),
        shape(2, width, inner_w),
        shape(2, 4, inner_w),
        shape(2, inner_w),
        shape(2, xwidth, inner_w),
        shape(2, rank, inner_w),
        shape(2, inner_w),
        shape(2, state, inner_w),
        shape(2, inner_w),
        shape(inner_w, width),
        shape(2, inner_w),
        shape(2, inner_w),
    ]
    outs = pl.pallas_call(
        functools.partial(finish_kernel, None),
        out_shape=outs,
        in_specs=[in_vmem] * 9 + [in_smem],
        out_specs=[in_vmem] * len(outs),
        compiler_params=pltpu.CompilerParams(vmem_limit_bytes=63 * 2**20),
    )(*sums, tiny, output, hidden_grad, inner_index)
    outs = list(outs)
    outs[0], outs[1] = outs[0][None], outs[1][None]
    outs[6] = jnp.swapaxes(outs[6], 1, 2)
    return tuple(outs)


def solution(mesh):
    in_specs = (
        P("rows", "inner", None),
        P("rows", None),
        P("rows"),
        P(),
        P(None, None, "inner"),
        P(None, None, "inner"),
        P(None, "inner"),
        P(None, "inner", None),
        P(None, None, "inner"),
        P(None, "inner"),
        P(None, None, "inner"),
        P(None, "inner"),
        P("inner", None),
        P("rows", "inner", None),
    )
    out_specs = (
        P("rows", "inner", None),
        P("rows", "inner", None),
        P("inner"),
        P(None, None, "inner"),
        P(None, None, "inner"),
        P(None, "inner"),
        P(None, "inner", None),
        P(None, None, "inner"),
        P(None, "inner"),
        P(None, None, "inner"),
        P(None, "inner"),
        P("inner", None),
        P(None, "inner"),
        P(None, "inner"),
    )
    return jax.shard_map(
        per_device, mesh=mesh, in_specs=in_specs, out_specs=out_specs, check_vma=False
    )
```

```python
import functools

import jax
import jax.numpy as jnp
from jax import lax
from jax.experimental import pallas as pl
from jax.experimental.pallas import tpu as pltpu
from jax.sharding import PartitionSpec as P

EPSILON = 1e-05
BLOCK = 16
LOG2E = 1.4426950408889634
MESH = pl.DeviceIdType.MESH
F32 = jnp.float32
BF16 = jnp.bfloat16


def dot(left, right):
    return jnp.dot(left, right, preferred_element_type=F32)


def dot_nt(left, right):
    return lax.dot_general(left, right, (((1,), (1,)), ((), ())), preferred_element_type=F32)


def dot_tn(left, right):
    return lax.dot_general(left, right, (((0,), (0,)), ((), ())), preferred_element_type=F32)


def logistic_of(value):
    return 0.5 * jnp.tanh(0.5 * value) + 0.5


def iota(shape, axis):
    return lax.broadcasted_iota(jnp.int32, shape, axis)


def round_up(value, unit):
    return (value + unit - 1) // unit * unit


def chunk_tiles(total, devices):
    each = -(-total // devices)
    first = max(1, each * 2 // 3)
    return first, max(1, each - first)


def tile_at(pair, tile):
    ref = pair[0]
    capacity = ref.shape[0] * ref.shape[1] * ref.shape[2] // BLOCK
    if tile >= capacity:
        tile, ref = tile - capacity, pair[1]
    each = ref.shape[2] // BLOCK
    chunk, place = tile // each, tile % each
    outer, middle = chunk // ref.shape[1], chunk % ref.shape[1]
    return ref, (outer, middle, slice(place * BLOCK, place * BLOCK + BLOCK), slice(None))


def put_tiles(place, value):
    columns = value.shape[1] // 128
    for tile in range(value.shape[0] // BLOCK):
        for lane in range(columns):
            ref, at = place(tile * columns + lane)
            part = value[tile * BLOCK : tile * BLOCK + BLOCK, lane * 128 : lane * 128 + 128]
            ref[at] = part.astype(BF16)


def small_place(late, mid, counts, first):
    whole, spare, _ = counts

    def place(tile):
        tile += first
        if tile < spare:
            return tile_at(late, whole + tile)
        return tile_at(mid, tile - spare)

    return place


def small_tiles(width, wide_tiles, rank, state):
    late = width // BLOCK * wide_tiles
    small = (2 * state + 2 * rank + 2 * (rank + 2 * state) + BLOCK) // BLOCK * wide_tiles
    spare = min(8, small)
    return late, spare, small - spare


class Reducer:
    def __init__(self, a, b, sems, near, far, my_near, my_far, near_peer, far_peer):
        self.ways = [
            (a, (near, my_near, near_peer), (far, my_far, far_peer)),
            (b, (far, my_far, far_peer), (near, my_near, near_peer)),
        ]
        self.sems = sems
        self.copies = [[], []]

    def sources(self):
        return (self.ways[0][0][0], self.ways[1][0][0])

    def put(self, first, value):
        put_tiles(lambda tile: tile_at(self.sources(), first + tile), value)

    def send(self, way, phase, make):
        refs, one, two = self.ways[way]
        number, mine, peer_of = one if phase in (0, 3) else two
        copies = []
        for offset in range(1, number):
            source, target = make(lax.rem(mine + offset, number))
            copies.append(
                pltpu.make_async_remote_copy(
                    src_ref=source,
                    dst_ref=target,
                    send_sem=self.sems.at[phase, 0, way, offset - 1],
                    recv_sem=self.sems.at[phase, 1, way, offset - 1],
                    device_id={"rows": peer_of(offset)},
                    device_id_type=MESH,
                )
            )
            copies[-1].start()
        self.copies[way] = copies

    def wait(self, way):
        for copy in self.copies[way]:
            copy.wait()

    def first(self):
        for way, (refs, one, two) in enumerate(self.ways):
            self.send(way, 0, lambda other: (refs[0].at[other], refs[1].at[one[1]]))

    def second(self):
        for way, (refs, one, two) in enumerate(self.ways):
            self.wait(way)
            number, mine, _ = one
            for part in range(two[0]):
                held = refs[0][mine, part].astype(F32)
                for offset in range(1, number):
                    held = held + refs[1][lax.rem(mine + offset, number), part].astype(F32)
                refs[2][part] = held.astype(BF16)
            self.send(way, 1, lambda other: (refs[2].at[other], refs[3].at[two[1]]))

    def third(self):
        for way, (refs, one, two) in enumerate(self.ways):
            self.wait(way)
            number, mine, _ = two
            held = refs[2][mine].astype(F32)
            for offset in range(1, number):
                held = held + refs[3][lax.rem(mine + offset, number)].astype(F32)
            refs[4][one[1], mine] = held.astype(BF16)
            whole = refs[4].at[one[1], mine]
            self.send(way, 2, lambda other: (whole, whole))

    def fourth(self):
        for way in (1, 0):
            refs, one, two = self.ways[way]
            self.wait(way)
            whole = refs[4].at[one[1]]
            self.send(way, 3, lambda other: (whole, whole))

    def finish(self):
        self.wait(0)
        self.wait(1)


class ShortReducer(Reducer):
    def second(self):
        for way, (refs, one, two) in enumerate(self.ways):
            self.wait(way)
            number, mine, _ = one
            for part in range(two[0]):
                held = refs[0][mine, part].astype(F32)
                for offset in range(1, number):
                    held = held + refs[1][lax.rem(mine + offset, number), part].astype(F32)
                refs[2][part] = held.astype(BF16)
            self.send(way, 1, lambda other: (refs[2], refs[3].at[two[1]]))
            refs[3][pl.ds(two[1], 1)] = refs[2][...][None]

    def third(self):
        for way, (refs, one, two) in enumerate(self.ways):
            self.wait(way)
            for part in range(two[0]):
                held = refs[3][0, part].astype(F32)
                for other in range(1, two[0]):
                    held = held + refs[3][other, part].astype(F32)
                refs[4][one[1], part] = held.astype(BF16)
            whole = refs[4].at[one[1]]
            self.send(way, 3, lambda other: (whole, whole))


def block_kernel(
    sizes,
    hidden,
    kept,
    counts,
    norm_gain,
    in_weight,
    conv_weight,
    conv_bias,
    x_weight,
    dt_weight,
    dt_bias,
    a_log,
    skip_gain,
    out_weight,
    cotangent,
    output,
    hidden_grad,
    early_a_out,
    early_b_out,
    mid_a_out,
    mid_b_out,
    late_a_out,
    late_b_out,
    tiny_out,
    picked,
    picked_in,
    cot_pair,
    gout_f,
    gout,
    gathered,
    inverse,
    normed,
    px,
    pz,
    slope,
    act,
    xw_cat,
    dtw_pad,
    rates2,
    rates,
    part,
    part_in,
    proj,
    projb,
    delta,
    sig,
    u,
    up,
    gate,
    zslope,
    zgrad,
    gated,
    terms,
    terms_pair,
    terms_in,
    blkm,
    turned_rows,
    sel,
    states,
    recent,
    ys,
    adj_0,
    adj_1,
    car_0,
    car_1,
    csum_0,
    csum_1,
    s1,
    cas,
    pgm,
    soft,
    actg,
    pgrad,
    pgrad_in,
    pgb,
    cgrad,
    xgrad,
    npart,
    npart_b,
    npart_in,
    sgrad,
    chosen,
    spread_rows,
    early_a,
    early_a1,
    early_am,
    early_a2,
    early_b,
    early_b1,
    early_bm,
    early_b2,
    mid_a,
    mid_a1,
    mid_am,
    mid_a2,
    mid_b,
    mid_b1,
    mid_bm,
    mid_b2,
    late_a,
    late_a1,
    late_am,
    late_a2,
    late_b,
    late_b1,
    late_bm,
    late_b2,
    tiny,
    tiny_low,
    tiny_mid,
    tiny_high,
    send_sem,
    recv_sem,
    early_sems,
    mid_sems,
    late_sems,
    tiny_sems,
):
    half_full, width, slots, padded, half_slots, half_pad, inner_w, rank, state, near, far = sizes
    blocks = padded // BLOCK
    inner = lax.axis_index("inner")
    peer = 1 - inner

    def remote(source, target, index):
        return pltpu.make_async_remote_copy(
            src_ref=source,
            dst_ref=target,
            send_sem=send_sem.at[index],
            recv_sem=recv_sem.at[index],
            device_id={"inner": peer},
            device_id_type=MESH,
        )

    def rows_at(block):
        return pl.ds(pl.multiple_of(block * BLOCK, BLOCK), BLOCK)

    def each_block(body, unroll=5):
        def step(block, carry):
            body(block)
            return carry

        lax.fori_loop(0, blocks, step, 0, unroll=unroll)

    row = lax.axis_index("rows")
    my_near, my_far = lax.rem(row, near), row // near

    def near_peer(offset):
        return my_far * near + lax.rem(my_near + offset, near)

    def far_peer(offset):
        return lax.rem(my_far + offset, far) * near + my_near

    barrier = pltpu.get_barrier_semaphore()
    pl.semaphore_signal(barrier, inc=1, device_id={"inner": peer}, device_id_type=MESH)
    for offset in range(1, near):
        pl.semaphore_signal(
            barrier, inc=1, device_id={"rows": near_peer(offset)}, device_id_type=MESH
        )
    for offset in range(1, far):
        pl.semaphore_signal(
            barrier, inc=1, device_id={"rows": far_peer(offset)}, device_id_type=MESH
        )

    early = Reducer(
        (early_a, early_a1, early_am, early_a2, early_a_out),
        (early_b, early_b1, early_bm, early_b2, early_b_out),
        early_sems, near, far, my_near, my_far, near_peer, far_peer,
    )
    mid = ShortReducer(
        (mid_a, mid_a1, mid_am, mid_a2, mid_a_out),
        (mid_b, mid_b1, mid_bm, mid_b2, mid_b_out),
        mid_sems, near, far, my_near, my_far, near_peer, far_peer,
    )
    late = Reducer(
        (late_a, late_a1, late_am, late_a2, late_a_out),
        (late_b, late_b1, late_bm, late_b2, late_b_out),
        late_sems, near, far, my_near, my_far, near_peer, far_peer,
    )

    count = counts[0]
    kept_row = kept[...].astype(F32)
    first = (inner * half_full).astype(F32)

    own_cot = cotangent[...].astype(F32)
    cot_rows = iota((half_slots, 1), 0) + inner * half_slots
    own_cot = jnp.where(cot_rows < count, own_cot, 0.0)
    cot_full = jnp.concatenate([own_cot, jnp.zeros((half_pad - half_slots, width), F32)], 0)
    cot_pair[pl.ds(inner, 1)] = cot_full.astype(BF16)[None]

    def pick_rows(block):
        rows = iota((BLOCK, slots), 0) + block * BLOCK
        mine = jnp.where(rows == iota((BLOCK, slots), 1), kept_row, 0.0)
        place = jnp.sum(mine, axis=1, keepdims=True) - first
        slot = iota((BLOCK, 1), 0) + block * BLOCK
        place = jnp.where(slot < count, place, -1.0)
        column = iota((BLOCK, half_full), 1).astype(F32)
        chosen[rows_at(block), :] = jnp.where(place == column, 1.0, 0.0).astype(BF16)

    each_block(pick_rows, 25)
    picked[...] = dot(chosen[...], hidden[...]).astype(BF16)
    pl.semaphore_wait(barrier, near + far - 1)
    send_pick = remote(picked, picked_in, 0)
    send_pick.start()
    send_cot = remote(cot_pair.at[inner], cot_pair.at[inner], 1)

    def at_rows(value, r):
        parts = [value, jnp.zeros((128 - 64 * r - value.shape[0], inner_w), F32)]
        if r:
            parts = [jnp.zeros((64 * r, inner_w), F32)] + parts
        return jnp.concatenate(parts, 0).astype(BF16)

    for r in range(2):
        xw_cat[r] = at_rows(x_weight[r].astype(F32), r)
        dtw_pad[r] = at_rows(dt_weight[r].astype(F32), r)
        rate = -jnp.exp(a_log[r])
        rates[r] = rate
        rates2[r] = rate * LOG2E
    lane = iota((128, 1024), 1)
    chunk = lane // 256
    start = jnp.where(
        chunk == 0,
        rank,
        jnp.where(chunk == 1, rank + state, jnp.where(chunk == 2, 64 + rank, 64 + rank + state)),
    )
    sel[...] = jnp.where(iota((128, 1024), 0) == start + lane % state, 1.0, 0.0).astype(BF16)
    zero_rows = jnp.zeros((8, inner_w), F32)
    px[0:8, :] = zero_rows
    px[8 + padded : 16 + padded, :] = zero_rows
    for r in range(2):
        cgrad[r, 0:8, :] = zero_rows
        cgrad[r, 8 + padded : 16 + padded, :] = zero_rows
    states[0, 0:16, :] = jnp.zeros((16, inner_w), BF16)
    states[1, padded * 16 : padded * 16 + 16, :] = jnp.zeros((16, inner_w), BF16)

    send_pick.wait()
    send_cot.start()
    gain = norm_gain[...].reshape(1, width)

    def norm_rows(block):
        rows = rows_at(block)
        held = picked[rows, :].astype(F32) + picked_in[rows, :].astype(F32)
        gathered[rows, :] = held
        scale = lax.rsqrt(jnp.sum(held * held, axis=1, keepdims=True) / width + EPSILON)
        inverse[rows, :] = scale
        normed[rows, :] = (held * scale * gain).astype(BF16)

    each_block(norm_rows)
    px[8 : 8 + padded, :] = dot(normed[...], in_weight[0])

    taps = conv_weight[...].astype(F32)

    span = 80

    def conv_rows(step, carry):
        base = pl.multiple_of(step * span, BLOCK)
        rows = pl.ds(base, span)
        valid = jnp.where(iota((span, 1), 0) + step * span < count, 1.0, 0.0)
        window = px[pl.ds(base, span + 16), :]
        for r in range(2):
            total = conv_bias[r : r + 1, :]
            for k in range(4):
                shift = k - 3 if r == 0 else 3 - k
                total = total + taps[r, k : k + 1, :] * window[8 + shift : 8 + shift + span, :]
            logistic = logistic_of(total)
            act[r, rows, :] = (total * logistic * valid).astype(BF16)
            slope[r, rows, :] = logistic * (1.0 + total * (1.0 - logistic)) * valid
        return carry

    lax.fori_loop(0, padded // span, conv_rows, 0)
    part[...] = dot_nt(act[0], xw_cat[0]) + dot_nt(act[1], xw_cat[1])
    send_part = remote(part, part_in, 2)
    send_part.start()

    pz[...] = dot(normed[...], in_weight[1])
    send_cot.wait()
    gout_f[0:half_pad, :] = cot_pair[0].astype(F32)
    gout_f[half_pad:, :] = jnp.zeros((gout_f.shape[0] - half_pad, width), F32)
    gout_f[half_slots : half_slots + half_pad, :] = cot_pair[1].astype(F32)
    gout[...] = gout_f[0:padded, :].astype(BF16)
    up[...] = dot_nt(gout[...], out_weight[...])

    def gate_rows(block):
        rows = rows_at(block)
        value = pz[rows, :]
        logistic = logistic_of(value)
        silu = value * logistic
        half_grad = 0.5 * up[rows, :]
        gate[rows, :] = 0.5 * silu
        zslope[rows, :] = half_grad * logistic * (1.0 + value * (1.0 - logistic))
        up[rows, :] = half_grad * silu

    each_block(gate_rows)

    send_part.wait()

    diagonal = jnp.where(iota((BLOCK, 1024), 0) == (iota((BLOCK, 1024), 1) // state) % BLOCK, 1.0, 0.0)

    def proj_rows(block):
        rows = rows_at(block)
        low = (part[rows, :] + part_in[rows, :]).astype(BF16)
        projb[rows, :] = low

    each_block(proj_rows)
    quarter = iota((64, 128), 0) // state
    start = rank + quarter % 2 * state + quarter // 2 * 64
    picks = jnp.where(iota((64, 128), 1) == start + iota((64, 128), 0) % state, 1.0, 0.0)
    picks = picks.astype(BF16)

    turned = dot_nt(picks, projb[...])
    for block in range(blocks):
        turned_rows[block] = turned[:, block * BLOCK : block * BLOCK + BLOCK]
    spread_rows[...] = dot(projb[...], sel[...])

    def mask_rows(block):
        rows = rows_at(block)
        blkm[rows, :] = (spread_rows[rows, :] * diagonal).astype(BF16)

    each_block(mask_rows)

    for r in range(2):
        sig[r] = dot(projb[...], dtw_pad[r])

    def delta_rows(block):
        rows = rows_at(block)
        for r in range(2):
            pre = sig[r, rows, :] + dt_bias[r : r + 1, :]
            small = jnp.exp(-jnp.abs(pre))
            sig[r, rows, :] = pre
            soft_plus = jnp.maximum(pre, 0.0) + jnp.log1p(small)
            delta[r, rows, :] = soft_plus
            u[r, rows, :] = soft_plus * act[r, rows, :].astype(F32)

    each_block(delta_rows)

    def state_rows(place):
        return pl.ds(pl.multiple_of(place * 16, 16), 16)

    def emit_y(step):
        for r in range(2):
            block = step if r == 0 else blocks - 1 - step
            held = recent[r]
            ys[r, rows_at(block), :] = dot(
                blkm[rows_at(block), 512 * r + 256 : 512 * r + 512], held
            )

    def forward_step(step, carry):
        emit_y(jnp.maximum(step - 1, 0))
        out = []
        for r in range(2):
            held = carry[r]
            block = step if r == 0 else blocks - 1 - step
            base = block * BLOCK
            b_cols = turned_rows[block, 32 * r : 32 * r + state, :]
            for j in range(BLOCK):
                t = j if r == 0 else BLOCK - 1 - j
                decay = jnp.exp2(delta[r, pl.ds(base + t, 1), :] * rates2[r])
                b_wide = jnp.broadcast_to(b_cols[:, t : t + 1], (state, inner_w))
                held = decay * held + u[r, pl.ds(base + t, 1), :] * b_wide
                low = held.astype(BF16)
                states[r, state_rows(base + t + (1 if r == 0 else 0)), :] = low
                recent[r, t * 16 : t * 16 + 16, :] = low
            out.append(held)
        return tuple(out)

    zero_state = jnp.zeros((state, inner_w), F32)
    lax.fori_loop(0, blocks, forward_step, (zero_state, zero_state))
    emit_y(blocks - 1)

    def mix_rows(block):
        rows = rows_at(block)
        summed = ys[0, rows, :] + ys[1, rows, :]
        for r in range(2):
            summed = summed + skip_gain[r : r + 1, :] * act[r, rows, :].astype(F32)
        gated[rows, :] = (summed * gate[rows, :]).astype(BF16)
        zgrad[rows, :] = (summed * zslope[rows, :]).astype(BF16)

    each_block(mix_rows)
    early.put(0, dot_tn(gated[...], gout[...]))
    early.put(inner_w // BLOCK * (width // 128), dot_tn(normed[...], zgrad[...]))
    early.first()

    adj_refs, car_refs = (adj_0, adj_1), (car_0, car_1)
    csum_refs = (csum_0, csum_1)
    block_mask = diagonal[:, 0:256]
    ones_block = block_mask.astype(BF16)
    ones_rows = jnp.ones((BLOCK, 128), BF16)

    def fold_lanes(value):
        total = value[:, 0:128]
        for at in range(128, inner_w, 128):
            total = total + value[:, at : at + 128]
        return total.astype(BF16)

    def emit_back(step):
        for r in range(2):
            block = blocks - 1 - step if r == 0 else step
            rows = rows_at(block)
            s1[r, rows, :] = dot(blkm[rows, 512 * r : 512 * r + 256], adj_refs[r][...])
            cas[r, rows, :] = dot(ones_block, car_refs[r][...])
            b_sums = dot_nt(u[r, rows, :].astype(BF16), adj_refs[r][...])
            c_sums = dot_nt(ones_rows, csum_refs[r][...])
            pgm[rows, 512 * r : 512 * r + 256] = (b_sums * block_mask).astype(BF16)
            pgm[rows, 512 * r + 256 : 512 * r + 512] = (c_sums * block_mask).astype(BF16)

    def backward_step(step, carry):
        emit_back(jnp.maximum(step - 1, 0))
        out = []
        for r in range(2):
            passed, rate_sum, after = carry[r]
            block = blocks - 1 - step if r == 0 else step
            base = block * BLOCK
            c_cols = turned_rows[block, 32 * r + state : 32 * r + 2 * state, :]
            for j in range(BLOCK):
                t = BLOCK - 1 - j if r == 0 else j
                own = slice(t * 16, t * 16 + 16)
                step_size = delta[r, pl.ds(base + t, 1), :]
                upstream = up[pl.ds(base + t, 1), :]
                decay = jnp.exp2(step_size * rates2[r])
                c_wide = jnp.broadcast_to(c_cols[:, t : t + 1], (state, inner_w))
                adjoint = upstream * c_wide + passed
                passed = decay * adjoint
                adj_refs[r][own, :] = adjoint.astype(BF16)
                before = states[r, state_rows(base + t + (0 if r == 0 else 1)), :].astype(F32)
                carried = passed * before
                car_refs[r][own, :] = (carried * rates[r]).astype(BF16)
                rate_sum = rate_sum + carried * step_size
                csum_refs[r][own, :] = fold_lanes(after * upstream)
                after = before
            out.append((passed, rate_sum, after))
        return tuple(out)

    last = states[0, padded * 16 : padded * 16 + 16, :].astype(F32)
    top = states[1, 0:16, :].astype(F32)
    cuts = [0, blocks * 12 // 25, blocks * 21 // 25, blocks]
    final = ((zero_state, zero_state, last), (zero_state, zero_state, top))
    final = lax.fori_loop(cuts[0], cuts[1], backward_step, final)
    early.second()
    final = lax.fori_loop(cuts[1], cuts[2], backward_step, final)
    early.third()
    final = lax.fori_loop(cuts[2], cuts[3], backward_step, final)
    emit_back(blocks - 1)
    wide_tiles = inner_w // 128
    at_dtw = 2 * state // BLOCK * wide_tiles
    at_xw = at_dtw + 2 * rank // BLOCK * wide_tiles
    at_small = at_xw + 2 * (rank + 2 * state) // BLOCK * wide_tiles
    tile_counts = small_tiles(width, wide_tiles, rank, state)

    def put_small(first, value):
        put_tiles(small_place(late.sources(), mid.sources(), tile_counts, first), value)

    def soft_rows(block, carry):
        rows = rows_at(block)
        slot = iota((BLOCK, 1), 0) + block * BLOCK
        valid = slot < count
        out = []
        upstream = up[rows, :]
        for r in range(2):
            bias_sum, skip_sum, delta_sum, square_sum = carry[r]
            active = act[r, rows, :].astype(F32)
            step_size = delta[r, rows, :]
            first_sum = s1[r, rows, :]
            pre_grad = (active * first_sum + cas[r, rows, :]) * jnp.exp(sig[r, rows, :] - step_size)
            soft[r, rows, :] = pre_grad.astype(BF16)
            actg[r, rows, :] = first_sum * step_size + skip_gain[r : r + 1, :] * upstream
            kept_step = jnp.where(valid, step_size, 0.0)
            out.append(
                (
                    bias_sum + pre_grad,
                    skip_sum + upstream * active,
                    delta_sum + kept_step,
                    square_sum + kept_step * step_size,
                )
            )
        return tuple(out)

    wide = jnp.zeros((BLOCK, inner_w), F32)
    sums = lax.fori_loop(0, blocks, soft_rows, ((wide,) * 4,) * 2, unroll=5)
    pgrad[...] = (
        dot_nt(pgm[...], sel[...]) + dot_nt(soft[0], dtw_pad[0]) + dot_nt(soft[1], dtw_pad[1])
    )
    send_pgrad = remote(pgrad, pgrad_in, 4)
    send_pgrad.start()
    early.fourth()
    low_grads = [
        dot_tn(projb[...], soft[r])[64 * r : 64 * r + rank, :] for r in range(2)
    ]
    put_small(at_dtw, jnp.concatenate(low_grads, 0))
    put_small(0, jnp.concatenate([final[r][1] * rates[r] for r in range(2)], 0))
    send_pgrad.wait()
    pgb[...] = (pgrad[...] + pgrad_in[...]).astype(BF16)
    for r in range(2):
        inside = slice(8, 8 + padded)
        cgrad[r, inside, :] = (actg[r] + dot(pgb[...], xw_cat[r])) * slope[r]

    def conv_back_rows(block):
        base = pl.multiple_of(block * BLOCK, BLOCK)
        total = jnp.zeros((BLOCK, inner_w), F32)
        for r in range(2):
            grads = cgrad[r, pl.ds(base, BLOCK + 16), :]
            for k in range(4):
                shift = k - 3 if r == 0 else 3 - k
                total = total + taps[r, k : k + 1, :] * grads[8 - shift : 8 - shift + BLOCK, :]
        xgrad[rows_at(block), :] = total.astype(BF16)

    each_block(conv_back_rows)
    late.put(0, dot_tn(normed[...], xgrad[...]))
    late.first()
    npart[...] = dot_nt(xgrad[...], in_weight[0]) + dot_nt(zgrad[...], in_weight[1])
    send_npart = remote(npart, npart_in, 5)
    send_npart.start()
    terms[0:padded, :] = dot(gated[...], out_weight[...])
    terms_pair[0] = terms[0:half_pad, :]
    terms_pair[1] = terms[half_slots : half_slots + half_pad, :]
    send_terms = remote(terms_pair.at[peer], terms_in, 3)
    send_terms.start()

    def conv_sum_rows(block, carry):
        base = pl.multiple_of(block * BLOCK, BLOCK)
        window = px[pl.ds(base, BLOCK + 16), :]
        out = []
        for r in range(2):
            here = cgrad[r, pl.ds(base + 8, BLOCK), :]
            for k in range(4):
                shift = k - 3 if r == 0 else 3 - k
                out.append(carry[5 * r + k] + here * window[8 + shift : 8 + shift + BLOCK, :])
            out.append(carry[5 * r + 4] + here)
        return tuple(out)

    conv_sums = lax.fori_loop(0, blocks, conv_sum_rows, (wide,) * 10, unroll=5)

    def total(value):
        return jnp.sum(value, axis=0, keepdims=True)

    for r in range(2):
        tiny[r : r + 1, :] = total(sums[r][2])
        tiny[2 + r : 3 + r, :] = total(sums[r][3])
    tiny[5:8, :] = jnp.full((3, inner_w), count.astype(F32))
    small = [total(conv_sums[5 * r + k]) for r in range(2) for k in range(4)]
    small += [total(conv_sums[5 * r + 4]) for r in range(2)]
    small += [total(sums[r][i]) for i in range(2) for r in range(2)]
    small += [jnp.zeros((BLOCK - len(small), inner_w), F32)]
    put_small(at_small, jnp.concatenate(small, 0))
    xwidth = rank + 2 * state
    xw_grads = [dot_tn(pgb[...], act[r])[64 * r : 64 * r + xwidth, :] for r in range(2)]
    put_small(at_xw, jnp.concatenate(xw_grads, 0))

    mid.first()

    send_npart.wait()

    def slot_rows(block, carry):
        rows = rows_at(block)
        whole = npart[rows, :] + npart_in[rows, :]
        held = gathered[rows, :]
        scale = inverse[rows, :]
        by_gain = whole * held * scale
        scaled = whole * gain
        row_dot = jnp.sum(scaled * held, axis=1, keepdims=True)
        factor = scale * scale * scale * row_dot / width
        grad = scale * scaled - held * factor + gout_f[rows, :]
        slot = iota((BLOCK, 1), 0) + block * BLOCK
        sgrad[rows, :] = jnp.where(slot < count, grad, 0.0).astype(BF16)
        return carry + by_gain

    gain_sum = lax.fori_loop(0, blocks, slot_rows, wide, unroll=5)
    tiny[4:5, :] = total(gain_sum)

    def tiny_sends(source, target, peer_of, mine, number, base):
        copies = []
        for offset in range(1, number):
            copies.append(
                pltpu.make_async_remote_copy(
                    src_ref=source,
                    dst_ref=target.at[mine],
                    send_sem=tiny_sems.at[0, base + offset - 1],
                    recv_sem=tiny_sems.at[1, base + offset - 1],
                    device_id={"rows": peer_of(offset)},
                    device_id_type=MESH,
                )
            )
            copies[-1].start()
        return copies

    copies = tiny_sends(tiny, tiny_low, near_peer, my_near, near, 0)
    late.second()
    mid.second()

    send_terms.wait()
    gathered_half = jnp.where(
        inner == 0, gathered[0:half_slots, :], gathered[half_slots : 2 * half_slots, :]
    )
    mixer = terms_pair[inner][0:half_slots, :] + terms_in[0:half_slots, :]
    output[...] = jnp.where(cot_rows < count, gathered_half + mixer, 0.0).astype(BF16)


    slot_lane = iota((1, slots), 1)
    places = jnp.where(slot_lane < count, kept_row - first, -1.0)
    spread = 112

    def scatter_rows(step, carry):
        base = pl.multiple_of(step * spread, 16)
        row = (iota((spread, slots), 0) + step * spread).astype(F32)
        chosen = jnp.where(row == places, 1.0, 0.0).astype(BF16)
        hidden_grad[pl.ds(base, spread), :] = dot(chosen, sgrad[0:slots, :]).astype(BF16)
        return carry

    lax.fori_loop(0, half_full // spread, scatter_rows, 0)
    for copy in copies:
        copy.wait()
    held = tiny[...]
    for offset in range(1, near):
        held = held + tiny_low[lax.rem(my_near + offset, near)]
    tiny_mid[...] = held
    copies = tiny_sends(tiny_mid, tiny_high, far_peer, my_far, far, near - 1)
    late.third()
    mid.third()
    for copy in copies:
        copy.wait()
    held = tiny_mid[...]
    for offset in range(1, far):
        held = held + tiny_high[lax.rem(my_far + offset, far)]
    tiny_out[...] = held
    late.fourth()
    early.finish()
    mid.finish()
    late.finish()


def finish_kernel(
    tiles,
    early_a,
    early_b,
    mid_a,
    mid_b,
    late_a,
    late_b,
    tiny,
    output_in,
    hidden_in,
    inner_ref,
    output,
    hidden_grad,
    gain_grad,
    in_grad,
    conv_w_grad,
    conv_b_grad,
    xw_grad,
    dtw_grad,
    dtb_grad,
    alog_grad,
    skip_grad,
    out_grad,
    dt_mean,
    dt_var,
):
    rank, state = dtw_grad.shape[1], alog_grad.shape[1]
    xwidth = rank + 2 * state
    width, inner_w = in_grad.shape[1:]
    wide_tiles = inner_w // 128

    def take(pair, first, rows, columns):
        return take_tiles(lambda tile: tile_at(pair, first + tile), rows, columns)

    def take_tiles(place, rows, columns):
        parts = []
        for tile in range(rows // BLOCK):
            line = []
            for lane in range(columns // 128):
                ref, at = place(tile * (columns // 128) + lane)
                line.append(ref[at])
            parts.append(jnp.concatenate(line, 1))
        return jnp.concatenate(parts, 0).astype(F32)

    early, mid, late = (early_a, early_b), (mid_a, mid_b), (late_a, late_b)
    out_grad[...] = take(early, 0, inner_w, width)
    in_grad[1] = take(early, inner_w // BLOCK * (width // 128), width, inner_w)
    in_grad[0] = take(late, 0, width, inner_w)
    tile_counts = small_tiles(width, wide_tiles, rank, state)
    at = 0

    def take_small(rows):
        nonlocal at
        value = take_tiles(small_place(late, mid, tile_counts, at), rows, inner_w)
        at += rows // BLOCK * wide_tiles
        return value

    for ref in (alog_grad, dtw_grad, xw_grad):
        each = ref.shape[1]
        both = take_small(2 * each)
        for r in range(2):
            ref[r] = both[r * each : (r + 1) * each, :]
    small = take_small(BLOCK)
    for r in range(2):
        conv_w_grad[r] = small[4 * r : 4 * r + 4, :]
    conv_b_grad[...] = small[8:10, :]
    dtb_grad[...] = small[10:12, :]
    skip_grad[...] = small[12:14, :]
    sums = tiny[...]
    mean = sums[0:2, :] / sums[5:6, :]
    dt_mean[...] = mean
    dt_var[...] = sums[2:4, :] / sums[5:6, :] - mean * mean
    part = width // 2
    gain = jnp.where(inner_ref[0] == 0, sums[4:5, 0:part], sums[4:5, part:width])
    gain_grad[...] = gain.reshape(part)
    output[...] = output_in[...]
    hidden_grad[...] = hidden_in[...]


def per_device(
    hidden,
    kept,
    counts,
    norm_gain,
    in_weight,
    conv_weight,
    conv_bias,
    x_weight,
    dt_weight,
    dt_bias,
    a_log,
    skip_gain,
    out_weight,
    cotangent,
):
    half_full, width = hidden.shape[1:]
    slots = kept.shape[1]
    half_slots = cotangent.shape[1]
    padded = round_up(slots, BLOCK)
    half_pad = round_up(half_slots, BLOCK)
    inner_w = in_weight.shape[2]
    rank = dt_weight.shape[1]
    state = a_log.shape[1]
    xwidth = x_weight.shape[2]
    rows_count = lax.axis_size("rows")
    near = 4 if rows_count % 4 == 0 else 1
    far = rows_count // near
    sizes = (
        half_full, width, slots, padded, half_slots, half_pad, inner_w, rank, state, near, far
    )
    wide_tiles = inner_w // 128
    early_tiles = 2 * (inner_w // BLOCK) * (width // 128)
    late_tiles, spare_tiles, mid_tiles = small_tiles(width, wide_tiles, rank, state)
    late_tiles += spare_tiles

    def shape(*dims, kind=F32):
        return jax.ShapeDtypeStruct(dims, kind)

    vm = pltpu.VMEM
    sum_outs, sum_scratch = [], []
    for short, tiles in ((False, early_tiles), (True, mid_tiles), (False, late_tiles)):
        for each, (one, two) in zip(
            chunk_tiles(tiles, rows_count), ((near, far), (far, near))
        ):
            sum_outs.append(shape(one, two, each * BLOCK, 128, kind=BF16))
            sum_scratch += [
                vm((one, two, each * BLOCK, 128), BF16),
                vm((one, two, each * BLOCK, 128), BF16),
                vm((two, each * BLOCK, 128), BF16),
                vm(((two, two) if short else (two,)) + (each * BLOCK, 128), BF16),
            ]
    outs = [
        shape(half_slots, width, kind=BF16),
        shape(half_full, width, kind=BF16),
        *sum_outs,
        shape(8, inner_w),
    ]
    scratch = [
        vm((padded, width), BF16),
        vm((padded, width), BF16),
        vm((2, half_pad, width), BF16),
        vm((round_up(half_slots + half_pad, BLOCK) + 16, width), F32),
        vm((padded, width), BF16),
        vm((padded, width), F32),
        vm((padded, 1), F32),
        vm((padded, width), BF16),
        vm((padded + 16, inner_w), F32),
        vm((padded, inner_w), F32),
        vm((2, padded, inner_w), F32),
        vm((2, padded, inner_w), BF16),
        vm((2, 128, inner_w), BF16),
        vm((2, 128, inner_w), BF16),
        vm((2, state, inner_w), F32),
        vm((2, state, inner_w), F32),
        vm((padded, 128), F32),
        vm((padded, 128), F32),
        vm((padded, 128), F32),
        vm((padded, 128), BF16),
        vm((2, padded, inner_w), F32),
        vm((2, padded, inner_w), F32),
        vm((2, padded, inner_w), F32),
        vm((padded, inner_w), F32),
        vm((padded, inner_w), F32),
        vm((padded, inner_w), F32),
        vm((padded, inner_w), BF16),
        vm((padded, inner_w), BF16),
        vm((round_up(half_slots + half_pad, BLOCK), width), F32),
        vm((2, half_pad, width), F32),
        vm((half_pad, width), F32),
        vm((padded, 1024), BF16),
        vm((padded // BLOCK, 64, BLOCK), F32),
        vm((128, 1024), BF16),
        vm((2, padded * 16 + 16, inner_w), BF16),
        vm((2, 256, inner_w), BF16),
        vm((2, padded, inner_w), F32),
        vm((256, inner_w), BF16),
        vm((256, inner_w), BF16),
        vm((256, inner_w), BF16),
        vm((256, inner_w), BF16),
        vm((256, 128), BF16),
        vm((256, 128), BF16),
        vm((2, padded, inner_w), F32),
        vm((2, padded, inner_w), F32),
        vm((padded, 1024), BF16),
        vm((2, padded, inner_w), BF16),
        vm((2, padded, inner_w), F32),
        vm((padded, 128), F32),
        vm((padded, 128), F32),
        vm((padded, 128), BF16),
        vm((2, padded + 16, inner_w), F32),
        vm((padded, inner_w), BF16),
        vm((padded, width), F32),
        vm((padded, width), BF16),
        vm((padded, width), F32),
        vm((padded, width), BF16),
        vm((padded, half_full), BF16),
        vm((padded, 1024), F32),
        *sum_scratch,
        vm((8, inner_w), F32),
        vm((near, 8, inner_w), F32),
        vm((8, inner_w), F32),
        vm((far, 8, inner_w), F32),
        pltpu.SemaphoreType.DMA((6,)),
        pltpu.SemaphoreType.DMA((6,)),
        pltpu.SemaphoreType.DMA((4, 2, 2, max(near, far) - 1)),
        pltpu.SemaphoreType.DMA((4, 2, 2, max(near, far) - 1)),
        pltpu.SemaphoreType.DMA((4, 2, 2, max(near, far) - 1)),
        pltpu.SemaphoreType.DMA((2, near + far - 2)),
    ]
    in_vmem = pl.BlockSpec(memory_space=pltpu.VMEM)
    in_smem = pl.BlockSpec(memory_space=pltpu.SMEM)
    in_specs = [in_vmem, in_vmem, in_smem] + [in_vmem] * 11
    output, hidden_grad, *sums, tiny = pl.pallas_call(
        functools.partial(block_kernel, sizes),
        out_shape=outs,
        in_specs=in_specs,
        out_specs=[in_vmem] * len(outs),
        scratch_shapes=scratch,
        compiler_params=pltpu.CompilerParams(
            collective_id=0, has_side_effects=True, vmem_limit_bytes=63 * 2**20
        ),
    )(
        hidden[0],
        kept,
        counts,
        norm_gain,
        in_weight,
        conv_weight,
        conv_bias,
        jnp.swapaxes(x_weight, 1, 2),
        dt_weight,
        dt_bias,
        a_log,
        skip_gain,
        out_weight,
        cotangent[0],
    )
    inner_index = lax.axis_index("inner").astype(jnp.int32)[None]
    outs = [
        shape(half_slots, width, kind=BF16),
        shape(half_full, width, kind=BF16),
        shape(width // lax.axis_size("inner")),
        shape(2, width, inner_w),
        shape(2, 4, inner_w),
        shape(2, inner_w),
        shape(2, xwidth, inner_w),
        shape(2, rank, inner_w),
        shape(2, inner_w),
        shape(2, state, inner_w),
        shape(2, inner_w),
        shape(inner_w, width),
        shape(2, inner_w),
        shape(2, inner_w),
    ]
    outs = pl.pallas_call(
        functools.partial(finish_kernel, None),
        out_shape=outs,
        in_specs=[in_vmem] * 9 + [in_smem],
        out_specs=[in_vmem] * len(outs),
        compiler_params=pltpu.CompilerParams(vmem_limit_bytes=63 * 2**20),
    )(*sums, tiny, output, hidden_grad, inner_index)
    outs = list(outs)
    outs[0], outs[1] = outs[0][None], outs[1][None]
    outs[6] = jnp.swapaxes(outs[6], 1, 2)
    return tuple(outs)


def solution(mesh):
    in_specs = (
        P("rows", "inner", None),
        P("rows", None),
        P("rows"),
        P(),
        P(None, None, "inner"),
        P(None, None, "inner"),
        P(None, "inner"),
        P(None, "inner", None),
        P(None, None, "inner"),
        P(None, "inner"),
        P(None, None, "inner"),
        P(None, "inner"),
        P("inner", None),
        P("rows", "inner", None),
    )
    out_specs = (
        P("rows", "inner", None),
        P("rows", "inner", None),
        P("inner"),
        P(None, None, "inner"),
        P(None, None, "inner"),
        P(None, "inner"),
        P(None, "inner", None),
        P(None, None, "inner"),
        P(None, "inner"),
        P(None, None, "inner"),
        P(None, "inner"),
        P("inner", None),
        P(None, "inner"),
        P(None, "inner"),
    )
    return jax.shard_map(
        per_device, mesh=mesh, in_specs=in_specs, out_specs=out_specs, check_vma=False
    )
```

```python
import functools

import jax
import jax.numpy as jnp
from jax import lax
from jax.experimental import pallas as pl
from jax.experimental.pallas import tpu as pltpu
from jax.sharding import PartitionSpec as P

EPSILON = 1e-05
BLOCK = 16
LOG2E = 1.4426950408889634
MESH = pl.DeviceIdType.MESH
F32 = jnp.float32
BF16 = jnp.bfloat16


def dot(left, right):
    return jnp.dot(left, right, preferred_element_type=F32)


def dot_nt(left, right):
    return lax.dot_general(left, right, (((1,), (1,)), ((), ())), preferred_element_type=F32)


def dot_tn(left, right):
    return lax.dot_general(left, right, (((0,), (0,)), ((), ())), preferred_element_type=F32)


def logistic_of(value):
    return 0.5 * jnp.tanh(0.5 * value) + 0.5


def iota(shape, axis):
    return lax.broadcasted_iota(jnp.int32, shape, axis)


def round_up(value, unit):
    return (value + unit - 1) // unit * unit


def chunk_tiles(total, devices):
    each = -(-total // devices)
    first = max(1, each * 2 // 3)
    return first, max(1, each - first)


def tile_at(pair, tile):
    ref = pair[0]
    capacity = ref.shape[0] * ref.shape[1] * ref.shape[2] // BLOCK
    if tile >= capacity:
        tile, ref = tile - capacity, pair[1]
    each = ref.shape[2] // BLOCK
    chunk, place = tile // each, tile % each
    outer, middle = chunk // ref.shape[1], chunk % ref.shape[1]
    return ref, (outer, middle, slice(place * BLOCK, place * BLOCK + BLOCK), slice(None))


def put_tiles(place, value):
    columns = value.shape[1] // 128
    for tile in range(value.shape[0] // BLOCK):
        for lane in range(columns):
            ref, at = place(tile * columns + lane)
            part = value[tile * BLOCK : tile * BLOCK + BLOCK, lane * 128 : lane * 128 + 128]
            ref[at] = part.astype(BF16)


def small_place(late, mid, counts, first):
    whole, spare, _ = counts

    def place(tile):
        tile += first
        if tile < spare:
            return tile_at(late, whole + tile)
        return tile_at(mid, tile - spare)

    return place


def small_tiles(width, wide_tiles, rank, state):
    late = width // BLOCK * wide_tiles
    small = (2 * state + 2 * rank + 2 * (rank + 2 * state) + BLOCK) // BLOCK * wide_tiles
    spare = min(8, small)
    return late, spare, small - spare


class Reducer:
    def __init__(self, a, b, sems, near, far, my_near, my_far, near_peer, far_peer):
        self.ways = [
            (a, (near, my_near, near_peer), (far, my_far, far_peer)),
            (b, (far, my_far, far_peer), (near, my_near, near_peer)),
        ]
        self.sems = sems
        self.copies = [[], []]

    def sources(self):
        return (self.ways[0][0][0], self.ways[1][0][0])

    def put(self, first, value):
        put_tiles(lambda tile: tile_at(self.sources(), first + tile), value)

    def send(self, way, phase, make):
        refs, one, two = self.ways[way]
        number, mine, peer_of = one if phase in (0, 3) else two
        copies = []
        for offset in range(1, number):
            source, target = make(lax.rem(mine + offset, number))
            copies.append(
                pltpu.make_async_remote_copy(
                    src_ref=source,
                    dst_ref=target,
                    send_sem=self.sems.at[phase, 0, way, offset - 1],
                    recv_sem=self.sems.at[phase, 1, way, offset - 1],
                    device_id={"rows": peer_of(offset)},
                    device_id_type=MESH,
                )
            )
            copies[-1].start()
        self.copies[way] = copies

    def wait(self, way):
        for copy in self.copies[way]:
            copy.wait()

    def first(self):
        for way, (refs, one, two) in enumerate(self.ways):
            self.send(way, 0, lambda other: (refs[0].at[other], refs[1].at[one[1]]))

    def second(self):
        for way, (refs, one, two) in enumerate(self.ways):
            self.wait(way)
            number, mine, _ = one
            for part in range(two[0]):
                held = refs[0][mine, part].astype(F32)
                for offset in range(1, number):
                    held = held + refs[1][lax.rem(mine + offset, number), part].astype(F32)
                refs[2][part] = held.astype(BF16)
            self.send(way, 1, lambda other: (refs[2].at[other], refs[3].at[two[1]]))

    def third(self):
        for way, (refs, one, two) in enumerate(self.ways):
            self.wait(way)
            number, mine, _ = two
            held = refs[2][mine].astype(F32)
            for offset in range(1, number):
                held = held + refs[3][lax.rem(mine + offset, number)].astype(F32)
            refs[4][one[1], mine] = held.astype(BF16)
            whole = refs[4].at[one[1], mine]
            self.send(way, 2, lambda other: (whole, whole))

    def fourth(self):
        for way in (1, 0):
            refs, one, two = self.ways[way]
            self.wait(way)
            whole = refs[4].at[one[1]]
            self.send(way, 3, lambda other: (whole, whole))

    def finish(self):
        self.wait(0)
        self.wait(1)


class ShortReducer(Reducer):
    def second(self):
        for way, (refs, one, two) in enumerate(self.ways):
            self.wait(way)
            number, mine, _ = one
            for part in range(two[0]):
                held = refs[0][mine, part].astype(F32)
                for offset in range(1, number):
                    held = held + refs[1][lax.rem(mine + offset, number), part].astype(F32)
                refs[2][part] = held.astype(BF16)
            self.send(way, 1, lambda other: (refs[2], refs[3].at[two[1]]))
            refs[3][pl.ds(two[1], 1)] = refs[2][...][None]

    def third(self):
        for way, (refs, one, two) in enumerate(self.ways):
            self.wait(way)
            for part in range(two[0]):
                held = refs[3][0, part].astype(F32)
                for other in range(1, two[0]):
                    held = held + refs[3][other, part].astype(F32)
                refs[4][one[1], part] = held.astype(BF16)
            whole = refs[4].at[one[1]]
            self.send(way, 3, lambda other: (whole, whole))


def block_kernel(
    sizes,
    hidden,
    kept,
    counts,
    norm_gain,
    in_weight,
    conv_weight,
    conv_bias,
    x_weight,
    dt_weight,
    dt_bias,
    a_log,
    skip_gain,
    out_weight,
    cotangent,
    output,
    hidden_grad,
    early_a_out,
    early_b_out,
    mid_a_out,
    mid_b_out,
    late_a_out,
    late_b_out,
    tiny_out,
    picked,
    picked_in,
    cot_pair,
    gout_f,
    gout,
    gathered,
    inverse,
    normed,
    px,
    pz,
    slope,
    act,
    xw_cat,
    dtw_pad,
    rates2,
    rates,
    part,
    part_in,
    proj,
    projb,
    delta,
    sig,
    u,
    up,
    gate,
    zslope,
    zgrad,
    gated,
    terms,
    terms_pair,
    terms_in,
    blkm,
    turned_rows,
    sel,
    states,
    recent,
    ys,
    adj_0,
    adj_1,
    car_0,
    car_1,
    csum_0,
    csum_1,
    s1,
    cas,
    pgm,
    soft,
    actg,
    pgrad,
    pgrad_in,
    pgb,
    cgrad,
    xgrad,
    npart,
    npart_b,
    npart_in,
    sgrad,
    chosen,
    spread_rows,
    early_a,
    early_a1,
    early_am,
    early_a2,
    early_b,
    early_b1,
    early_bm,
    early_b2,
    mid_a,
    mid_a1,
    mid_am,
    mid_a2,
    mid_b,
    mid_b1,
    mid_bm,
    mid_b2,
    late_a,
    late_a1,
    late_am,
    late_a2,
    late_b,
    late_b1,
    late_bm,
    late_b2,
    tiny,
    tiny_low,
    tiny_mid,
    tiny_high,
    send_sem,
    recv_sem,
    early_sems,
    mid_sems,
    late_sems,
    tiny_sems,
):
    half_full, width, slots, padded, half_slots, half_pad, inner_w, rank, state, near, far = sizes
    blocks = padded // BLOCK
    inner = lax.axis_index("inner")
    peer = 1 - inner

    def remote(source, target, index):
        return pltpu.make_async_remote_copy(
            src_ref=source,
            dst_ref=target,
            send_sem=send_sem.at[index],
            recv_sem=recv_sem.at[index],
            device_id={"inner": peer},
            device_id_type=MESH,
        )

    def rows_at(block):
        return pl.ds(pl.multiple_of(block * BLOCK, BLOCK), BLOCK)

    def each_block(body, unroll=5):
        def step(block, carry):
            body(block)
            return carry

        lax.fori_loop(0, blocks, step, 0, unroll=unroll)

    row = lax.axis_index("rows")
    my_near, my_far = lax.rem(row, near), row // near

    def near_peer(offset):
        return my_far * near + lax.rem(my_near + offset, near)

    def far_peer(offset):
        return lax.rem(my_far + offset, far) * near + my_near

    barrier = pltpu.get_barrier_semaphore()
    pl.semaphore_signal(barrier, inc=1, device_id={"inner": peer}, device_id_type=MESH)
    for offset in range(1, near):
        pl.semaphore_signal(
            barrier, inc=1, device_id={"rows": near_peer(offset)}, device_id_type=MESH
        )
    for offset in range(1, far):
        pl.semaphore_signal(
            barrier, inc=1, device_id={"rows": far_peer(offset)}, device_id_type=MESH
        )

    early = Reducer(
        (early_a, early_a1, early_am, early_a2, early_a_out),
        (early_b, early_b1, early_bm, early_b2, early_b_out),
        early_sems, near, far, my_near, my_far, near_peer, far_peer,
    )
    mid = ShortReducer(
        (mid_a, mid_a1, mid_am, mid_a2, mid_a_out),
        (mid_b, mid_b1, mid_bm, mid_b2, mid_b_out),
        mid_sems, near, far, my_near, my_far, near_peer, far_peer,
    )
    late = Reducer(
        (late_a, late_a1, late_am, late_a2, late_a_out),
        (late_b, late_b1, late_bm, late_b2, late_b_out),
        late_sems, near, far, my_near, my_far, near_peer, far_peer,
    )

    count = counts[0]
    kept_row = kept[...].astype(F32)
    first = (inner * half_full).astype(F32)

    own_cot = cotangent[...].astype(F32)
    cot_rows = iota((half_slots, 1), 0) + inner * half_slots
    own_cot = jnp.where(cot_rows < count, own_cot, 0.0)
    cot_full = jnp.concatenate([own_cot, jnp.zeros((half_pad - half_slots, width), F32)], 0)
    cot_pair[pl.ds(inner, 1)] = cot_full.astype(BF16)[None]

    def pick_rows(block):
        rows = iota((BLOCK, slots), 0) + block * BLOCK
        mine = jnp.where(rows == iota((BLOCK, slots), 1), kept_row, 0.0)
        place = jnp.sum(mine, axis=1, keepdims=True) - first
        slot = iota((BLOCK, 1), 0) + block * BLOCK
        place = jnp.where(slot < count, place, -1.0)
        column = iota((BLOCK, half_full), 1).astype(F32)
        chosen[rows_at(block), :] = jnp.where(place == column, 1.0, 0.0).astype(BF16)

    def some_blocks(body, lower, upper):
        def step(block, carry):
            body(block)
            return carry

        lax.fori_loop(lower, upper, step, 0, unroll=upper - lower)

    half_blocks = (blocks + 1) // 2
    send_picks = []
    for index, (lower, upper) in ((0, (0, half_blocks)), (6, (half_blocks, blocks))):
        some_blocks(pick_rows, lower, upper)
        rows = pl.ds(lower * BLOCK, (upper - lower) * BLOCK)
        picked[rows, :] = dot(chosen[rows, :], hidden[...]).astype(BF16)
        if lower == 0:
            pl.semaphore_wait(barrier, near + far - 1)
        send_picks.append(remote(picked.at[rows], picked_in.at[rows], index))
        send_picks[-1].start()
    send_cot = remote(cot_pair.at[inner], cot_pair.at[inner], 1)

    def at_rows(value, r):
        parts = [value, jnp.zeros((128 - 64 * r - value.shape[0], inner_w), F32)]
        if r:
            parts = [jnp.zeros((64 * r, inner_w), F32)] + parts
        return jnp.concatenate(parts, 0).astype(BF16)

    for r in range(2):
        xw_cat[r] = at_rows(x_weight[r].astype(F32), r)
        dtw_pad[r] = at_rows(dt_weight[r].astype(F32), r)
        rate = -jnp.exp(a_log[r])
        rates[r] = rate
        rates2[r] = rate * LOG2E
    lane = iota((128, 1024), 1)
    chunk = lane // 256
    start = jnp.where(
        chunk == 0,
        rank,
        jnp.where(chunk == 1, rank + state, jnp.where(chunk == 2, 64 + rank, 64 + rank + state)),
    )
    sel[...] = jnp.where(iota((128, 1024), 0) == start + lane % state, 1.0, 0.0).astype(BF16)
    zero_rows = jnp.zeros((8, inner_w), F32)
    px[0:8, :] = zero_rows
    px[8 + padded : 16 + padded, :] = zero_rows
    for r in range(2):
        cgrad[r, 0:8, :] = zero_rows
        cgrad[r, 8 + padded : 16 + padded, :] = zero_rows
    states[0, 0:16, :] = jnp.zeros((16, inner_w), BF16)
    states[1, padded * 16 : padded * 16 + 16, :] = jnp.zeros((16, inner_w), BF16)

    gain = norm_gain[...].reshape(1, width)

    def norm_rows(block):
        rows = rows_at(block)
        held = picked[rows, :].astype(F32) + picked_in[rows, :].astype(F32)
        gathered[rows, :] = held
        scale = lax.rsqrt(jnp.sum(held * held, axis=1, keepdims=True) / width + EPSILON)
        inverse[rows, :] = scale
        normed[rows, :] = (held * scale * gain).astype(BF16)

    send_picks[0].wait()
    some_blocks(norm_rows, 0, half_blocks)
    send_picks[1].wait()
    send_cot.start()
    some_blocks(norm_rows, half_blocks, blocks)
    px[8 : 8 + padded, :] = dot(normed[...], in_weight[0])

    taps = conv_weight[...].astype(F32)

    span = 80

    def conv_rows(step, carry):
        base = pl.multiple_of(step * span, BLOCK)
        rows = pl.ds(base, span)
        valid = jnp.where(iota((span, 1), 0) + step * span < count, 1.0, 0.0)
        window = px[pl.ds(base, span + 16), :]
        for r in range(2):
            total = conv_bias[r : r + 1, :]
            for k in range(4):
                shift = k - 3 if r == 0 else 3 - k
                total = total + taps[r, k : k + 1, :] * window[8 + shift : 8 + shift + span, :]
            logistic = logistic_of(total)
            act[r, rows, :] = (total * logistic * valid).astype(BF16)
            slope[r, rows, :] = logistic * (1.0 + total * (1.0 - logistic)) * valid
        return carry

    lax.fori_loop(0, padded // span, conv_rows, 0)
    part[...] = dot_nt(act[0], xw_cat[0]) + dot_nt(act[1], xw_cat[1])
    send_part = remote(part, part_in, 2)
    send_part.start()

    pz[...] = dot(normed[...], in_weight[1])
    send_cot.wait()
    gout_f[0:half_pad, :] = cot_pair[0].astype(F32)
    gout_f[half_pad:, :] = jnp.zeros((gout_f.shape[0] - half_pad, width), F32)
    gout_f[half_slots : half_slots + half_pad, :] = cot_pair[1].astype(F32)
    gout[...] = gout_f[0:padded, :].astype(BF16)
    up[...] = dot_nt(gout[...], out_weight[...])

    def gate_rows(block):
        rows = rows_at(block)
        value = pz[rows, :]
        logistic = logistic_of(value)
        silu = value * logistic
        half_grad = 0.5 * up[rows, :]
        gate[rows, :] = 0.5 * silu
        zslope[rows, :] = half_grad * logistic * (1.0 + value * (1.0 - logistic))
        up[rows, :] = half_grad * silu

    each_block(gate_rows)

    send_part.wait()

    diagonal = jnp.where(iota((BLOCK, 1024), 0) == (iota((BLOCK, 1024), 1) // state) % BLOCK, 1.0, 0.0)

    def proj_rows(block):
        rows = rows_at(block)
        low = (part[rows, :] + part_in[rows, :]).astype(BF16)
        projb[rows, :] = low

    each_block(proj_rows)
    quarter = iota((64, 128), 0) // state
    start = rank + quarter % 2 * state + quarter // 2 * 64
    picks = jnp.where(iota((64, 128), 1) == start + iota((64, 128), 0) % state, 1.0, 0.0)
    picks = picks.astype(BF16)

    turned = dot_nt(picks, projb[...])
    for block in range(blocks):
        turned_rows[block] = turned[:, block * BLOCK : block * BLOCK + BLOCK]
    spread_rows[...] = dot(projb[...], sel[...])

    def mask_rows(block):
        rows = rows_at(block)
        blkm[rows, :] = (spread_rows[rows, :] * diagonal).astype(BF16)

    each_block(mask_rows)

    for r in range(2):
        sig[r] = dot(projb[...], dtw_pad[r])

    def delta_rows(block):
        rows = rows_at(block)
        for r in range(2):
            pre = sig[r, rows, :] + dt_bias[r : r + 1, :]
            small = jnp.exp(-jnp.abs(pre))
            sig[r, rows, :] = pre
            soft_plus = jnp.maximum(pre, 0.0) + jnp.log1p(small)
            delta[r, rows, :] = soft_plus
            u[r, rows, :] = soft_plus * act[r, rows, :].astype(F32)

    each_block(delta_rows)

    def state_rows(place):
        return pl.ds(pl.multiple_of(place * 16, 16), 16)

    def emit_y(step):
        for r in range(2):
            block = step if r == 0 else blocks - 1 - step
            held = recent[r]
            ys[r, rows_at(block), :] = dot(
                blkm[rows_at(block), 512 * r + 256 : 512 * r + 512], held
            )

    def forward_step(step, carry):
        emit_y(jnp.maximum(step - 1, 0))
        out = []
        for r in range(2):
            held = carry[r]
            block = step if r == 0 else blocks - 1 - step
            base = block * BLOCK
            b_cols = turned_rows[block, 32 * r : 32 * r + state, :]
            for j in range(BLOCK):
                t = j if r == 0 else BLOCK - 1 - j
                decay = jnp.exp2(delta[r, pl.ds(base + t, 1), :] * rates2[r])
                b_wide = jnp.broadcast_to(b_cols[:, t : t + 1], (state, inner_w))
                held = decay * held + u[r, pl.ds(base + t, 1), :] * b_wide
                low = held.astype(BF16)
                states[r, state_rows(base + t + (1 if r == 0 else 0)), :] = low
                recent[r, t * 16 : t * 16 + 16, :] = low
            out.append(held)
        return tuple(out)

    zero_state = jnp.zeros((state, inner_w), F32)
    lax.fori_loop(0, blocks, forward_step, (zero_state, zero_state))
    emit_y(blocks - 1)

    def mix_rows(block):
        rows = rows_at(block)
        summed = ys[0, rows, :] + ys[1, rows, :]
        for r in range(2):
            summed = summed + skip_gain[r : r + 1, :] * act[r, rows, :].astype(F32)
        gated[rows, :] = (summed * gate[rows, :]).astype(BF16)
        zgrad[rows, :] = (summed * zslope[rows, :]).astype(BF16)

    each_block(mix_rows)
    early.put(0, dot_tn(gated[...], gout[...]))
    early.put(inner_w // BLOCK * (width // 128), dot_tn(normed[...], zgrad[...]))
    early.first()

    adj_refs, car_refs = (adj_0, adj_1), (car_0, car_1)
    csum_refs = (csum_0, csum_1)
    block_mask = diagonal[:, 0:256]
    ones_block = block_mask.astype(BF16)
    ones_rows = jnp.ones((BLOCK, 128), BF16)

    def fold_lanes(value):
        total = value[:, 0:128]
        for at in range(128, inner_w, 128):
            total = total + value[:, at : at + 128]
        return total.astype(BF16)

    def emit_back(step):
        for r in range(2):
            block = blocks - 1 - step if r == 0 else step
            rows = rows_at(block)
            s1[r, rows, :] = dot(blkm[rows, 512 * r : 512 * r + 256], adj_refs[r][...])
            cas[r, rows, :] = dot(ones_block, car_refs[r][...])
            b_sums = dot_nt(u[r, rows, :].astype(BF16), adj_refs[r][...])
            c_sums = dot_nt(ones_rows, csum_refs[r][...])
            pgm[rows, 512 * r : 512 * r + 256] = (b_sums * block_mask).astype(BF16)
            pgm[rows, 512 * r + 256 : 512 * r + 512] = (c_sums * block_mask).astype(BF16)

    def backward_step(step, carry):
        emit_back(jnp.maximum(step - 1, 0))
        out = []
        for r in range(2):
            passed, rate_sum, after = carry[r]
            block = blocks - 1 - step if r == 0 else step
            base = block * BLOCK
            c_cols = turned_rows[block, 32 * r + state : 32 * r + 2 * state, :]
            for j in range(BLOCK):
                t = BLOCK - 1 - j if r == 0 else j
                own = slice(t * 16, t * 16 + 16)
                step_size = delta[r, pl.ds(base + t, 1), :]
                upstream = up[pl.ds(base + t, 1), :]
                decay = jnp.exp2(step_size * rates2[r])
                c_wide = jnp.broadcast_to(c_cols[:, t : t + 1], (state, inner_w))
                adjoint = upstream * c_wide + passed
                passed = decay * adjoint
                adj_refs[r][own, :] = adjoint.astype(BF16)
                before = states[r, state_rows(base + t + (0 if r == 0 else 1)), :].astype(F32)
                carried = passed * before
                car_refs[r][own, :] = (carried * rates[r]).astype(BF16)
                rate_sum = rate_sum + carried * step_size
                csum_refs[r][own, :] = fold_lanes(after * upstream)
                after = before
            out.append((passed, rate_sum, after))
        return tuple(out)

    last = states[0, padded * 16 : padded * 16 + 16, :].astype(F32)
    top = states[1, 0:16, :].astype(F32)
    cuts = [0, blocks * 12 // 25, blocks * 21 // 25, blocks]
    final = ((zero_state, zero_state, last), (zero_state, zero_state, top))
    final = lax.fori_loop(cuts[0], cuts[1], backward_step, final)
    early.second()
    final = lax.fori_loop(cuts[1], cuts[2], backward_step, final)
    early.third()
    final = lax.fori_loop(cuts[2], cuts[3], backward_step, final)
    emit_back(blocks - 1)
    wide_tiles = inner_w // 128
    at_dtw = 2 * state // BLOCK * wide_tiles
    at_xw = at_dtw + 2 * rank // BLOCK * wide_tiles
    at_small = at_xw + 2 * (rank + 2 * state) // BLOCK * wide_tiles
    tile_counts = small_tiles(width, wide_tiles, rank, state)

    def put_small(first, value):
        put_tiles(small_place(late.sources(), mid.sources(), tile_counts, first), value)

    def soft_rows(block, carry):
        rows = rows_at(block)
        slot = iota((BLOCK, 1), 0) + block * BLOCK
        valid = slot < count
        out = []
        upstream = up[rows, :]
        for r in range(2):
            bias_sum, skip_sum, delta_sum, square_sum = carry[r]
            active = act[r, rows, :].astype(F32)
            step_size = delta[r, rows, :]
            first_sum = s1[r, rows, :]
            pre_grad = (active * first_sum + cas[r, rows, :]) * jnp.exp(sig[r, rows, :] - step_size)
            soft[r, rows, :] = pre_grad.astype(BF16)
            actg[r, rows, :] = first_sum * step_size + skip_gain[r : r + 1, :] * upstream
            kept_step = jnp.where(valid, step_size, 0.0)
            out.append(
                (
                    bias_sum + pre_grad,
                    skip_sum + upstream * active,
                    delta_sum + kept_step,
                    square_sum + kept_step * step_size,
                )
            )
        return tuple(out)

    wide = jnp.zeros((BLOCK, inner_w), F32)
    sums = lax.fori_loop(0, blocks, soft_rows, ((wide,) * 4,) * 2, unroll=5)
    pgrad[...] = (
        dot_nt(pgm[...], sel[...]) + dot_nt(soft[0], dtw_pad[0]) + dot_nt(soft[1], dtw_pad[1])
    )
    send_pgrad = remote(pgrad, pgrad_in, 4)
    send_pgrad.start()
    early.fourth()
    low_grads = [
        dot_tn(projb[...], soft[r])[64 * r : 64 * r + rank, :] for r in range(2)
    ]
    put_small(at_dtw, jnp.concatenate(low_grads, 0))
    put_small(0, jnp.concatenate([final[r][1] * rates[r] for r in range(2)], 0))
    send_pgrad.wait()
    pgb[...] = (pgrad[...] + pgrad_in[...]).astype(BF16)
    for r in range(2):
        inside = slice(8, 8 + padded)
        cgrad[r, inside, :] = (actg[r] + dot(pgb[...], xw_cat[r])) * slope[r]

    def conv_back_rows(block):
        base = pl.multiple_of(block * BLOCK, BLOCK)
        total = jnp.zeros((BLOCK, inner_w), F32)
        for r in range(2):
            grads = cgrad[r, pl.ds(base, BLOCK + 16), :]
            for k in range(4):
                shift = k - 3 if r == 0 else 3 - k
                total = total + taps[r, k : k + 1, :] * grads[8 - shift : 8 - shift + BLOCK, :]
        xgrad[rows_at(block), :] = total.astype(BF16)

    each_block(conv_back_rows)
    late.put(0, dot_tn(normed[...], xgrad[...]))
    late.first()
    npart[...] = dot_nt(xgrad[...], in_weight[0]) + dot_nt(zgrad[...], in_weight[1])
    send_npart = remote(npart, npart_in, 5)
    send_npart.start()
    terms[0:padded, :] = dot(gated[...], out_weight[...])
    terms_pair[0] = terms[0:half_pad, :]
    terms_pair[1] = terms[half_slots : half_slots + half_pad, :]
    send_terms = remote(terms_pair.at[peer], terms_in, 3)
    send_terms.start()

    def conv_sum_rows(block, carry):
        base = pl.multiple_of(block * BLOCK, BLOCK)
        window = px[pl.ds(base, BLOCK + 16), :]
        out = []
        for r in range(2):
            here = cgrad[r, pl.ds(base + 8, BLOCK), :]
            for k in range(4):
                shift = k - 3 if r == 0 else 3 - k
                out.append(carry[5 * r + k] + here * window[8 + shift : 8 + shift + BLOCK, :])
            out.append(carry[5 * r + 4] + here)
        return tuple(out)

    conv_sums = lax.fori_loop(0, blocks, conv_sum_rows, (wide,) * 10, unroll=5)

    def total(value):
        return jnp.sum(value, axis=0, keepdims=True)

    for r in range(2):
        tiny[r : r + 1, :] = total(sums[r][2])
        tiny[2 + r : 3 + r, :] = total(sums[r][3])
    tiny[5:8, :] = jnp.full((3, inner_w), count.astype(F32))
    small = [total(conv_sums[5 * r + k]) for r in range(2) for k in range(4)]
    small += [total(conv_sums[5 * r + 4]) for r in range(2)]
    small += [total(sums[r][i]) for i in range(2) for r in range(2)]
    small += [jnp.zeros((BLOCK - len(small), inner_w), F32)]
    put_small(at_small, jnp.concatenate(small, 0))
    xwidth = rank + 2 * state
    xw_grads = [dot_tn(pgb[...], act[r])[64 * r : 64 * r + xwidth, :] for r in range(2)]
    put_small(at_xw, jnp.concatenate(xw_grads, 0))

    mid.first()

    send_npart.wait()

    def slot_rows(block, carry):
        rows = rows_at(block)
        whole = npart[rows, :] + npart_in[rows, :]
        held = gathered[rows, :]
        scale = inverse[rows, :]
        by_gain = whole * held * scale
        scaled = whole * gain
        row_dot = jnp.sum(scaled * held, axis=1, keepdims=True)
        factor = scale * scale * scale * row_dot / width
        grad = scale * scaled - held * factor + gout_f[rows, :]
        slot = iota((BLOCK, 1), 0) + block * BLOCK
        sgrad[rows, :] = jnp.where(slot < count, grad, 0.0).astype(BF16)
        return carry + by_gain

    gain_sum = lax.fori_loop(0, blocks, slot_rows, wide, unroll=5)
    tiny[4:5, :] = total(gain_sum)

    def tiny_sends(source, target, peer_of, mine, number, base):
        copies = []
        for offset in range(1, number):
            copies.append(
                pltpu.make_async_remote_copy(
                    src_ref=source,
                    dst_ref=target.at[mine],
                    send_sem=tiny_sems.at[0, base + offset - 1],
                    recv_sem=tiny_sems.at[1, base + offset - 1],
                    device_id={"rows": peer_of(offset)},
                    device_id_type=MESH,
                )
            )
            copies[-1].start()
        return copies

    copies = tiny_sends(tiny, tiny_low, near_peer, my_near, near, 0)
    late.second()
    mid.second()

    send_terms.wait()
    gathered_half = jnp.where(
        inner == 0, gathered[0:half_slots, :], gathered[half_slots : 2 * half_slots, :]
    )
    mixer = terms_pair[inner][0:half_slots, :] + terms_in[0:half_slots, :]
    output[...] = jnp.where(cot_rows < count, gathered_half + mixer, 0.0).astype(BF16)


    slot_lane = iota((1, slots), 1)
    places = jnp.where(slot_lane < count, kept_row - first, -1.0)
    spread = 112

    def scatter_rows(step, carry):
        base = pl.multiple_of(step * spread, 16)
        row = (iota((spread, slots), 0) + step * spread).astype(F32)
        chosen = jnp.where(row == places, 1.0, 0.0).astype(BF16)
        hidden_grad[pl.ds(base, spread), :] = dot(chosen, sgrad[0:slots, :]).astype(BF16)
        return carry

    lax.fori_loop(0, half_full // spread, scatter_rows, 0)
    for copy in copies:
        copy.wait()
    held = tiny[...]
    for offset in range(1, near):
        held = held + tiny_low[lax.rem(my_near + offset, near)]
    tiny_mid[...] = held
    copies = tiny_sends(tiny_mid, tiny_high, far_peer, my_far, far, near - 1)
    late.third()
    mid.third()
    for copy in copies:
        copy.wait()
    held = tiny_mid[...]
    for offset in range(1, far):
        held = held + tiny_high[lax.rem(my_far + offset, far)]
    tiny_out[...] = held
    late.fourth()
    early.finish()
    mid.finish()
    late.finish()


def finish_kernel(
    tiles,
    early_a,
    early_b,
    mid_a,
    mid_b,
    late_a,
    late_b,
    tiny,
    output_in,
    hidden_in,
    inner_ref,
    output,
    hidden_grad,
    gain_grad,
    in_grad,
    conv_w_grad,
    conv_b_grad,
    xw_grad,
    dtw_grad,
    dtb_grad,
    alog_grad,
    skip_grad,
    out_grad,
    dt_mean,
    dt_var,
):
    rank, state = dtw_grad.shape[1], alog_grad.shape[1]
    xwidth = rank + 2 * state
    width, inner_w = in_grad.shape[1:]
    wide_tiles = inner_w // 128

    def take(pair, first, rows, columns):
        return take_tiles(lambda tile: tile_at(pair, first + tile), rows, columns)

    def take_tiles(place, rows, columns):
        parts = []
        for tile in range(rows // BLOCK):
            line = []
            for lane in range(columns // 128):
                ref, at = place(tile * (columns // 128) + lane)
                line.append(ref[at])
            parts.append(jnp.concatenate(line, 1))
        return jnp.concatenate(parts, 0).astype(F32)

    early, mid, late = (early_a, early_b), (mid_a, mid_b), (late_a, late_b)
    out_grad[...] = take(early, 0, inner_w, width)
    in_grad[1] = take(early, inner_w // BLOCK * (width // 128), width, inner_w)
    in_grad[0] = take(late, 0, width, inner_w)
    tile_counts = small_tiles(width, wide_tiles, rank, state)
    at = 0

    def take_small(rows):
        nonlocal at
        value = take_tiles(small_place(late, mid, tile_counts, at), rows, inner_w)
        at += rows // BLOCK * wide_tiles
        return value

    for ref in (alog_grad, dtw_grad, xw_grad):
        each = ref.shape[1]
        both = take_small(2 * each)
        for r in range(2):
            ref[r] = both[r * each : (r + 1) * each, :]
    small = take_small(BLOCK)
    for r in range(2):
        conv_w_grad[r] = small[4 * r : 4 * r + 4, :]
    conv_b_grad[...] = small[8:10, :]
    dtb_grad[...] = small[10:12, :]
    skip_grad[...] = small[12:14, :]
    sums = tiny[...]
    mean = sums[0:2, :] / sums[5:6, :]
    dt_mean[...] = mean
    dt_var[...] = sums[2:4, :] / sums[5:6, :] - mean * mean
    part = width // 2
    gain = jnp.where(inner_ref[0] == 0, sums[4:5, 0:part], sums[4:5, part:width])
    gain_grad[...] = gain.reshape(part)
    output[...] = output_in[...]
    hidden_grad[...] = hidden_in[...]


def per_device(
    hidden,
    kept,
    counts,
    norm_gain,
    in_weight,
    conv_weight,
    conv_bias,
    x_weight,
    dt_weight,
    dt_bias,
    a_log,
    skip_gain,
    out_weight,
    cotangent,
):
    half_full, width = hidden.shape[1:]
    slots = kept.shape[1]
    half_slots = cotangent.shape[1]
    padded = round_up(slots, BLOCK)
    half_pad = round_up(half_slots, BLOCK)
    inner_w = in_weight.shape[2]
    rank = dt_weight.shape[1]
    state = a_log.shape[1]
    xwidth = x_weight.shape[2]
    rows_count = lax.axis_size("rows")
    near = 4 if rows_count % 4 == 0 else 1
    far = rows_count // near
    sizes = (
        half_full, width, slots, padded, half_slots, half_pad, inner_w, rank, state, near, far
    )
    wide_tiles = inner_w // 128
    early_tiles = 2 * (inner_w // BLOCK) * (width // 128)
    late_tiles, spare_tiles, mid_tiles = small_tiles(width, wide_tiles, rank, state)
    late_tiles += spare_tiles

    def shape(*dims, kind=F32):
        return jax.ShapeDtypeStruct(dims, kind)

    vm = pltpu.VMEM
    sum_outs, sum_scratch = [], []
    for short, tiles in ((False, early_tiles), (True, mid_tiles), (False, late_tiles)):
        for each, (one, two) in zip(
            chunk_tiles(tiles, rows_count), ((near, far), (far, near))
        ):
            sum_outs.append(shape(one, two, each * BLOCK, 128, kind=BF16))
            sum_scratch += [
                vm((one, two, each * BLOCK, 128), BF16),
                vm((one, two, each * BLOCK, 128), BF16),
                vm((two, each * BLOCK, 128), BF16),
                vm(((two, two) if short else (two,)) + (each * BLOCK, 128), BF16),
            ]
    outs = [
        shape(half_slots, width, kind=BF16),
        shape(half_full, width, kind=BF16),
        *sum_outs,
        shape(8, inner_w),
    ]
    scratch = [
        vm((padded, width), BF16),
        vm((padded, width), BF16),
        vm((2, half_pad, width), BF16),
        vm((round_up(half_slots + half_pad, BLOCK) + 16, width), F32),
        vm((padded, width), BF16),
        vm((padded, width), F32),
        vm((padded, 1), F32),
        vm((padded, width), BF16),
        vm((padded + 16, inner_w), F32),
        vm((padded, inner_w), F32),
        vm((2, padded, inner_w), F32),
        vm((2, padded, inner_w), BF16),
        vm((2, 128, inner_w), BF16),
        vm((2, 128, inner_w), BF16),
        vm((2, state, inner_w), F32),
        vm((2, state, inner_w), F32),
        vm((padded, 128), F32),
        vm((padded, 128), F32),
        vm((padded, 128), F32),
        vm((padded, 128), BF16),
        vm((2, padded, inner_w), F32),
        vm((2, padded, inner_w), F32),
        vm((2, padded, inner_w), F32),
        vm((padded, inner_w), F32),
        vm((padded, inner_w), F32),
        vm((padded, inner_w), F32),
        vm((padded, inner_w), BF16),
        vm((padded, inner_w), BF16),
        vm((round_up(half_slots + half_pad, BLOCK), width), F32),
        vm((2, half_pad, width), F32),
        vm((half_pad, width), F32),
        vm((padded, 1024), BF16),
        vm((padded // BLOCK, 64, BLOCK), F32),
        vm((128, 1024), BF16),
        vm((2, padded * 16 + 16, inner_w), BF16),
        vm((2, 256, inner_w), BF16),
        vm((2, padded, inner_w), F32),
        vm((256, inner_w), BF16),
        vm((256, inner_w), BF16),
        vm((256, inner_w), BF16),
        vm((256, inner_w), BF16),
        vm((256, 128), BF16),
        vm((256, 128), BF16),
        vm((2, padded, inner_w), F32),
        vm((2, padded, inner_w), F32),
        vm((padded, 1024), BF16),
        vm((2, padded, inner_w), BF16),
        vm((2, padded, inner_w), F32),
        vm((padded, 128), F32),
        vm((padded, 128), F32),
        vm((padded, 128), BF16),
        vm((2, padded + 16, inner_w), F32),
        vm((padded, inner_w), BF16),
        vm((padded, width), F32),
        vm((padded, width), BF16),
        vm((padded, width), F32),
        vm((padded, width), BF16),
        vm((padded, half_full), BF16),
        vm((padded, 1024), F32),
        *sum_scratch,
        vm((8, inner_w), F32),
        vm((near, 8, inner_w), F32),
        vm((8, inner_w), F32),
        vm((far, 8, inner_w), F32),
        pltpu.SemaphoreType.DMA((7,)),
        pltpu.SemaphoreType.DMA((7,)),
        pltpu.SemaphoreType.DMA((4, 2, 2, max(near, far) - 1)),
        pltpu.SemaphoreType.DMA((4, 2, 2, max(near, far) - 1)),
        pltpu.SemaphoreType.DMA((4, 2, 2, max(near, far) - 1)),
        pltpu.SemaphoreType.DMA((2, near + far - 2)),
    ]
    in_vmem = pl.BlockSpec(memory_space=pltpu.VMEM)
    in_smem = pl.BlockSpec(memory_space=pltpu.SMEM)
    in_specs = [in_vmem, in_vmem, in_smem] + [in_vmem] * 11
    output, hidden_grad, *sums, tiny = pl.pallas_call(
        functools.partial(block_kernel, sizes),
        out_shape=outs,
        in_specs=in_specs,
        out_specs=[in_vmem] * len(outs),
        scratch_shapes=scratch,
        compiler_params=pltpu.CompilerParams(
            collective_id=0, has_side_effects=True, vmem_limit_bytes=63 * 2**20
        ),
    )(
        hidden[0],
        kept,
        counts,
        norm_gain,
        in_weight,
        conv_weight,
        conv_bias,
        jnp.swapaxes(x_weight, 1, 2),
        dt_weight,
        dt_bias,
        a_log,
        skip_gain,
        out_weight,
        cotangent[0],
    )
    inner_index = lax.axis_index("inner").astype(jnp.int32)[None]
    outs = [
        shape(half_slots, width, kind=BF16),
        shape(half_full, width, kind=BF16),
        shape(width // lax.axis_size("inner")),
        shape(2, width, inner_w),
        shape(2, 4, inner_w),
        shape(2, inner_w),
        shape(2, xwidth, inner_w),
        shape(2, rank, inner_w),
        shape(2, inner_w),
        shape(2, state, inner_w),
        shape(2, inner_w),
        shape(inner_w, width),
        shape(2, inner_w),
        shape(2, inner_w),
    ]
    outs = pl.pallas_call(
        functools.partial(finish_kernel, None),
        out_shape=outs,
        in_specs=[in_vmem] * 9 + [in_smem],
        out_specs=[in_vmem] * len(outs),
        compiler_params=pltpu.CompilerParams(vmem_limit_bytes=63 * 2**20),
    )(*sums, tiny, output, hidden_grad, inner_index)
    outs = list(outs)
    outs[0], outs[1] = outs[0][None], outs[1][None]
    outs[6] = jnp.swapaxes(outs[6], 1, 2)
    return tuple(outs)


def solution(mesh):
    in_specs = (
        P("rows", "inner", None),
        P("rows", None),
        P("rows"),
        P(),
        P(None, None, "inner"),
        P(None, None, "inner"),
        P(None, "inner"),
        P(None, "inner", None),
        P(None, None, "inner"),
        P(None, "inner"),
        P(None, None, "inner"),
        P(None, "inner"),
        P("inner", None),
        P("rows", "inner", None),
    )
    out_specs = (
        P("rows", "inner", None),
        P("rows", "inner", None),
        P("inner"),
        P(None, None, "inner"),
        P(None, None, "inner"),
        P(None, "inner"),
        P(None, "inner", None),
        P(None, None, "inner"),
        P(None, "inner"),
        P(None, None, "inner"),
        P(None, "inner"),
        P("inner", None),
        P(None, "inner"),
        P(None, "inner"),
    )
    return jax.shard_map(
        per_device, mesh=mesh, in_specs=in_specs, out_specs=out_specs, check_vma=False
    )
```

```python
import functools

import jax
import jax.numpy as jnp
from jax import lax
from jax.experimental import pallas as pl
from jax.experimental.pallas import tpu as pltpu
from jax.sharding import PartitionSpec as P

EPSILON = 1e-05
BLOCK = 16
LOG2E = 1.4426950408889634
MESH = pl.DeviceIdType.MESH
F32 = jnp.float32
BF16 = jnp.bfloat16


def dot(left, right):
    return jnp.dot(left, right, preferred_element_type=F32)


def dot_nt(left, right):
    return lax.dot_general(left, right, (((1,), (1,)), ((), ())), preferred_element_type=F32)


def dot_tn(left, right):
    return lax.dot_general(left, right, (((0,), (0,)), ((), ())), preferred_element_type=F32)


def logistic_of(value):
    return 0.5 * jnp.tanh(0.5 * value) + 0.5


def iota(shape, axis):
    return lax.broadcasted_iota(jnp.int32, shape, axis)


def round_up(value, unit):
    return (value + unit - 1) // unit * unit


def chunk_tiles(total, devices):
    each = -(-total // devices)
    first = max(1, each * 2 // 3)
    return first, max(1, each - first)


def tile_at(pair, tile):
    ref = pair[0]
    capacity = ref.shape[0] * ref.shape[1] * ref.shape[2] // BLOCK
    if tile >= capacity:
        tile, ref = tile - capacity, pair[1]
    each = ref.shape[2] // BLOCK
    chunk, place = tile // each, tile % each
    outer, middle = chunk // ref.shape[1], chunk % ref.shape[1]
    return ref, (outer, middle, slice(place * BLOCK, place * BLOCK + BLOCK), slice(None))


def put_tiles(place, value):
    columns = value.shape[1] // 128
    for tile in range(value.shape[0] // BLOCK):
        for lane in range(columns):
            ref, at = place(tile * columns + lane)
            part = value[tile * BLOCK : tile * BLOCK + BLOCK, lane * 128 : lane * 128 + 128]
            ref[at] = part.astype(BF16)


def small_place(late, mid, counts, first):
    whole, spare, _ = counts

    def place(tile):
        tile += first
        if tile < spare:
            return tile_at(late, whole + tile)
        return tile_at(mid, tile - spare)

    return place


def small_tiles(width, wide_tiles, rank, state):
    late = width // BLOCK * wide_tiles
    small = (2 * state + 2 * rank + 2 * (rank + 2 * state) + BLOCK) // BLOCK * wide_tiles
    spare = min(8, small)
    return late, spare, small - spare


class Reducer:
    def __init__(self, a, b, sems, near, far, my_near, my_far, near_peer, far_peer):
        self.ways = [
            (a, (near, my_near, near_peer), (far, my_far, far_peer)),
            (b, (far, my_far, far_peer), (near, my_near, near_peer)),
        ]
        self.sems = sems
        self.copies = [[], []]

    def sources(self):
        return (self.ways[0][0][0], self.ways[1][0][0])

    def put(self, first, value):
        put_tiles(lambda tile: tile_at(self.sources(), first + tile), value)

    def send(self, way, phase, make):
        refs, one, two = self.ways[way]
        number, mine, peer_of = one if phase in (0, 3) else two
        copies = []
        for offset in range(1, number):
            source, target = make(lax.rem(mine + offset, number))
            copies.append(
                pltpu.make_async_remote_copy(
                    src_ref=source,
                    dst_ref=target,
                    send_sem=self.sems.at[phase, 0, way, offset - 1],
                    recv_sem=self.sems.at[phase, 1, way, offset - 1],
                    device_id={"rows": peer_of(offset)},
                    device_id_type=MESH,
                )
            )
            copies[-1].start()
        self.copies[way] = copies

    def wait(self, way):
        for copy in self.copies[way]:
            copy.wait()

    def first(self):
        for way, (refs, one, two) in enumerate(self.ways):
            self.send(way, 0, lambda other: (refs[0].at[other], refs[1].at[one[1]]))

    def second(self):
        for way, (refs, one, two) in enumerate(self.ways):
            self.wait(way)
            number, mine, _ = one
            for part in range(two[0]):
                held = refs[0][mine, part].astype(F32)
                for offset in range(1, number):
                    held = held + refs[1][lax.rem(mine + offset, number), part].astype(F32)
                refs[2][part] = held.astype(BF16)
            self.send(way, 1, lambda other: (refs[2].at[other], refs[3].at[two[1]]))

    def third(self):
        for way, (refs, one, two) in enumerate(self.ways):
            self.wait(way)
            number, mine, _ = two
            held = refs[2][mine].astype(F32)
            for offset in range(1, number):
                held = held + refs[3][lax.rem(mine + offset, number)].astype(F32)
            refs[4][one[1], mine] = held.astype(BF16)
            whole = refs[4].at[one[1], mine]
            self.send(way, 2, lambda other: (whole, whole))

    def fourth(self):
        for way in (1, 0):
            refs, one, two = self.ways[way]
            self.wait(way)
            whole = refs[4].at[one[1]]
            self.send(way, 3, lambda other: (whole, whole))

    def finish(self):
        self.wait(0)
        self.wait(1)


class ShortReducer(Reducer):
    def second(self):
        for way, (refs, one, two) in enumerate(self.ways):
            self.wait(way)
            number, mine, _ = one
            for part in range(two[0]):
                held = refs[0][mine, part].astype(F32)
                for offset in range(1, number):
                    held = held + refs[1][lax.rem(mine + offset, number), part].astype(F32)
                refs[2][part] = held.astype(BF16)
            self.send(way, 1, lambda other: (refs[2], refs[3].at[two[1]]))
            refs[3][pl.ds(two[1], 1)] = refs[2][...][None]

    def third(self):
        for way, (refs, one, two) in enumerate(self.ways):
            self.wait(way)
            for part in range(two[0]):
                held = refs[3][0, part].astype(F32)
                for other in range(1, two[0]):
                    held = held + refs[3][other, part].astype(F32)
                refs[4][one[1], part] = held.astype(BF16)
            whole = refs[4].at[one[1]]
            self.send(way, 3, lambda other: (whole, whole))


def block_kernel(
    sizes,
    hidden,
    kept,
    counts,
    norm_gain,
    in_weight,
    conv_weight,
    conv_bias,
    x_weight,
    dt_weight,
    dt_bias,
    a_log,
    skip_gain,
    out_weight,
    cotangent,
    output,
    hidden_grad,
    early_a_out,
    early_b_out,
    mid_a_out,
    mid_b_out,
    late_a_out,
    late_b_out,
    tiny_out,
    picked,
    picked_in,
    cot_pair,
    gout_f,
    gout,
    gathered,
    inverse,
    normed,
    px,
    pz,
    slope,
    act,
    xw_cat,
    dtw_pad,
    rates2,
    rates,
    part,
    part_in,
    proj,
    projb,
    delta,
    sig,
    u,
    up,
    gate,
    zslope,
    zgrad,
    gated,
    terms,
    terms_pair,
    terms_in,
    blkm,
    turned_rows,
    sel,
    states,
    recent,
    ys,
    adj_0,
    adj_1,
    car_0,
    car_1,
    csum_0,
    csum_1,
    s1,
    cas,
    pgm,
    soft,
    actg,
    pgrad,
    pgrad_in,
    pgb,
    cgrad,
    xgrad,
    npart,
    npart_b,
    npart_in,
    sgrad,
    chosen,
    spread_rows,
    early_a,
    early_a1,
    early_am,
    early_a2,
    early_b,
    early_b1,
    early_bm,
    early_b2,
    mid_a,
    mid_a1,
    mid_am,
    mid_a2,
    mid_b,
    mid_b1,
    mid_bm,
    mid_b2,
    late_a,
    late_a1,
    late_am,
    late_a2,
    late_b,
    late_b1,
    late_bm,
    late_b2,
    tiny,
    tiny_low,
    tiny_mid,
    tiny_high,
    send_sem,
    recv_sem,
    early_sems,
    mid_sems,
    late_sems,
    tiny_sems,
):
    half_full, width, slots, padded, half_slots, half_pad, inner_w, rank, state, near, far = sizes
    blocks = padded // BLOCK
    inner = lax.axis_index("inner")
    peer = 1 - inner

    def remote(source, target, index):
        return pltpu.make_async_remote_copy(
            src_ref=source,
            dst_ref=target,
            send_sem=send_sem.at[index],
            recv_sem=recv_sem.at[index],
            device_id={"inner": peer},
            device_id_type=MESH,
        )

    def rows_at(block):
        return pl.ds(pl.multiple_of(block * BLOCK, BLOCK), BLOCK)

    def each_block(body, unroll=5):
        def step(block, carry):
            body(block)
            return carry

        lax.fori_loop(0, blocks, step, 0, unroll=unroll)

    row = lax.axis_index("rows")
    my_near, my_far = lax.rem(row, near), row // near

    def near_peer(offset):
        return my_far * near + lax.rem(my_near + offset, near)

    def far_peer(offset):
        return lax.rem(my_far + offset, far) * near + my_near

    barrier = pltpu.get_barrier_semaphore()
    pl.semaphore_signal(barrier, inc=1, device_id={"inner": peer}, device_id_type=MESH)
    for offset in range(1, near):
        pl.semaphore_signal(
            barrier, inc=1, device_id={"rows": near_peer(offset)}, device_id_type=MESH
        )
    for offset in range(1, far):
        pl.semaphore_signal(
            barrier, inc=1, device_id={"rows": far_peer(offset)}, device_id_type=MESH
        )

    early = Reducer(
        (early_a, early_a1, early_am, early_a2, early_a_out),
        (early_b, early_b1, early_bm, early_b2, early_b_out),
        early_sems, near, far, my_near, my_far, near_peer, far_peer,
    )
    mid = ShortReducer(
        (mid_a, mid_a1, mid_am, mid_a2, mid_a_out),
        (mid_b, mid_b1, mid_bm, mid_b2, mid_b_out),
        mid_sems, near, far, my_near, my_far, near_peer, far_peer,
    )
    late = Reducer(
        (late_a, late_a1, late_am, late_a2, late_a_out),
        (late_b, late_b1, late_bm, late_b2, late_b_out),
        late_sems, near, far, my_near, my_far, near_peer, far_peer,
    )

    count = counts[0]
    kept_row = kept[...].astype(F32)
    first = (inner * half_full).astype(F32)

    own_cot = cotangent[...].astype(F32)
    cot_rows = iota((half_slots, 1), 0) + inner * half_slots
    own_cot = jnp.where(cot_rows < count, own_cot, 0.0)
    cot_full = jnp.concatenate([own_cot, jnp.zeros((half_pad - half_slots, width), F32)], 0)
    cot_pair[pl.ds(inner, 1)] = cot_full.astype(BF16)[None]

    def pick_rows(block):
        rows = iota((BLOCK, slots), 0) + block * BLOCK
        mine = jnp.where(rows == iota((BLOCK, slots), 1), kept_row, 0.0)
        place = jnp.sum(mine, axis=1, keepdims=True) - first
        slot = iota((BLOCK, 1), 0) + block * BLOCK
        place = jnp.where(slot < count, place, -1.0)
        column = iota((BLOCK, half_full), 1).astype(F32)
        chosen[rows_at(block), :] = jnp.where(place == column, 1.0, 0.0).astype(BF16)

    def some_blocks(body, lower, upper):
        def step(block, carry):
            body(block)
            return carry

        lax.fori_loop(lower, upper, step, 0, unroll=upper - lower)

    half_blocks = (blocks + 1) // 2
    send_picks = []
    for index, (lower, upper) in ((0, (0, half_blocks)), (6, (half_blocks, blocks))):
        some_blocks(pick_rows, lower, upper)
        rows = pl.ds(lower * BLOCK, (upper - lower) * BLOCK)
        picked[rows, :] = dot(chosen[rows, :], hidden[...]).astype(BF16)
        if lower == 0:
            pl.semaphore_wait(barrier, near + far - 1)
        send_picks.append(remote(picked.at[rows], picked_in.at[rows], index))
        send_picks[-1].start()
    send_cot = remote(cot_pair.at[inner], cot_pair.at[inner], 1)

    def at_rows(value, r):
        parts = [value, jnp.zeros((128 - 64 * r - value.shape[0], inner_w), F32)]
        if r:
            parts = [jnp.zeros((64 * r, inner_w), F32)] + parts
        return jnp.concatenate(parts, 0).astype(BF16)

    for r in range(2):
        xw_cat[r] = at_rows(x_weight[r].astype(F32), r)
        dtw_pad[r] = at_rows(dt_weight[r].astype(F32), r)
        rate = -jnp.exp(a_log[r])
        rates[r] = rate
        rates2[r] = rate * LOG2E
    lane = iota((128, 1024), 1)
    chunk = lane // 256
    start = jnp.where(
        chunk == 0,
        rank,
        jnp.where(chunk == 1, rank + state, jnp.where(chunk == 2, 64 + rank, 64 + rank + state)),
    )
    sel[...] = jnp.where(iota((128, 1024), 0) == start + lane % state, 1.0, 0.0).astype(BF16)
    zero_rows = jnp.zeros((8, inner_w), F32)
    px[0:8, :] = zero_rows
    px[8 + padded : 16 + padded, :] = zero_rows
    for r in range(2):
        cgrad[r, 0:8, :] = zero_rows
        cgrad[r, 8 + padded : 16 + padded, :] = zero_rows
    states[0, 0:16, :] = jnp.zeros((16, inner_w), BF16)
    states[1, padded * 16 : padded * 16 + 16, :] = jnp.zeros((16, inner_w), BF16)

    gain = norm_gain[...].reshape(1, width)

    def norm_rows(block):
        rows = rows_at(block)
        held = picked[rows, :].astype(F32) + picked_in[rows, :].astype(F32)
        gathered[rows, :] = held
        scale = lax.rsqrt(jnp.sum(held * held, axis=1, keepdims=True) / width + EPSILON)
        inverse[rows, :] = scale
        normed[rows, :] = (held * scale * gain).astype(BF16)

    send_picks[0].wait()
    some_blocks(norm_rows, 0, half_blocks)
    send_picks[1].wait()
    some_blocks(norm_rows, half_blocks, blocks)
    px[8 : 8 + padded, :] = dot(normed[...], in_weight[0])
    send_cot.start()

    taps = conv_weight[...].astype(F32)

    span = 80

    def conv_rows(step, carry):
        base = pl.multiple_of(step * span, BLOCK)
        rows = pl.ds(base, span)
        valid = jnp.where(iota((span, 1), 0) + step * span < count, 1.0, 0.0)
        window = px[pl.ds(base, span + 16), :]
        for r in range(2):
            total = conv_bias[r : r + 1, :]
            for k in range(4):
                shift = k - 3 if r == 0 else 3 - k
                total = total + taps[r, k : k + 1, :] * window[8 + shift : 8 + shift + span, :]
            logistic = logistic_of(total)
            act[r, rows, :] = (total * logistic * valid).astype(BF16)
            slope[r, rows, :] = logistic * (1.0 + total * (1.0 - logistic)) * valid
        return carry

    lax.fori_loop(0, padded // span, conv_rows, 0)
    part[...] = dot_nt(act[0], xw_cat[0]) + dot_nt(act[1], xw_cat[1])
    send_part = remote(part, part_in, 2)
    send_part.start()

    pz[...] = dot(normed[...], in_weight[1])
    send_cot.wait()
    gout_f[0:half_pad, :] = cot_pair[0].astype(F32)
    gout_f[half_pad:, :] = jnp.zeros((gout_f.shape[0] - half_pad, width), F32)
    gout_f[half_slots : half_slots + half_pad, :] = cot_pair[1].astype(F32)
    gout[...] = gout_f[0:padded, :].astype(BF16)
    up[...] = dot_nt(gout[...], out_weight[...])

    def gate_rows(block):
        rows = rows_at(block)
        value = pz[rows, :]
        logistic = logistic_of(value)
        silu = value * logistic
        half_grad = 0.5 * up[rows, :]
        gate[rows, :] = 0.5 * silu
        zslope[rows, :] = half_grad * logistic * (1.0 + value * (1.0 - logistic))
        up[rows, :] = half_grad * silu

    each_block(gate_rows)

    send_part.wait()

    diagonal = jnp.where(iota((BLOCK, 1024), 0) == (iota((BLOCK, 1024), 1) // state) % BLOCK, 1.0, 0.0)

    def proj_rows(block):
        rows = rows_at(block)
        low = (part[rows, :] + part_in[rows, :]).astype(BF16)
        projb[rows, :] = low

    each_block(proj_rows)
    quarter = iota((64, 128), 0) // state
    start = rank + quarter % 2 * state + quarter // 2 * 64
    picks = jnp.where(iota((64, 128), 1) == start + iota((64, 128), 0) % state, 1.0, 0.0)
    picks = picks.astype(BF16)

    turned = dot_nt(picks, projb[...])
    for block in range(blocks):
        turned_rows[block] = turned[:, block * BLOCK : block * BLOCK + BLOCK]
    spread_rows[...] = dot(projb[...], sel[...])

    def mask_rows(block):
        rows = rows_at(block)
        blkm[rows, :] = (spread_rows[rows, :] * diagonal).astype(BF16)

    each_block(mask_rows)

    for r in range(2):
        sig[r] = dot(projb[...], dtw_pad[r])

    def delta_rows(block):
        rows = rows_at(block)
        for r in range(2):
            pre = sig[r, rows, :] + dt_bias[r : r + 1, :]
            small = jnp.exp(-jnp.abs(pre))
            sig[r, rows, :] = pre
            soft_plus = jnp.maximum(pre, 0.0) + jnp.log1p(small)
            delta[r, rows, :] = soft_plus
            u[r, rows, :] = soft_plus * act[r, rows, :].astype(F32)

    each_block(delta_rows)

    def state_rows(place):
        return pl.ds(pl.multiple_of(place * 16, 16), 16)

    def emit_y(step):
        for r in range(2):
            block = step if r == 0 else blocks - 1 - step
            held = recent[r]
            ys[r, rows_at(block), :] = dot(
                blkm[rows_at(block), 512 * r + 256 : 512 * r + 512], held
            )

    def forward_step(step, carry):
        emit_y(jnp.maximum(step - 1, 0))
        out = []
        for r in range(2):
            held = carry[r]
            block = step if r == 0 else blocks - 1 - step
            base = block * BLOCK
            b_cols = turned_rows[block, 32 * r : 32 * r + state, :]
            for j in range(BLOCK):
                t = j if r == 0 else BLOCK - 1 - j
                decay = jnp.exp2(delta[r, pl.ds(base + t, 1), :] * rates2[r])
                b_wide = jnp.broadcast_to(b_cols[:, t : t + 1], (state, inner_w))
                held = decay * held + u[r, pl.ds(base + t, 1), :] * b_wide
                low = held.astype(BF16)
                states[r, state_rows(base + t + (1 if r == 0 else 0)), :] = low
                recent[r, t * 16 : t * 16 + 16, :] = low
            out.append(held)
        return tuple(out)

    zero_state = jnp.zeros((state, inner_w), F32)
    lax.fori_loop(0, blocks, forward_step, (zero_state, zero_state))
    emit_y(blocks - 1)

    def mix_rows(block):
        rows = rows_at(block)
        summed = ys[0, rows, :] + ys[1, rows, :]
        for r in range(2):
            summed = summed + skip_gain[r : r + 1, :] * act[r, rows, :].astype(F32)
        gated[rows, :] = (summed * gate[rows, :]).astype(BF16)
        zgrad[rows, :] = (summed * zslope[rows, :]).astype(BF16)

    each_block(mix_rows)
    early.put(0, dot_tn(gated[...], gout[...]))
    early.put(inner_w // BLOCK * (width // 128), dot_tn(normed[...], zgrad[...]))
    early.first()

    adj_refs, car_refs = (adj_0, adj_1), (car_0, car_1)
    csum_refs = (csum_0, csum_1)
    block_mask = diagonal[:, 0:256]
    ones_block = block_mask.astype(BF16)
    ones_rows = jnp.ones((BLOCK, 128), BF16)

    def fold_lanes(value):
        total = value[:, 0:128]
        for at in range(128, inner_w, 128):
            total = total + value[:, at : at + 128]
        return total.astype(BF16)

    def emit_back(step):
        for r in range(2):
            block = blocks - 1 - step if r == 0 else step
            rows = rows_at(block)
            s1[r, rows, :] = dot(blkm[rows, 512 * r : 512 * r + 256], adj_refs[r][...])
            cas[r, rows, :] = dot(ones_block, car_refs[r][...])
            b_sums = dot_nt(u[r, rows, :].astype(BF16), adj_refs[r][...])
            c_sums = dot_nt(ones_rows, csum_refs[r][...])
            pgm[rows, 512 * r : 512 * r + 256] = (b_sums * block_mask).astype(BF16)
            pgm[rows, 512 * r + 256 : 512 * r + 512] = (c_sums * block_mask).astype(BF16)

    def backward_step(step, carry):
        emit_back(jnp.maximum(step - 1, 0))
        out = []
        for r in range(2):
            passed, rate_sum, after = carry[r]
            block = blocks - 1 - step if r == 0 else step
            base = block * BLOCK
            c_cols = turned_rows[block, 32 * r + state : 32 * r + 2 * state, :]
            for j in range(BLOCK):
                t = BLOCK - 1 - j if r == 0 else j
                own = slice(t * 16, t * 16 + 16)
                step_size = delta[r, pl.ds(base + t, 1), :]
                upstream = up[pl.ds(base + t, 1), :]
                decay = jnp.exp2(step_size * rates2[r])
                c_wide = jnp.broadcast_to(c_cols[:, t : t + 1], (state, inner_w))
                adjoint = upstream * c_wide + passed
                passed = decay * adjoint
                adj_refs[r][own, :] = adjoint.astype(BF16)
                before = states[r, state_rows(base + t + (0 if r == 0 else 1)), :].astype(F32)
                carried = passed * before
                car_refs[r][own, :] = (carried * rates[r]).astype(BF16)
                rate_sum = rate_sum + carried * step_size
                csum_refs[r][own, :] = fold_lanes(after * upstream)
                after = before
            out.append((passed, rate_sum, after))
        return tuple(out)

    last = states[0, padded * 16 : padded * 16 + 16, :].astype(F32)
    top = states[1, 0:16, :].astype(F32)
    cuts = [0, blocks * 12 // 25, blocks * 21 // 25, blocks]
    final = ((zero_state, zero_state, last), (zero_state, zero_state, top))
    final = lax.fori_loop(cuts[0], cuts[1], backward_step, final)
    early.second()
    final = lax.fori_loop(cuts[1], cuts[2], backward_step, final)
    early.third()
    final = lax.fori_loop(cuts[2], cuts[3], backward_step, final)
    emit_back(blocks - 1)
    wide_tiles = inner_w // 128
    at_dtw = 2 * state // BLOCK * wide_tiles
    at_xw = at_dtw + 2 * rank // BLOCK * wide_tiles
    at_small = at_xw + 2 * (rank + 2 * state) // BLOCK * wide_tiles
    tile_counts = small_tiles(width, wide_tiles, rank, state)

    def put_small(first, value):
        put_tiles(small_place(late.sources(), mid.sources(), tile_counts, first), value)

    def soft_rows(block, carry):
        rows = rows_at(block)
        slot = iota((BLOCK, 1), 0) + block * BLOCK
        valid = slot < count
        out = []
        upstream = up[rows, :]
        for r in range(2):
            bias_sum, skip_sum, delta_sum, square_sum = carry[r]
            active = act[r, rows, :].astype(F32)
            step_size = delta[r, rows, :]
            first_sum = s1[r, rows, :]
            pre_grad = (active * first_sum + cas[r, rows, :]) * jnp.exp(sig[r, rows, :] - step_size)
            soft[r, rows, :] = pre_grad.astype(BF16)
            actg[r, rows, :] = first_sum * step_size + skip_gain[r : r + 1, :] * upstream
            kept_step = jnp.where(valid, step_size, 0.0)
            out.append(
                (
                    bias_sum + pre_grad,
                    skip_sum + upstream * active,
                    delta_sum + kept_step,
                    square_sum + kept_step * step_size,
                )
            )
        return tuple(out)

    wide = jnp.zeros((BLOCK, inner_w), F32)
    sums = lax.fori_loop(0, blocks, soft_rows, ((wide,) * 4,) * 2, unroll=5)
    pgrad[...] = (
        dot_nt(pgm[...], sel[...]) + dot_nt(soft[0], dtw_pad[0]) + dot_nt(soft[1], dtw_pad[1])
    )
    send_pgrad = remote(pgrad, pgrad_in, 4)
    send_pgrad.start()
    early.fourth()
    low_grads = [
        dot_tn(projb[...], soft[r])[64 * r : 64 * r + rank, :] for r in range(2)
    ]
    put_small(at_dtw, jnp.concatenate(low_grads, 0))
    put_small(0, jnp.concatenate([final[r][1] * rates[r] for r in range(2)], 0))
    send_pgrad.wait()
    pgb[...] = (pgrad[...] + pgrad_in[...]).astype(BF16)
    for r in range(2):
        inside = slice(8, 8 + padded)
        cgrad[r, inside, :] = (actg[r] + dot(pgb[...], xw_cat[r])) * slope[r]

    def conv_back_rows(block):
        base = pl.multiple_of(block * BLOCK, BLOCK)
        total = jnp.zeros((BLOCK, inner_w), F32)
        for r in range(2):
            grads = cgrad[r, pl.ds(base, BLOCK + 16), :]
            for k in range(4):
                shift = k - 3 if r == 0 else 3 - k
                total = total + taps[r, k : k + 1, :] * grads[8 - shift : 8 - shift + BLOCK, :]
        xgrad[rows_at(block), :] = total.astype(BF16)

    each_block(conv_back_rows)
    late.put(0, dot_tn(normed[...], xgrad[...]))
    late.first()
    npart[...] = dot_nt(xgrad[...], in_weight[0]) + dot_nt(zgrad[...], in_weight[1])
    send_npart = remote(npart, npart_in, 5)
    send_npart.start()
    terms[0:padded, :] = dot(gated[...], out_weight[...])
    terms_pair[0] = terms[0:half_pad, :]
    terms_pair[1] = terms[half_slots : half_slots + half_pad, :]
    send_terms = remote(terms_pair.at[peer], terms_in, 3)
    send_terms.start()

    def conv_sum_rows(block, carry):
        base = pl.multiple_of(block * BLOCK, BLOCK)
        window = px[pl.ds(base, BLOCK + 16), :]
        out = []
        for r in range(2):
            here = cgrad[r, pl.ds(base + 8, BLOCK), :]
            for k in range(4):
                shift = k - 3 if r == 0 else 3 - k
                out.append(carry[5 * r + k] + here * window[8 + shift : 8 + shift + BLOCK, :])
            out.append(carry[5 * r + 4] + here)
        return tuple(out)

    conv_sums = lax.fori_loop(0, blocks, conv_sum_rows, (wide,) * 10, unroll=5)

    def total(value):
        return jnp.sum(value, axis=0, keepdims=True)

    for r in range(2):
        tiny[r : r + 1, :] = total(sums[r][2])
        tiny[2 + r : 3 + r, :] = total(sums[r][3])
    tiny[5:8, :] = jnp.full((3, inner_w), count.astype(F32))
    small = [total(conv_sums[5 * r + k]) for r in range(2) for k in range(4)]
    small += [total(conv_sums[5 * r + 4]) for r in range(2)]
    small += [total(sums[r][i]) for i in range(2) for r in range(2)]
    small += [jnp.zeros((BLOCK - len(small), inner_w), F32)]
    put_small(at_small, jnp.concatenate(small, 0))
    xwidth = rank + 2 * state
    xw_grads = [dot_tn(pgb[...], act[r])[64 * r : 64 * r + xwidth, :] for r in range(2)]
    put_small(at_xw, jnp.concatenate(xw_grads, 0))

    mid.first()

    send_npart.wait()

    def slot_rows(block, carry):
        rows = rows_at(block)
        whole = npart[rows, :] + npart_in[rows, :]
        held = gathered[rows, :]
        scale = inverse[rows, :]
        by_gain = whole * held * scale
        scaled = whole * gain
        row_dot = jnp.sum(scaled * held, axis=1, keepdims=True)
        factor = scale * scale * scale * row_dot / width
        grad = scale * scaled - held * factor + gout_f[rows, :]
        slot = iota((BLOCK, 1), 0) + block * BLOCK
        sgrad[rows, :] = jnp.where(slot < count, grad, 0.0).astype(BF16)
        return carry + by_gain

    gain_sum = lax.fori_loop(0, blocks, slot_rows, wide, unroll=5)
    tiny[4:5, :] = total(gain_sum)

    def tiny_sends(source, target, peer_of, mine, number, base):
        copies = []
        for offset in range(1, number):
            copies.append(
                pltpu.make_async_remote_copy(
                    src_ref=source,
                    dst_ref=target.at[mine],
                    send_sem=tiny_sems.at[0, base + offset - 1],
                    recv_sem=tiny_sems.at[1, base + offset - 1],
                    device_id={"rows": peer_of(offset)},
                    device_id_type=MESH,
                )
            )
            copies[-1].start()
        return copies

    copies = tiny_sends(tiny, tiny_low, near_peer, my_near, near, 0)
    late.second()
    mid.second()

    send_terms.wait()
    gathered_half = jnp.where(
        inner == 0, gathered[0:half_slots, :], gathered[half_slots : 2 * half_slots, :]
    )
    mixer = terms_pair[inner][0:half_slots, :] + terms_in[0:half_slots, :]
    output[...] = jnp.where(cot_rows < count, gathered_half + mixer, 0.0).astype(BF16)


    slot_lane = iota((1, slots), 1)
    places = jnp.where(slot_lane < count, kept_row - first, -1.0)
    spread = 112

    def scatter_rows(step, carry):
        base = pl.multiple_of(step * spread, 16)
        row = (iota((spread, slots), 0) + step * spread).astype(F32)
        chosen = jnp.where(row == places, 1.0, 0.0).astype(BF16)
        hidden_grad[pl.ds(base, spread), :] = dot(chosen, sgrad[0:slots, :]).astype(BF16)
        return carry

    lax.fori_loop(0, half_full // spread, scatter_rows, 0)
    for copy in copies:
        copy.wait()
    held = tiny[...]
    for offset in range(1, near):
        held = held + tiny_low[lax.rem(my_near + offset, near)]
    tiny_mid[...] = held
    copies = tiny_sends(tiny_mid, tiny_high, far_peer, my_far, far, near - 1)
    late.third()
    mid.third()
    for copy in copies:
        copy.wait()
    held = tiny_mid[...]
    for offset in range(1, far):
        held = held + tiny_high[lax.rem(my_far + offset, far)]
    tiny_out[...] = held
    late.fourth()
    early.finish()
    mid.finish()
    late.finish()


def finish_kernel(
    tiles,
    early_a,
    early_b,
    mid_a,
    mid_b,
    late_a,
    late_b,
    tiny,
    output_in,
    hidden_in,
    inner_ref,
    output,
    hidden_grad,
    gain_grad,
    in_grad,
    conv_w_grad,
    conv_b_grad,
    xw_grad,
    dtw_grad,
    dtb_grad,
    alog_grad,
    skip_grad,
    out_grad,
    dt_mean,
    dt_var,
):
    rank, state = dtw_grad.shape[1], alog_grad.shape[1]
    xwidth = rank + 2 * state
    width, inner_w = in_grad.shape[1:]
    wide_tiles = inner_w // 128

    def take(pair, first, rows, columns):
        return take_tiles(lambda tile: tile_at(pair, first + tile), rows, columns)

    def take_tiles(place, rows, columns):
        parts = []
        for tile in range(rows // BLOCK):
            line = []
            for lane in range(columns // 128):
                ref, at = place(tile * (columns // 128) + lane)
                line.append(ref[at])
            parts.append(jnp.concatenate(line, 1))
        return jnp.concatenate(parts, 0).astype(F32)

    early, mid, late = (early_a, early_b), (mid_a, mid_b), (late_a, late_b)
    out_grad[...] = take(early, 0, inner_w, width)
    in_grad[1] = take(early, inner_w // BLOCK * (width // 128), width, inner_w)
    in_grad[0] = take(late, 0, width, inner_w)
    tile_counts = small_tiles(width, wide_tiles, rank, state)
    at = 0

    def take_small(rows):
        nonlocal at
        value = take_tiles(small_place(late, mid, tile_counts, at), rows, inner_w)
        at += rows // BLOCK * wide_tiles
        return value

    for ref in (alog_grad, dtw_grad, xw_grad):
        each = ref.shape[1]
        both = take_small(2 * each)
        for r in range(2):
            ref[r] = both[r * each : (r + 1) * each, :]
    small = take_small(BLOCK)
    for r in range(2):
        conv_w_grad[r] = small[4 * r : 4 * r + 4, :]
    conv_b_grad[...] = small[8:10, :]
    dtb_grad[...] = small[10:12, :]
    skip_grad[...] = small[12:14, :]
    sums = tiny[...]
    mean = sums[0:2, :] / sums[5:6, :]
    dt_mean[...] = mean
    dt_var[...] = sums[2:4, :] / sums[5:6, :] - mean * mean
    part = width // 2
    gain = jnp.where(inner_ref[0] == 0, sums[4:5, 0:part], sums[4:5, part:width])
    gain_grad[...] = gain.reshape(part)
    output[...] = output_in[...]
    hidden_grad[...] = hidden_in[...]


def per_device(
    hidden,
    kept,
    counts,
    norm_gain,
    in_weight,
    conv_weight,
    conv_bias,
    x_weight,
    dt_weight,
    dt_bias,
    a_log,
    skip_gain,
    out_weight,
    cotangent,
):
    half_full, width = hidden.shape[1:]
    slots = kept.shape[1]
    half_slots = cotangent.shape[1]
    padded = round_up(slots, BLOCK)
    half_pad = round_up(half_slots, BLOCK)
    inner_w = in_weight.shape[2]
    rank = dt_weight.shape[1]
    state = a_log.shape[1]
    xwidth = x_weight.shape[2]
    rows_count = lax.axis_size("rows")
    near = 4 if rows_count % 4 == 0 else 1
    far = rows_count // near
    sizes = (
        half_full, width, slots, padded, half_slots, half_pad, inner_w, rank, state, near, far
    )
    wide_tiles = inner_w // 128
    early_tiles = 2 * (inner_w // BLOCK) * (width // 128)
    late_tiles, spare_tiles, mid_tiles = small_tiles(width, wide_tiles, rank, state)
    late_tiles += spare_tiles

    def shape(*dims, kind=F32):
        return jax.ShapeDtypeStruct(dims, kind)

    vm = pltpu.VMEM
    sum_outs, sum_scratch = [], []
    for short, tiles in ((False, early_tiles), (True, mid_tiles), (False, late_tiles)):
        for each, (one, two) in zip(
            chunk_tiles(tiles, rows_count), ((near, far), (far, near))
        ):
            sum_outs.append(shape(one, two, each * BLOCK, 128, kind=BF16))
            sum_scratch += [
                vm((one, two, each * BLOCK, 128), BF16),
                vm((one, two, each * BLOCK, 128), BF16),
                vm((two, each * BLOCK, 128), BF16),
                vm(((two, two) if short else (two,)) + (each * BLOCK, 128), BF16),
            ]
    outs = [
        shape(half_slots, width, kind=BF16),
        shape(half_full, width, kind=BF16),
        *sum_outs,
        shape(8, inner_w),
    ]
    scratch = [
        vm((padded, width), BF16),
        vm((padded, width), BF16),
        vm((2, half_pad, width), BF16),
        vm((round_up(half_slots + half_pad, BLOCK) + 16, width), F32),
        vm((padded, width), BF16),
        vm((padded, width), F32),
        vm((padded, 1), F32),
        vm((padded, width), BF16),
        vm((padded + 16, inner_w), F32),
        vm((padded, inner_w), F32),
        vm((2, padded, inner_w), F32),
        vm((2, padded, inner_w), BF16),
        vm((2, 128, inner_w), BF16),
        vm((2, 128, inner_w), BF16),
        vm((2, state, inner_w), F32),
        vm((2, state, inner_w), F32),
        vm((padded, 128), F32),
        vm((padded, 128), F32),
        vm((padded, 128), F32),
        vm((padded, 128), BF16),
        vm((2, padded, inner_w), F32),
        vm((2, padded, inner_w), F32),
        vm((2, padded, inner_w), F32),
        vm((padded, inner_w), F32),
        vm((padded, inner_w), F32),
        vm((padded, inner_w), F32),
        vm((padded, inner_w), BF16),
        vm((padded, inner_w), BF16),
        vm((round_up(half_slots + half_pad, BLOCK), width), F32),
        vm((2, half_pad, width), F32),
        vm((half_pad, width), F32),
        vm((padded, 1024), BF16),
        vm((padded // BLOCK, 64, BLOCK), F32),
        vm((128, 1024), BF16),
        vm((2, padded * 16 + 16, inner_w), BF16),
        vm((2, 256, inner_w), BF16),
        vm((2, padded, inner_w), F32),
        vm((256, inner_w), BF16),
        vm((256, inner_w), BF16),
        vm((256, inner_w), BF16),
        vm((256, inner_w), BF16),
        vm((256, 128), BF16),
        vm((256, 128), BF16),
        vm((2, padded, inner_w), F32),
        vm((2, padded, inner_w), F32),
        vm((padded, 1024), BF16),
        vm((2, padded, inner_w), BF16),
        vm((2, padded, inner_w), F32),
        vm((padded, 128), F32),
        vm((padded, 128), F32),
        vm((padded, 128), BF16),
        vm((2, padded + 16, inner_w), F32),
        vm((padded, inner_w), BF16),
        vm((padded, width), F32),
        vm((padded, width), BF16),
        vm((padded, width), F32),
        vm((padded, width), BF16),
        vm((padded, half_full), BF16),
        vm((padded, 1024), F32),
        *sum_scratch,
        vm((8, inner_w), F32),
        vm((near, 8, inner_w), F32),
        vm((8, inner_w), F32),
        vm((far, 8, inner_w), F32),
        pltpu.SemaphoreType.DMA((7,)),
        pltpu.SemaphoreType.DMA((7,)),
        pltpu.SemaphoreType.DMA((4, 2, 2, max(near, far) - 1)),
        pltpu.SemaphoreType.DMA((4, 2, 2, max(near, far) - 1)),
        pltpu.SemaphoreType.DMA((4, 2, 2, max(near, far) - 1)),
        pltpu.SemaphoreType.DMA((2, near + far - 2)),
    ]
    in_vmem = pl.BlockSpec(memory_space=pltpu.VMEM)
    in_smem = pl.BlockSpec(memory_space=pltpu.SMEM)
    in_specs = [in_vmem, in_vmem, in_smem] + [in_vmem] * 11
    output, hidden_grad, *sums, tiny = pl.pallas_call(
        functools.partial(block_kernel, sizes),
        out_shape=outs,
        in_specs=in_specs,
        out_specs=[in_vmem] * len(outs),
        scratch_shapes=scratch,
        compiler_params=pltpu.CompilerParams(
            collective_id=0, has_side_effects=True, vmem_limit_bytes=63 * 2**20
        ),
    )(
        hidden[0],
        kept,
        counts,
        norm_gain,
        in_weight,
        conv_weight,
        conv_bias,
        jnp.swapaxes(x_weight, 1, 2),
        dt_weight,
        dt_bias,
        a_log,
        skip_gain,
        out_weight,
        cotangent[0],
    )
    inner_index = lax.axis_index("inner").astype(jnp.int32)[None]
    outs = [
        shape(half_slots, width, kind=BF16),
        shape(half_full, width, kind=BF16),
        shape(width // lax.axis_size("inner")),
        shape(2, width, inner_w),
        shape(2, 4, inner_w),
        shape(2, inner_w),
        shape(2, xwidth, inner_w),
        shape(2, rank, inner_w),
        shape(2, inner_w),
        shape(2, state, inner_w),
        shape(2, inner_w),
        shape(inner_w, width),
        shape(2, inner_w),
        shape(2, inner_w),
    ]
    outs = pl.pallas_call(
        functools.partial(finish_kernel, None),
        out_shape=outs,
        in_specs=[in_vmem] * 9 + [in_smem],
        out_specs=[in_vmem] * len(outs),
        compiler_params=pltpu.CompilerParams(vmem_limit_bytes=63 * 2**20),
    )(*sums, tiny, output, hidden_grad, inner_index)
    outs = list(outs)
    outs[0], outs[1] = outs[0][None], outs[1][None]
    outs[6] = jnp.swapaxes(outs[6], 1, 2)
    return tuple(outs)


def solution(mesh):
    in_specs = (
        P("rows", "inner", None),
        P("rows", None),
        P("rows"),
        P(),
        P(None, None, "inner"),
        P(None, None, "inner"),
        P(None, "inner"),
        P(None, "inner", None),
        P(None, None, "inner"),
        P(None, "inner"),
        P(None, None, "inner"),
        P(None, "inner"),
        P("inner", None),
        P("rows", "inner", None),
    )
    out_specs = (
        P("rows", "inner", None),
        P("rows", "inner", None),
        P("inner"),
        P(None, None, "inner"),
        P(None, None, "inner"),
        P(None, "inner"),
        P(None, "inner", None),
        P(None, None, "inner"),
        P(None, "inner"),
        P(None, None, "inner"),
        P(None, "inner"),
        P("inner", None),
        P(None, "inner"),
        P(None, "inner"),
    )
    return jax.shard_map(
        per_device, mesh=mesh, in_specs=in_specs, out_specs=out_specs, check_vma=False
    )
```
